32 devices in a mesh: seq: 8 (over z, core), wt: 4 (over y, x).
Axes of the slice: x: 2, y: 2, z: 4, core: 2. Of those that a mesh axis runs over, the one named last changes fastest.
Arguments:
- tokens: bfloat16 [4, 1024, 1024], P('wt', 'seq'), may hold values from -6 to 6
- cotangent: bfloat16 [4, 1024, 1024], P('wt', 'seq'), may hold values from -6 to 6
- doc_bounds: int32 [4, 2], P('wt'), may hold values from 1 to 1023, as said below
- attn_master: float32 [4, 1024, 1024], P(None, 'wt'), may hold values from -0.375 to 0.375
- mlp_master: float32 [3, 1024, 2816], P(None, 'wt'), may hold values from -0.15075567 to 0.15075567
- attn_momentum: float32 [4, 1024, 1024], P(None, 'wt'), may hold values from -512 to 512
- mlp_momentum: float32 [3, 1024, 2816], P(None, 'wt'), may hold values from -179.2 to 179.2
- gains: float32 [2, 1024], P(None, 'wt'), may hold values from 0.5 to 1.5
- gain_first: float32 [2, 1024], P(None, 'wt'), may hold values from -51.2 to 51.2
- gain_second: float32 [2, 1024], P(None, 'wt'), may hold values from 819.2 to 3276.8
- qkv_bias: float32 [3, 1024], P(None, 'wt'), may hold values from -2.5 to 2.5
- bias_first: float32 [3, 1024], P(None, 'wt'), may hold values from -51.2 to 51.2
- bias_second: float32 [3, 1024], P(None, 'wt'), may hold values from 819.2 to 3276.8
Outputs:
- output: bfloat16 [4, 1024, 1024], P('wt', 'seq')
- tokens_grad: float32 [4, 1024, 1024], P('wt', 'seq')
- attn_grad: float32 [4, 1024, 1024], P(None, 'wt')
- mlp_grad: float32 [3, 1024, 2816], P(None, 'wt')
- attn_momentum_new: float32 [4, 1024, 1024], P(None, 'wt')
- mlp_momentum_new: float32 [3, 1024, 2816], P(None, 'wt')
- attn_new: float32 [4, 1024, 1024], P(None, 'wt', 'seq')
- mlp_new: float32 [3, 1024, 2816], P(None, 'wt', 'seq')
- gain_grad: float32 [2, 1024], P(None, 'wt')
- gain_second_new: float32 [2, 1024], P(None, 'wt')
- gain_new: float32 [2, 1024], P(None, 'wt')
- bias_grad: float32 [3, 1024], P(None, 'wt')
- bias_second_new: float32 [3, 1024], P(None, 'wt')
- bias_new: float32 [3, 1024], P(None, 'wt')
The draws below stay inside these ranges and needn't reach their ends.
Inputs may be any that keep to these rules, and one draw needn't show every extreme that they name: `doc_bounds`: row g holds the first tokens of documents 1 and 2 of sequence g: 0 < first < 128 and 896 < second < 1024.
All inputs are finite; a program needn't handle non-finite values.
Results may differ from the reference program's by a relative error of at most 0.018.
The reference program's roundings to bfloat16 on the way count: a program that leaves them out, or rounds other values in their place, can miss the bound.
Values may be sent and summed in bfloat16 or wider, within the bound.
No kernel may reach another device: no remote copies, remote signals or barrier semaphores. Data moves between devices by JAX's collectives and lax.ppermute only.
A program may use at most 320 MiB of HBM per device.

```python
import math
import jax
import jax.numpy as jnp
from jax import lax

HEADS = 16
HEAD_DIM = 64
D = 1024
FF = 2816
TOK_DEV = 128
NS_STEPS = 5
STEP = 10
SEQ_LEN = 1024
GROUPS = 4
TOKENS = 4096


def draw_doc_bounds(key, part):
    key = jax.random.fold_in(key, 11)
    key_first, key_second, key_pick = jax.random.split(key, 3)
    first_bound = jax.random.randint(key_first, (GROUPS,), 1, TOK_DEV)
    second_bound = jax.random.randint(key_second, (GROUPS,), SEQ_LEN - TOK_DEV + 1, SEQ_LEN)
    picks = jax.random.randint(key_pick, (2,), 0, GROUPS)
    row_ids = jnp.arange(GROUPS)
    first_bound = jnp.where(row_ids == picks[0], 1, first_bound)
    second_bound = jnp.where(row_ids == picks[1], SEQ_LEN - 1, second_bound)
    return jnp.stack([first_bound, second_bound], axis=1).astype(jnp.int32)


def scaled_normal(key, shape, factors):
    values = jnp.clip(jax.random.normal(key, shape, jnp.float32), -4.0, 4.0)
    return values * jnp.array(factors, jnp.float32)[:, None, None]


def draw_attn_master(key, part):
    key = jax.random.fold_in(key, 21)
    base = 1.0 / math.sqrt(D)
    return scaled_normal(key, (4, D, D), [1.5 * base, 1.5 * base, base, 3.0 * base])


def draw_mlp_master(key, part):
    key = jax.random.fold_in(key, 22)
    return scaled_normal(key, (3, D, FF), [1.0 / math.sqrt(D), 1.0 / math.sqrt(D), 2.0 / math.sqrt(FF)])


def draw_attn_momentum(key, part):
    key = jax.random.fold_in(key, 23)
    root = math.sqrt(TOKENS)
    return scaled_normal(key, (4, D, D), [2.0 * root, 2.0 * root, root, 0.5 * root])


def draw_mlp_momentum(key, part):
    key = jax.random.fold_in(key, 24)
    root = math.sqrt(TOKENS)
    return scaled_normal(key, (3, D, FF), [0.5 * root, 0.5 * root, 0.7 * root])


def level_of(key, extent, shards, smallest, largest):
    factor_of, own = 1.0, jax.random.fold_in(key, 6)
    for axis_at, shards_of in shards:
        heights = jnp.exp(jax.random.uniform(jax.random.fold_in(own, axis_at), (shards_of,), jnp.float32, smallest / len(shards), largest / len(shards)))
        factor_of = factor_of * jnp.repeat(heights, extent[axis_at] // shards_of).reshape([-1 if axis == axis_at else 1 for axis in range(len(extent))])
    return factor_of


def noise(own_key, dims, scale, most, cuts=(), kind=jnp.bfloat16):
    gain = level_of(own_key, dims, cuts, -0.22, 0.18) if cuts else 1.0
    entries = jax.random.normal(own_key, dims, jnp.float32) * scale * gain
    return jnp.minimum(jnp.maximum(entries, -most), most).astype(kind)


def setup_inputs(seed: int = 0) -> dict:
    streams_of = jax.random.split(jax.random.key(seed), 14)
    return {
        "tokens": noise(streams_of[0], (GROUPS, SEQ_LEN, D), 1.0, 6.0, ((0, 4), (1, 8))),
        "cotangent": noise(streams_of[1], (GROUPS, SEQ_LEN, D), 1.0, 6.0, ((0, 4), (1, 8))),
        "doc_bounds": draw_doc_bounds(jax.random.fold_in(streams_of[13], 71), 0),
        "attn_master": draw_attn_master(jax.random.fold_in(streams_of[13], 71), 0),
        "mlp_master": draw_mlp_master(jax.random.fold_in(streams_of[13], 71), 0),
        "attn_momentum": draw_attn_momentum(jax.random.fold_in(streams_of[13], 71), 0),
        "mlp_momentum": draw_mlp_momentum(jax.random.fold_in(streams_of[13], 71), 0),
        "gains": jnp.clip(1.0 + 0.1 * jax.random.normal(streams_of[7], (2, D), jnp.float32), 0.5, 1.5),
        "gain_first": noise(streams_of[8], (2, D), (0.2 * TOKENS ** 0.5), 51.2, ((1, 4),), jnp.float32),
        "gain_second": jnp.clip(jnp.exp(math.log(3276.8) - 1.3862944 * jax.random.uniform(streams_of[9], (2, D), jnp.float32) ** level_of(streams_of[9], (2, D), ((1, 4),), -0.2, 0.2)), 819.2, 3276.8),
        "qkv_bias": noise(streams_of[10], (3, D), 0.5, 2.5, ((1, 4),), jnp.float32),
        "bias_first": noise(streams_of[11], (3, D), (0.2 * TOKENS ** 0.5), 51.2, ((1, 4),), jnp.float32),
        "bias_second": jnp.clip(jnp.exp(math.log(3276.8) - 1.3862944 * jax.random.uniform(streams_of[12], (3, D), jnp.float32) ** level_of(streams_of[12], (3, D), ((1, 4),), -0.2, 0.2)), 819.2, 3276.8),
    }


@jax.custom_vjp
def low(v):
    return lax.optimization_barrier(v.astype(jnp.bfloat16)).astype(jnp.float32)

@jax.custom_vjp
def low_back(v):
    return v

def low_keep(v):
    return (low(v), None)

def low_pass(kept, grad):
    return (grad,)

def back_keep(v):
    return (v, None)

def back_low(kept, grad):
    return (low(grad),)
low.defvjp(low_keep, low_pass)
low_back.defvjp(back_keep, back_low)
norm_eps = 1e-06
rope_base = 1000000.0
coef_a = 3.4445
coef_b = -4.775
coef_c = 2.0315
momentum_decay = 0.95
matrix_rate = 0.5
decay_rate = 0.01
first_decay = 0.9
second_decay = 0.95
vector_rate = 0.25
adam_eps = 1e-08
ortho_eps = 1e-07
block_limit = 512
masked_score = -1e+30
highest = lax.Precision.HIGHEST

def doc_layout(bounds, length):
    places = jnp.arange(length, dtype=jnp.int32)
    first_bound = bounds[0]
    second_bound = bounds[1]
    doc_index = (places >= first_bound).astype(jnp.int32) + (places >= second_bound).astype(jnp.int32)
    doc_start = jnp.where(places < first_bound, 0, jnp.where(places < second_bound, first_bound, second_bound))
    return (doc_index, (places - doc_start).astype(jnp.float32))

def rope_tables(position, head_dim):
    half_dim = head_dim // 2
    frequency = rope_base ** (-2.0 * jnp.arange(half_dim, dtype=jnp.float32) / head_dim)
    angles = frequency[:, None] * position[None, :]
    cosine_table = jnp.cos(angles)
    sine_table = jnp.sin(angles)
    return (jnp.concatenate([cosine_table, cosine_table], 0), jnp.concatenate([sine_table, sine_table], 0))

def rotate_half(values):
    half_dim = values.shape[-2] // 2
    return jnp.concatenate([-values[..., half_dim:, :], values[..., :half_dim, :]], axis=-2)

def apply_rope(values, cosine_table, sine_table):
    return values * cosine_table + rotate_half(values) * sine_table

def attend_reference(query_rot, key_rot, value_heads, doc_index):
    head_count, head_dim, length = query_rot.shape
    block_size = min(block_limit, length)
    score_scale = head_dim ** (-0.5)
    key_places = jnp.arange(length, dtype=jnp.int32)

    def one_block(block_index):
        first_row = block_index * block_size
        query_block = lax.dynamic_slice_in_dim(query_rot, first_row, block_size, 2)
        query_places = first_row + jnp.arange(block_size, dtype=jnp.int32)
        query_docs = lax.dynamic_slice_in_dim(doc_index, first_row, block_size)
        allowed = (query_docs[:, None] == doc_index[None, :]) & (key_places[None, :] <= query_places[:, None])
        scores = low_back(jnp.einsum('hdq,hdk->hqk', query_block, key_rot, precision=highest) * score_scale)
        scores = jnp.where(allowed[None], scores, masked_score)
        row_peak = lax.optimization_barrier(jnp.max(scores, axis=-1, keepdims=True))
        exponent = jnp.exp(scores - row_peak)
        weights = exponent / lax.optimization_barrier(jnp.sum(exponent, axis=-1, keepdims=True))
        return jnp.einsum('hqk,hdk->hdq', low(weights), value_heads, precision=highest)
    blocks = lax.map(jax.checkpoint(one_block), jnp.arange(length // block_size, dtype=jnp.int32))
    return jnp.moveaxis(blocks, 0, 2).reshape(head_count, head_dim, length)

def norm_apply(values, gain_row):
    inverse = lax.rsqrt(lax.optimization_barrier(jnp.mean(values * values, axis=-1, keepdims=True)) + norm_eps)
    return low(values * inverse * gain_row)

def layer_group(params, token_values, bounds):
    attn_w, mlp_w, gain_w, bias_w = params
    length = token_values.shape[0]
    doc_index, position = doc_layout(bounds, length)
    cosine_table, sine_table = rope_tables(position, HEAD_DIM)
    normed_one = norm_apply(token_values, gain_w[0])
    projected = jnp.einsum('td,jdc->jct', normed_one, attn_w[:3], precision=highest) + bias_w[:, :, None]
    projected = low_back(low(projected)).reshape(3, HEADS, HEAD_DIM, length)
    query_rot = low(apply_rope(projected[0], cosine_table, sine_table))
    key_rot = low(apply_rope(projected[1], cosine_table, sine_table))
    attended = low_back(low(attend_reference(query_rot, key_rot, projected[2], doc_index)))
    attn_flat = attended.reshape(D, length)
    resid = token_values + low_back(jnp.einsum('ct,cd->td', attn_flat, attn_w[3], precision=highest))
    normed_two = norm_apply(resid, gain_w[1])
    gate_act = low_back(jnp.dot(normed_two, mlp_w[0], precision=highest))
    up_act = low_back(jnp.dot(normed_two, mlp_w[1], precision=highest))
    hidden = low(gate_act * jax.nn.sigmoid(gate_act) * up_act)
    return resid + low_back(jnp.einsum('tf,df->td', hidden, mlp_w[2], precision=highest))

def orthogonalize(matrix):
    frobenius = jnp.sqrt(jnp.sum(matrix * matrix))
    iterate = low(matrix / (frobenius + ortho_eps))
    for repeat_index in range(NS_STEPS):
        gram_low = low(jnp.dot(iterate, iterate.T, precision=highest))
        poly_low = low(coef_b * gram_low + coef_c * jnp.dot(gram_low, gram_low, precision=highest))
        iterate = low(coef_a * iterate + jnp.dot(poly_low, iterate, precision=highest))
    return iterate

def adam_update(parameter, gradient, first_state, second_state):
    first_new = first_decay * first_state + (1.0 - first_decay) * gradient
    second_new = second_decay * second_state + (1.0 - second_decay) * gradient * gradient
    first_hat = first_new / (1.0 - first_decay ** STEP)
    second_hat = second_new / (1.0 - second_decay ** STEP)
    return (parameter - vector_rate * first_hat / (jnp.sqrt(second_hat) + adam_eps), second_new)

def reference(tokens, cotangent, doc_bounds, attn_master, mlp_master, attn_momentum, mlp_momentum, gains, gain_first, gain_second, qkv_bias, bias_first, bias_second):

    def forward(attn_param, mlp_param, gain_param, bias_param, token_values):
        params = (low(attn_param), low(mlp_param), low(gain_param), low(bias_param))

        def one_group(group_data):
            return layer_group(params, group_data[0], group_data[1])
        return lax.map(jax.checkpoint(one_group), (token_values, doc_bounds))
    result, pullback = jax.vjp(forward, attn_master, mlp_master, gains, qkv_bias, tokens.astype(jnp.float32))
    attn_grad, mlp_grad, gain_grad, bias_grad, tokens_grad = pullback(cotangent.astype(jnp.float32))
    attn_mom = momentum_decay * attn_momentum + attn_grad
    mlp_mom = momentum_decay * mlp_momentum + mlp_grad
    ortho_attn = lax.map(orthogonalize, attn_mom)
    ortho_mlp = lax.map(orthogonalize, mlp_mom)
    rms_attn = jnp.sqrt(lax.optimization_barrier(jnp.mean(jnp.square(low(attn_master)), axis=(1, 2))))
    rms_mlp = jnp.sqrt(lax.optimization_barrier(jnp.mean(jnp.square(low(mlp_master)), axis=(1, 2))))
    attn_new = attn_master * (1.0 - matrix_rate * decay_rate) - (matrix_rate * math.sqrt(D) * rms_attn)[:, None, None] * ortho_attn
    mlp_new = mlp_master * (1.0 - matrix_rate * decay_rate) - (matrix_rate * math.sqrt(FF) * rms_mlp)[:, None, None] * ortho_mlp
    gain_new, gain_second_new = adam_update(gains, gain_grad, gain_first, gain_second)
    bias_new, bias_second_new = adam_update(qkv_bias, bias_grad, bias_first, bias_second)
    return (result.astype(jnp.bfloat16), tokens_grad, attn_grad, mlp_grad, attn_mom, mlp_mom, attn_new, mlp_new, gain_grad, gain_second_new, gain_new, bias_grad, bias_second_new, bias_new)
```

```python
import math

import jax
import jax.numpy as jnp
from jax import lax
from jax.sharding import PartitionSpec as P

HEAD_DIM = 64
NS_STEPS = 5
STEP = 10

norm_eps = 1e-06
rope_base = 1000000.0
coef_a = 3.4445
coef_b = -4.775
coef_c = 2.0315
momentum_decay = 0.95
matrix_rate = 0.5
decay_rate = 0.01
first_decay = 0.9
second_decay = 0.95
vector_rate = 0.25
adam_eps = 1e-08
ortho_eps = 1e-07
masked_score = -1e30

MLP_OWNERS = (0, 2, 4)
ATTN_OWNERS = (1, 3, 5, 6)

f32 = jnp.float32
bf16 = jnp.bfloat16


def dot32(a, b, ca, cb):
    return lax.dot_general(a, b, (((ca,), (cb,)), ((), ())), preferred_element_type=f32)


def doc_layout(bounds, length):
    places = jnp.arange(length, dtype=jnp.int32)
    first_bound = bounds[0]
    second_bound = bounds[1]
    doc_index = (places >= first_bound).astype(jnp.int32) + (places >= second_bound).astype(
        jnp.int32
    )
    doc_start = jnp.where(
        places < first_bound, 0, jnp.where(places < second_bound, first_bound, second_bound)
    )
    return (doc_index, (places - doc_start).astype(f32))


def rope_tables(position, head_dim):
    half_dim = head_dim // 2
    frequency = rope_base ** (-2.0 * jnp.arange(half_dim, dtype=f32) / head_dim)
    angles = position[:, None] * frequency[None, :]
    cosine_table = jnp.cos(angles)
    sine_table = jnp.sin(angles)
    return (
        jnp.concatenate([cosine_table, cosine_table], 1),
        jnp.concatenate([sine_table, sine_table], 1),
    )


def rotate_half(values):
    half_dim = values.shape[-1] // 2
    return jnp.concatenate([-values[..., half_dim:], values[..., :half_dim]], axis=-1)


def apply_rope(values, cosine_table, sine_table):
    return values * cosine_table + rotate_half(values) * sine_table


def undo_rope(gradient, cosine_table, sine_table):
    return gradient * cosine_table - rotate_half(gradient * sine_table)


def masked_scores(query, key, doc_index):
    length = key.shape[1]
    places = jnp.arange(length, dtype=jnp.int32)
    allowed = (doc_index[:, None] == doc_index[None, :]) & (places[None, :] <= places[:, None])
    scores = jnp.einsum("hqd,hkd->hqk", query, key, preferred_element_type=f32)
    return jnp.where(allowed[None], scores * HEAD_DIM ** (-0.5), masked_score)


def attend_forward(query, key, value, doc_index):
    scores = masked_scores(query, key, doc_index)
    row_peak = jnp.max(scores, axis=-1, keepdims=True)
    exponent = jnp.exp(scores - row_peak)
    row_total = jnp.sum(exponent, axis=-1, keepdims=True)
    weights = (exponent / row_total).astype(bf16)
    attended = jnp.einsum("hqk,hkd->hqd", weights, value, preferred_element_type=f32)
    return attended.astype(bf16), row_peak + jnp.log(row_total)


def attend_backward(query, key, value, doc_index, log_total, d_attended):
    scores = masked_scores(query, key, doc_index)
    weights = jnp.exp(scores - log_total)
    d_value = jnp.einsum(
        "hqk,hqd->hkd", weights.astype(bf16), d_attended, preferred_element_type=f32
    )
    d_weights = jnp.einsum("hqd,hkd->hqk", d_attended, value, preferred_element_type=f32)
    inner = jnp.sum(weights * d_weights, axis=-1, keepdims=True)
    d_scores = (weights * (d_weights - inner)).astype(bf16)
    scale = HEAD_DIM ** (-0.5)
    d_query = jnp.einsum("hqk,hkd->hqd", d_scores, key, preferred_element_type=f32) * scale
    d_key = jnp.einsum("hqk,hqd->hkd", d_scores, query, preferred_element_type=f32) * scale
    return d_query, d_key, d_value


def norm_backward(d_normed, values, inverse, gain_row):
    scaled = d_normed * gain_row
    gain_part = jnp.sum(d_normed * values * inverse, axis=0)
    d_values = inverse * scaled - values * inverse**3 * jnp.mean(
        scaled * values, axis=-1, keepdims=True
    )
    return (d_values, gain_part)


def orthogonalize(matrix):
    wide = matrix.astype(f32)
    frobenius = jnp.sqrt(jnp.sum(wide * wide))
    iterate = (wide / (frobenius + ortho_eps)).astype(bf16)
    for _ in range(NS_STEPS):
        gram_low = dot32(iterate, iterate, 1, 1).astype(bf16)
        poly_low = (
            coef_b * gram_low.astype(f32) + coef_c * dot32(gram_low, gram_low, 1, 0)
        ).astype(bf16)
        iterate = (coef_a * iterate.astype(f32) + dot32(poly_low, iterate, 1, 0)).astype(bf16)
    return iterate


def adam_update(parameter, gradient, first_state, second_state):
    first_new = first_decay * first_state + (1.0 - first_decay) * gradient
    second_new = second_decay * second_state + (1.0 - second_decay) * gradient * gradient
    first_hat = first_new / (1.0 - first_decay**STEP)
    second_hat = second_new / (1.0 - second_decay**STEP)
    return (parameter - vector_rate * first_hat / (jnp.sqrt(second_hat) + adam_eps), second_new)


def swap(value, axis, bits, count):
    return lax.ppermute(value, axis, [(i, i ^ bits) for i in range(count)])


def sum_all(value, axis, count):
    bits = 1
    while bits < count:
        value = value + swap(value, axis, bits, count)
        bits *= 2
    return value


def gather_wt(block, wt_index, wt_count):
    rows = block.shape[0]
    whole = jnp.zeros((rows * wt_count,) + block.shape[1:], block.dtype)
    zeros = (0,) * (block.ndim - 1)
    for bits in range(wt_count):
        part = block if bits == 0 else swap(block, "wt", bits, wt_count)
        whole = lax.dynamic_update_slice(whole, part, ((wt_index ^ bits) * rows,) + zeros)
    return whole


def scatter_sum_wt(partial, wt_index, wt_count):
    rows = partial.shape[0] // wt_count
    total = lax.dynamic_slice_in_dim(partial, wt_index * rows, rows, 0)
    for bits in range(1, wt_count):
        sent = lax.dynamic_slice_in_dim(partial, (wt_index ^ bits) * rows, rows, 0).astype(bf16)
        total = total + swap(sent, "wt", bits, wt_count).astype(f32)
    return total


def scatter_sum_seq(partial, seq_index, seq_count):
    rows = partial.shape[0] // seq_count
    blocks = partial.reshape((seq_count // 2, 2, rows) + partial.shape[1:])
    core = seq_index % 2
    chip = seq_index // 2
    mine = lax.dynamic_index_in_dim(blocks, core, 1, keepdims=False)
    other = lax.dynamic_index_in_dim(blocks, 1 - core, 1, keepdims=False).astype(bf16)
    pair = mine + swap(other, "seq", 1, seq_count).astype(f32)
    total = lax.dynamic_index_in_dim(pair, chip, 0, keepdims=False)
    for bits in range(1, seq_count // 2):
        sent = lax.dynamic_index_in_dim(pair, chip ^ bits, 0, keepdims=False).astype(bf16)
        total = total + swap(sent, "seq", 2 * bits, seq_count).astype(f32)
    return total


def gather_owned(block, owners, wt_index, wt_count):
    rows, cols = block.shape
    whole = jnp.zeros((rows * wt_count, cols), block.dtype)
    whole = lax.dynamic_update_slice(whole, block, (wt_index * rows, 0))
    for bits in range(1, wt_count):
        pairs = [
            (owner * wt_count + w, owner * wt_count + (w ^ bits))
            for owner in owners
            for w in range(wt_count)
        ]
        part = lax.ppermute(block, ("seq", "wt"), pairs)
        whole = lax.dynamic_update_slice(whole, part, ((wt_index ^ bits) * rows, 0))
    return whole


def spread_owned(rows_block, owners, seq_index, seq_count):
    cols = rows_block.shape[1] // seq_count
    got = []
    for turn in range(seq_count):
        place = (seq_index + turn) % seq_count
        block = lax.dynamic_slice_in_dim(rows_block, place * cols, cols, 1)
        if turn:
            block = lax.ppermute(
                block, "seq", [(owner, (owner + turn) % seq_count) for owner in owners]
            )
        got.append(block)
    got = jnp.stack(got)
    return jnp.stack(
        [
            lax.dynamic_index_in_dim(got, (seq_index - owner) % seq_count, 0, keepdims=False)
            for owner in owners
        ]
    )


def per_device(
    tokens,
    cotangent,
    doc_bounds,
    attn_master,
    mlp_master,
    attn_momentum,
    mlp_momentum,
    gains,
    gain_first,
    gain_second,
    qkv_bias,
    bias_first,
    bias_second,
):
    seq_count = lax.axis_size("seq")
    wt_count = lax.axis_size("wt")
    seq_index = lax.axis_index("seq")
    wt_index = lax.axis_index("wt")
    row_count = tokens.shape[1]
    width = tokens.shape[2]
    ff = mlp_master.shape[2]
    shard = attn_master.shape[1]
    length = row_count * seq_count
    head_cols = width // seq_count
    ff_cols = ff // seq_count
    heads = head_cols // HEAD_DIM

    x_low = lax.all_gather(tokens[0], "seq", axis=0, tiled=True)
    dy_low = lax.all_gather(cotangent[0], "seq", axis=0, tiled=True)

    vectors = jnp.concatenate([gains, qkv_bias, jnp.zeros((3, shard), f32)], 0).astype(bf16)
    vectors = gather_wt(vectors[None], wt_index, wt_count)
    vectors = jnp.moveaxis(vectors, 0, 1).reshape(8, width).astype(f32)
    attn_own = lax.dynamic_slice_in_dim(attn_master, seq_index * head_cols, head_cols, 2)
    mlp_own = lax.dynamic_slice_in_dim(mlp_master, seq_index * ff_cols, ff_cols, 2)
    qkv_w = gather_wt(
        jnp.concatenate([attn_own[0], attn_own[1], attn_own[2]], 1).astype(bf16),
        wt_index,
        wt_count,
    )
    out_w = gather_wt(attn_master[3].astype(bf16), wt_index, wt_count)
    mlp_w = gather_wt(
        jnp.concatenate([mlp_own[0], mlp_own[1], mlp_own[2]], 1).astype(bf16),
        wt_index,
        wt_count,
    )
    gate_up_w = mlp_w[:, : 2 * ff_cols]
    down_w = mlp_w[:, 2 * ff_cols :]

    squares = jnp.concatenate(
        [
            jnp.sum(jnp.square(attn_master.astype(bf16).astype(f32)), axis=(1, 2)),
            jnp.sum(jnp.square(mlp_master.astype(bf16).astype(f32)), axis=(1, 2)),
        ]
    )
    squares = sum_all(jnp.pad(squares, (0, 121))[None], "wt", wt_count)[0]
    rms_attn = jnp.sqrt(squares[:4] / (width * width))
    rms_mlp = jnp.sqrt(squares[4:7] / (width * ff))

    gain_attn = vectors[0]
    gain_mlp = vectors[1]
    x_all = x_low.astype(f32)
    inverse_one = lax.rsqrt(jnp.mean(x_all * x_all, axis=-1, keepdims=True) + norm_eps)
    normed_one = (x_all * inverse_one * gain_attn).astype(bf16)
    bias_own = lax.dynamic_slice_in_dim(vectors[2:5], seq_index * head_cols, head_cols, 1)
    projected = (dot32(normed_one, qkv_w, 1, 0) + bias_own.reshape(1, 3 * head_cols)).astype(bf16)
    projected = jnp.moveaxis(projected.reshape(length, 3, heads, HEAD_DIM), 0, 2)
    doc_index, position = doc_layout(doc_bounds[0], length)
    cosine_table, sine_table = rope_tables(position, HEAD_DIM)
    query = apply_rope(projected[0].astype(f32), cosine_table, sine_table).astype(bf16)
    key = apply_rope(projected[1].astype(f32), cosine_table, sine_table).astype(bf16)
    value = projected[2]
    attended, log_total = attend_forward(query, key, value, doc_index)
    attended = jnp.moveaxis(attended, 0, 1).reshape(length, head_cols)
    attn_all = lax.all_gather(attended, "seq", axis=0)
    attn_all = jnp.moveaxis(attn_all, 0, 1).reshape(length, width)
    resid = x_all + dot32(attn_all, out_w, 1, 0)
    inverse_two = lax.rsqrt(jnp.mean(resid * resid, axis=-1, keepdims=True) + norm_eps)
    normed_two = (resid * inverse_two * gain_mlp).astype(bf16)
    gate_up = dot32(normed_two, gate_up_w, 1, 0)
    gate = gate_up[:, :ff_cols]
    up = gate_up[:, ff_cols:]
    sigmoid = jax.nn.sigmoid(gate)
    silu = gate * sigmoid
    hidden = (silu * up).astype(bf16)

    d_hidden = dot32(dy_low, down_w, 1, 0)
    d_gate = (d_hidden * up * (sigmoid * (1.0 + gate * (1.0 - sigmoid)))).astype(bf16)
    d_up = (d_hidden * silu).astype(bf16)
    d_gate_up = jnp.concatenate([d_gate, d_up], 1)
    d_normed_two = scatter_sum_seq(dot32(d_gate_up, gate_up_w, 1, 1), seq_index, seq_count)
    own_rows = seq_index * row_count
    x_own = tokens[0].astype(f32)
    resid_own = lax.dynamic_slice_in_dim(resid, own_rows, row_count, 0)
    inverse_two_own = lax.dynamic_slice_in_dim(inverse_two, own_rows, row_count, 0)
    d_resid_mlp, gain_part_two = norm_backward(d_normed_two, resid_own, inverse_two_own, gain_mlp)
    d_resid = cotangent[0].astype(f32) + d_resid_mlp
    d_resid_low = d_resid.astype(bf16)
    d_attn = dot32(d_resid_low, out_w, 1, 1).astype(bf16)
    pair = jnp.stack([d_attn, d_resid_low]).reshape(2, row_count, seq_count, head_cols)
    pair = lax.all_to_all(jnp.moveaxis(pair, 2, 0), "seq", split_axis=0, concat_axis=0)
    pair = jnp.moveaxis(pair, 0, 1).reshape(2, length, head_cols)
    d_attended = jnp.moveaxis(pair[0].reshape(length, heads, HEAD_DIM), 1, 0)

    mlp_part = jnp.concatenate(
        [dot32(normed_two, d_gate_up, 0, 0), dot32(dy_low, hidden, 0, 0)], 1
    )
    mlp_share = scatter_sum_wt(mlp_part, wt_index, wt_count).astype(bf16)
    mlp_grad = lax.all_gather(mlp_share, "seq", axis=0)
    mlp_grad = jnp.moveaxis(mlp_grad.reshape(seq_count, shard, 3, ff_cols), 0, 2)
    mlp_grad = mlp_grad.reshape(shard, 3, ff).swapaxes(0, 1).astype(f32)
    mlp_mom = momentum_decay * mlp_momentum + mlp_grad

    d_query, d_key, d_value = attend_backward(
        query, key, value, doc_index, log_total, d_attended
    )
    d_qkv = jnp.stack(
        [
            undo_rope(d_query, cosine_table, sine_table),
            undo_rope(d_key, cosine_table, sine_table),
            d_value,
        ]
    ).astype(bf16)
    d_qkv = jnp.moveaxis(d_qkv, 2, 0).reshape(length, 3 * head_cols)
    attn_part = jnp.concatenate(
        [dot32(normed_one, d_qkv, 0, 0), dot32(attn_all, pair[1], 0, 0)], 1
    )
    attn_share = scatter_sum_wt(attn_part, wt_index, wt_count).astype(bf16)
    attn_grad = lax.all_gather(attn_share, "seq", axis=0)
    attn_grad = jnp.moveaxis(attn_grad.reshape(seq_count, shard, 4, head_cols), 0, 2)
    attn_grad = attn_grad.reshape(shard, 4, width).swapaxes(0, 1).astype(f32)
    attn_mom = momentum_decay * attn_momentum + attn_grad
    bias_part = jnp.sum(d_qkv.astype(f32), axis=0).reshape(3, head_cols)

    mlp_pick = jnp.minimum(seq_index // 2, 2)
    attn_pick = jnp.minimum(seq_index // 2, 3)
    full_mlp = gather_owned(
        lax.dynamic_index_in_dim(mlp_mom, mlp_pick, 0, keepdims=False).astype(bf16),
        MLP_OWNERS,
        wt_index,
        wt_count,
    )
    full_attn = gather_owned(
        lax.dynamic_index_in_dim(attn_mom, attn_pick, 0, keepdims=False).astype(bf16),
        ATTN_OWNERS,
        wt_index,
        wt_count,
    )
    own_mlp = (seq_index == 0) | (seq_index == 2) | (seq_index == 4)
    own_attn = (seq_index == 1) | (seq_index == 3) | (seq_index == 5) | (seq_index == 6)

    def own_block(matrix):
        return lax.dynamic_slice_in_dim(orthogonalize(matrix), wt_index * shard, shard, 0)

    def empty_block(matrix):
        return jnp.zeros((shard, matrix.shape[1]), bf16)

    mlp_rows = lax.cond(own_mlp, own_block, empty_block, full_mlp)
    attn_rows = lax.cond(own_attn, own_block, empty_block, full_attn)
    mlp_steps = spread_owned(mlp_rows, MLP_OWNERS, seq_index, seq_count).astype(f32)
    attn_steps = spread_owned(attn_rows, ATTN_OWNERS, seq_index, seq_count).astype(f32)
    attn_new = (
        attn_own * (1.0 - matrix_rate * decay_rate)
        - (matrix_rate * math.sqrt(width) * rms_attn)[:, None, None] * attn_steps
    )
    mlp_new = (
        mlp_own * (1.0 - matrix_rate * decay_rate)
        - (matrix_rate * math.sqrt(ff) * rms_mlp)[:, None, None] * mlp_steps
    )

    layer_part = scatter_sum_seq(dot32(hidden, down_w, 1, 1), seq_index, seq_count)
    layer_out = (resid_own + layer_part).astype(bf16)
    d_normed_one = scatter_sum_seq(dot32(d_qkv, qkv_w, 1, 1), seq_index, seq_count)
    inverse_one_own = lax.dynamic_slice_in_dim(inverse_one, own_rows, row_count, 0)
    d_input_norm, gain_part_one = norm_backward(d_normed_one, x_own, inverse_one_own, gain_attn)
    tokens_grad = d_resid + d_input_norm

    bias_wide = lax.dynamic_update_slice(
        jnp.zeros((3, width), f32), bias_part, (0, seq_index * head_cols)
    )
    small = jnp.concatenate(
        [gain_part_one[None], gain_part_two[None], bias_wide, jnp.zeros((3, width), f32)], 0
    )
    small = sum_all(sum_all(small, "seq", seq_count), "wt", wt_count)
    small = lax.dynamic_slice_in_dim(small, wt_index * shard, shard, 1)
    gain_grad = small[:2]
    bias_grad = small[2:5]
    gain_new, gain_second_new = adam_update(gains, gain_grad, gain_first, gain_second)
    bias_new, bias_second_new = adam_update(qkv_bias, bias_grad, bias_first, bias_second)
    return (
        layer_out[None],
        tokens_grad[None],
        attn_grad,
        mlp_grad,
        attn_mom,
        mlp_mom,
        attn_new,
        mlp_new,
        gain_grad,
        gain_second_new,
        gain_new,
        bias_grad,
        bias_second_new,
        bias_new,
    )


def solution(mesh):
    return jax.shard_map(
        per_device,
        mesh=mesh,
        in_specs=(
            P("wt", "seq", None),
            P("wt", "seq", None),
            P("wt", None),
            P(None, "wt", None),
            P(None, "wt", None),
            P(None, "wt", None),
            P(None, "wt", None),
            P(None, "wt"),
            P(None, "wt"),
            P(None, "wt"),
            P(None, "wt"),
            P(None, "wt"),
            P(None, "wt"),
        ),
        out_specs=(
            P("wt", "seq", None),
            P("wt", "seq", None),
            P(None, "wt", None),
            P(None, "wt", None),
            P(None, "wt", None),
            P(None, "wt", None),
            P(None, "wt", "seq"),
            P(None, "wt", "seq"),
            P(None, "wt"),
            P(None, "wt"),
            P(None, "wt"),
            P(None, "wt"),
            P(None, "wt"),
            P(None, "wt"),
        ),
        check_vma=False,
    )
```

```python
import functools
import math

import jax
import jax.numpy as jnp
from jax import lax
from jax.experimental import pallas as pl
from jax.experimental.pallas import tpu as pltpu
from jax.sharding import PartitionSpec as P

HEAD_DIM = 64
NS_STEPS = 5
STEP = 10

norm_eps = 1e-06
rope_base = 1000000.0
coef_a = 3.4445
coef_b = -4.775
coef_c = 2.0315
momentum_decay = 0.95
matrix_rate = 0.5
decay_rate = 0.01
first_decay = 0.9
second_decay = 0.95
vector_rate = 0.25
adam_eps = 1e-08
ortho_eps = 1e-07
masked_score = -1e30
tile = 256

MLP_OWNERS = (0, 2, 4)
ATTN_OWNERS = (1, 3, 5, 6)

f32 = jnp.float32
bf16 = jnp.bfloat16


def dot32(a, b, ca, cb):
    return lax.dot_general(a, b, (((ca,), (cb,)), ((), ())), preferred_element_type=f32)


def doc_layout(bounds, length):
    places = jnp.arange(length, dtype=jnp.int32)
    first_bound = bounds[0]
    second_bound = bounds[1]
    doc_index = (places >= first_bound).astype(jnp.int32) + (places >= second_bound).astype(
        jnp.int32
    )
    doc_start = jnp.where(
        places < first_bound, 0, jnp.where(places < second_bound, first_bound, second_bound)
    )
    return (doc_index, (places - doc_start).astype(f32))


def rope_tables(position, cols):
    half_dim = HEAD_DIM // 2
    lane = jnp.arange(cols, dtype=jnp.int32) % HEAD_DIM
    frequency = rope_base ** (-2.0 * jnp.arange(half_dim, dtype=f32) / HEAD_DIM)
    angles = position[:, None] * frequency[None, :]
    repeat = cols // half_dim
    cosine = jnp.concatenate([jnp.cos(angles)] * repeat, 1)
    sine = jnp.concatenate([jnp.sin(angles)] * repeat, 1)
    return cosine, jnp.where(lane < half_dim, -1.0, 1.0)[None, :] * sine


def swap_halves(values):
    half_dim = HEAD_DIM // 2
    parts = []
    for first in range(0, values.shape[1], HEAD_DIM):
        parts.append(values[:, first + half_dim : first + HEAD_DIM])
        parts.append(values[:, first : first + half_dim])
    return jnp.concatenate(parts, axis=1)


def visible(bounds_ref, first, rows, length):
    query = first + lax.broadcasted_iota(jnp.int32, (rows, length), 0)
    key = lax.broadcasted_iota(jnp.int32, (rows, length), 1)
    one, two = bounds_ref[0, 0], bounds_ref[0, 1]
    start = jnp.where(query < one, 0, jnp.where(query < two, one, two))
    return (key <= query) & (key >= start)


def front_kernel(
    bounds_ref,
    place_ref,
    same_ref,
    other_ref,
    weight_ref,
    gain_ref,
    bias_ref,
    cosine_ref,
    sine_ref,
    x_ref,
    normed_ref,
    query_ref,
    key_ref,
    value_ref,
    attended_ref,
    log_ref,
):
    length = x_ref.shape[0]
    cols = query_ref.shape[1]
    chips, rows, _ = same_ref.shape
    for chip in range(chips):
        at = pl.ds(chip * 2 * rows, 2 * rows)
        slot = place_ref[0] ^ chip
        low = pl.ds(chip * 2 * rows + place_ref[1] * rows, rows)
        high = pl.ds(chip * 2 * rows + (1 - place_ref[1]) * rows, rows)
        x_ref[low, :] = same_ref[slot]
        x_ref[high, :] = other_ref[slot]
        x = x_ref[at, :].astype(f32)
        inverse = lax.rsqrt(jnp.mean(x * x, axis=-1, keepdims=True) + norm_eps)
        normed = (x * inverse * gain_ref[...]).astype(bf16)
        normed_ref[at, :] = normed
        projected = (dot32(normed, weight_ref[...], 1, 0) + bias_ref[...]).astype(bf16).astype(f32)
        cosine, sine = cosine_ref[at, :], sine_ref[at, :]
        query = projected[:, :cols]
        key = projected[:, cols : 2 * cols]
        query_ref[at, :] = (query * cosine + swap_halves(query) * sine).astype(bf16)
        key_ref[at, :] = (key * cosine + swap_halves(key) * sine).astype(bf16)
        value_ref[at, :] = projected[:, 2 * cols :].astype(bf16)
    for first in range(0, length, tile):
        at, keys = pl.ds(first, tile), pl.ds(0, first + tile)
        allowed = visible(bounds_ref, first, tile, first + tile)
        attended = []
        for head in range(cols // HEAD_DIM):
            lanes = pl.ds(head * HEAD_DIM, HEAD_DIM)
            scores = dot32(query_ref[at, lanes], key_ref[keys, lanes], 1, 1)
            scores = jnp.where(allowed, scores * HEAD_DIM ** (-0.5), masked_score)
            peak = jnp.max(scores, axis=-1, keepdims=True)
            exponent = jnp.exp(scores - peak)
            total = jnp.sum(exponent, axis=-1, keepdims=True)
            weights = (exponent * (1.0 / total)).astype(bf16)
            attended.append(dot32(weights, value_ref[keys, lanes], 1, 0))
            log_ref[at, pl.ds(head, 1)] = peak + jnp.log(total)
        attended_ref[at, :] = jnp.concatenate(attended, axis=1).astype(bf16)


def vmem_specs(count):
    return [pl.BlockSpec(memory_space=pltpu.VMEM)] * count


def whole_spec(shape):
    return pl.BlockSpec(shape, lambda i: (0,) * len(shape))


def whole_specs(arrays):
    return [whole_spec(value.shape) for value in arrays]


def any_specs(count):
    return [pl.BlockSpec(memory_space=pl.ANY)] * count


def smem_spec():
    return pl.BlockSpec(memory_space=pltpu.SMEM)


def front(bounds, place, same, other, weight, gain, bias, cosine, sine):
    chips, rows, width = same.shape
    length, cols = cosine.shape
    part = jax.ShapeDtypeStruct((length, cols), bf16)
    shapes = [
        jax.ShapeDtypeStruct((length, width), bf16),
        jax.ShapeDtypeStruct((length, width), bf16),
        part,
        part,
        part,
        part,
        jax.ShapeDtypeStruct((length, cols // HEAD_DIM), f32),
    ]
    args = (same, other, weight, gain, bias, cosine, sine)
    return pl.pallas_call(
        front_kernel,
        grid=(1,),
        in_specs=[smem_spec()] * 2 + whole_specs(args),
        out_specs=whole_specs(shapes),
        out_shape=shapes,
        compiler_params=pltpu.CompilerParams(vmem_limit_bytes=56 * 2**20),
        cost_estimate=pl.CostEstimate(
            flops=8 * 10**9, bytes_accessed=8 * 10**6, transcendentals=2 * 10**6
        ),
        name="front",
    )(bounds, place, *args)


def store_split(place_ref, mine_ref, other_ref, index, value):
    chips, _, rows, _ = mine_ref.shape
    core = place_ref[1]
    for at in range(chips):
        slot = at ^ (place_ref[0] & (chips - 1))
        top = value[2 * at * rows : (2 * at + 1) * rows]
        low = value[(2 * at + 1) * rows : (2 * at + 2) * rows]
        mine_ref[slot, index] = jnp.where(core == 0, top, low)
        other_ref[slot, index] = jnp.where(core == 0, low, top).astype(bf16)


def split_out(chips, step, sums, rows, width):
    spec = pl.BlockSpec(
        (step, sums, rows, width), lambda i, place: (i ^ (place[0] // step), 0, 0, 0)
    )
    shape = (chips, sums, rows, width)
    return [spec, spec], [jax.ShapeDtypeStruct(shape, f32), jax.ShapeDtypeStruct(shape, bf16)]


def middle_kernel(
    place_ref,
    attended_ref,
    x_ref,
    dy_ref,
    weight_ref,
    gain_ref,
    normed_ref,
    d_gate_ref,
    d_up_ref,
    hidden_ref,
    d_mine_ref,
    d_other_ref,
    resid_ref,
):
    width = x_ref.shape[1]
    cols = d_gate_ref.shape[1]
    count = attended_ref.shape[0]
    chips, _, rows, _ = d_mine_ref.shape
    gate_w = weight_ref.at[:, pl.ds(width, cols)]
    up_w = weight_ref.at[:, pl.ds(width + cols, cols)]
    down_w = weight_ref.at[:, pl.ds(width + 2 * cols, cols)]
    attended = jnp.concatenate([attended_ref[part] for part in range(count)], axis=1)
    resid = x_ref[...].astype(f32) + dot32(attended, weight_ref[:, pl.ds(0, width)], 1, 0)
    for at in range(2 * chips):

        @pl.when(pl.program_id(0) * 2 * chips + at == place_ref[0] * 2 + place_ref[1])
        def _():
            resid_ref[...] = resid[at * rows : (at + 1) * rows]

    inverse = lax.rsqrt(jnp.mean(resid * resid, axis=-1, keepdims=True) + norm_eps)
    normed = (resid * inverse * gain_ref[...]).astype(bf16)
    normed_ref[...] = normed
    gate = dot32(normed, gate_w[...], 1, 0)
    up = dot32(normed, up_w[...], 1, 0)
    d_hidden = dot32(dy_ref[...], down_w[...], 1, 0)
    sigmoid = jax.nn.sigmoid(gate)
    silu = gate * sigmoid
    hidden = (silu * up).astype(bf16)
    hidden_ref[...] = hidden
    d_gate = (d_hidden * up * (sigmoid * (1.0 + gate * (1.0 - sigmoid)))).astype(bf16)
    d_up = (d_hidden * silu).astype(bf16)
    d_gate_ref[...] = d_gate
    d_up_ref[...] = d_up
    d_normed = dot32(d_gate, gate_w[...], 1, 1) + dot32(d_up, up_w[...], 1, 1)
    store_split(place_ref, d_mine_ref, d_other_ref, 0, d_normed)


def middle(place, attended, x, dy, weight, gain):
    count, length, head_cols = attended.shape
    width = x.shape[1]
    cols = (weight.shape[1] - width) // 3
    chips = count // 2
    half = length // count
    step = 1
    rows = step * 2 * half

    def block(size):
        return pl.BlockSpec((rows, size), lambda i, place: (i, 0))

    def whole(shape):
        return pl.BlockSpec(shape, lambda i, place: (0,) * len(shape))

    split_specs, split_shapes = split_out(chips, step, 1, half, width)
    wide = jax.ShapeDtypeStruct((length, cols), bf16)
    return pl.pallas_call(
        middle_kernel,
        grid_spec=pltpu.PrefetchScalarGridSpec(
            num_scalar_prefetch=1,
            grid=(chips // step,),
            in_specs=[
                pl.BlockSpec((count, rows, head_cols), lambda i, place: (0, i, 0)),
                block(width),
                block(width),
                whole(weight.shape),
                whole(gain.shape),
            ],
            out_specs=[
                block(width),
                block(cols),
                block(cols),
                block(cols),
                *split_specs,
                whole((half, width)),
            ],
        ),
        out_shape=[
            jax.ShapeDtypeStruct((length, width), bf16),
            wide,
            wide,
            wide,
            *split_shapes,
            jax.ShapeDtypeStruct((half, width), f32),
        ],
        compiler_params=pltpu.CompilerParams(vmem_limit_bytes=56 * 2**20),
        cost_estimate=pl.CostEstimate(
            flops=10 * 10**9, bytes_accessed=20 * 10**6, transcendentals=10**6
        ),
        name="middle",
    )(place, attended, x, dy, weight, gain)


def pair_kernel(mine_ref, got_ref, *outs):
    outs[0][...] = mine_ref[0] + got_ref[0].astype(f32)
    for slot in range(1, len(outs)):
        outs[slot][...] = (mine_ref[slot] + got_ref[slot].astype(f32)).astype(bf16)


def pair_sums(mine, got):
    chips = mine.shape[0]
    shapes = [jax.ShapeDtypeStruct(mine.shape[1:], f32)]
    shapes += [jax.ShapeDtypeStruct(mine.shape[1:], bf16)] * (chips - 1)
    return pl.pallas_call(
        pair_kernel,
        grid=(1,),
        in_specs=whole_specs((mine, got)),
        out_specs=whole_specs(shapes),
        out_shape=shapes,
        compiler_params=pltpu.CompilerParams(vmem_limit_bytes=48 * 2**20),
        name="pair_sums",
    )(mine, got)


def post_kernel(
    own_ref, resid_ref, dy_ref, gain_ref, weight_ref, *refs
):
    arrived, (pair_ref, d_resid_ref, gain_part_ref) = refs[:-3], refs[-3:]
    d_normed = own_ref[0]
    for ref in arrived:
        d_normed = d_normed + ref[0].astype(f32)
    resid = resid_ref[...]
    inverse = lax.rsqrt(jnp.mean(resid * resid, axis=-1, keepdims=True) + norm_eps)
    scaled = d_normed * gain_ref[...]
    gain_part_ref[...] = jnp.sum(d_normed * resid * inverse, axis=0, keepdims=True)
    d_resid = (
        dy_ref[...].astype(f32)
        + inverse * scaled
        - resid * (inverse * inverse * inverse) * jnp.mean(scaled * resid, axis=-1, keepdims=True)
    )
    d_resid_ref[...] = d_resid
    low = d_resid.astype(bf16)
    d_attn = dot32(low, weight_ref[...], 1, 1).astype(bf16)
    cols = pair_ref.shape[3]
    for part in range(pair_ref.shape[0]):
        pair_ref[part, 0] = d_attn[:, part * cols : (part + 1) * cols]
        pair_ref[part, 1] = low[:, part * cols : (part + 1) * cols]


def post(own, arrived, resid, dy, gain, weight, count):
    rows, width = resid.shape
    cols = width // count

    def whole(shape):
        return pl.BlockSpec(shape, lambda i: (0,) * len(shape))

    return pl.pallas_call(
        post_kernel,
        grid=(1,),
        in_specs=[whole(own.shape), whole(resid.shape), whole(dy.shape), whole(gain.shape)]
        + [whole((width, width))]
        + [whole(value.shape) for value in arrived],
        out_specs=[whole((count, 2, rows, cols)), whole((rows, width)), whole((1, width))],
        out_shape=[
            jax.ShapeDtypeStruct((count, 2, rows, cols), bf16),
            jax.ShapeDtypeStruct((rows, width), f32),
            jax.ShapeDtypeStruct((1, width), f32),
        ],
        compiler_params=pltpu.CompilerParams(vmem_limit_bytes=40 * 2**20),
        name="post",
    )(own, resid, dy, gain, weight, *arrived)


def mlp_grads_kernel(parts, control_ref, normed_ref, dy_ref, d_gate_ref, d_up_ref, hidden_ref, *outs):
    shard = outs[0].shape[1]
    for part in range(parts):
        at = pl.ds(pl.multiple_of((control_ref[2] ^ part) * shard, 128), shard)
        normed = normed_ref[:, at]
        outs[part][0] = dot32(normed, d_gate_ref[...], 0, 0).astype(bf16)
        outs[part][1] = dot32(normed, d_up_ref[...], 0, 0).astype(bf16)
        outs[part][2] = dot32(dy_ref[:, at], hidden_ref[...], 0, 0).astype(bf16)


def mlp_grads(control, normed, dy, d_gate, d_up, hidden, parts):
    length, width = normed.shape
    cols = hidden.shape[1]
    args = (normed, dy, d_gate, d_up, hidden)
    shapes = [jax.ShapeDtypeStruct((3, width // parts, cols), bf16)] * parts
    return pl.pallas_call(
        functools.partial(mlp_grads_kernel, parts),
        grid=(1,),
        in_specs=[smem_spec()] + whole_specs(args),
        out_specs=whole_specs(shapes),
        out_shape=shapes,
        compiler_params=pltpu.CompilerParams(vmem_limit_bytes=56 * 2**20),
        cost_estimate=pl.CostEstimate(
            flops=3 * 10**9, bytes_accessed=9 * 10**6, transcendentals=0
        ),
        name="mlp_grads",
    )(control, *args)


def back_kernel(
    parts,
    bounds_ref,
    control_ref,
    query_ref,
    key_ref,
    value_ref,
    log_ref,
    arrived_ref,
    normed_ref,
    attended_ref,
    cosine_ref,
    sine_ref,
    d_qkv_ref,
    bias_ref,
    *refs,
):
    grads_refs, (d_key_ref, d_value_ref, d_attn_ref, d_resid_ref) = refs[:parts], refs[parts:]
    length, cols = query_ref.shape
    count, _, rows, _ = arrived_ref.shape
    scale = HEAD_DIM ** (-0.5)
    for part in range(count):
        d_attn_ref[pl.ds(part * rows, rows), :] = arrived_ref[part, 0]
        d_resid_ref[pl.ds(part * rows, rows), :] = arrived_ref[part, 1]
    d_key_ref[...] = jnp.zeros_like(d_key_ref)
    d_value_ref[...] = jnp.zeros_like(d_value_ref)

    def undo(values, at):
        return values * cosine_ref[at, :] - swap_halves(values) * sine_ref[at, :]

    for first in range(0, length, tile):
        at, keys = pl.ds(first, tile), pl.ds(0, first + tile)
        allowed = visible(bounds_ref, first, tile, first + tile)
        d_query, d_key, d_value = [], [], []
        for head in range(cols // HEAD_DIM):
            lanes = pl.ds(head * HEAD_DIM, HEAD_DIM)
            query, d_out = query_ref[at, lanes], d_attn_ref[at, lanes]
            key, value = key_ref[keys, lanes], value_ref[keys, lanes]
            scores = jnp.where(allowed, dot32(query, key, 1, 1) * scale, masked_score)
            weights = jnp.exp(scores - log_ref[at, pl.ds(head, 1)])
            d_value.append(dot32(weights.astype(bf16), d_out, 0, 0))
            d_weights = dot32(d_out, value, 1, 1)
            inner = jnp.sum(weights * d_weights, axis=-1, keepdims=True)
            d_scores = (weights * (d_weights - inner)).astype(bf16)
            d_query.append(dot32(d_scores, key, 1, 0) * scale)
            d_key.append(dot32(d_scores, query, 0, 0) * scale)
        d_key_ref[keys, :] += jnp.concatenate(d_key, axis=1)
        d_value_ref[keys, :] += jnp.concatenate(d_value, axis=1)
        d_qkv_ref[at, pl.ds(0, cols)] = undo(jnp.concatenate(d_query, axis=1), at).astype(bf16)
    for first in range(0, length, tile):
        at = pl.ds(first, tile)
        d_qkv_ref[at, pl.ds(cols, cols)] = undo(d_key_ref[at, :], at).astype(bf16)
        d_qkv_ref[at, pl.ds(2 * cols, cols)] = d_value_ref[at, :].astype(bf16)
    bias_ref[...] = jnp.sum(d_qkv_ref[...].astype(f32), axis=0, keepdims=True)
    shard, pad = grads_refs[0].shape[1:]
    for part in range(parts):
        block = control_ref[2] ^ part
        grads_ref = grads_refs[part]
        at = pl.ds(pl.multiple_of(block * shard, 128), shard)
        grads = dot32(normed_ref[:, at], d_qkv_ref[...], 0, 0).astype(bf16)
        for index in range(3):
            grads_ref[index, :, pl.ds(0, cols)] = grads[:, index * cols : (index + 1) * cols]
        for piece in range(shard // cols):
            grads_ref[3, pl.ds(piece * cols, cols), pl.ds(0, cols)] = dot32(
                attended_ref[block * (shard // cols) + piece], d_resid_ref[...], 0, 0
            ).astype(bf16)
        if pad > cols:
            grads_ref[:, :, pl.ds(cols, pad - cols)] = jnp.zeros((4, shard, pad - cols), bf16)


def back(bounds, control, query, key, value, log_total, arrived, normed, attended, cosine, sine, parts):
    length, cols = query.shape
    width = normed.shape[1]
    pad = -(-cols // 128) * 128
    args = (query, key, value, log_total, arrived, normed, attended, cosine, sine)
    shapes = [
        jax.ShapeDtypeStruct((length, 3 * cols), bf16),
        jax.ShapeDtypeStruct((1, 3 * cols), f32),
    ]
    shapes += [jax.ShapeDtypeStruct((4, width // parts, pad), bf16)] * parts
    results = pl.pallas_call(
        functools.partial(back_kernel, parts),
        grid=(1,),
        in_specs=[smem_spec()] * 2 + whole_specs(args),
        out_specs=whole_specs(shapes),
        out_shape=shapes,
        scratch_shapes=[
            pltpu.VMEM((length, cols), f32),
            pltpu.VMEM((length, cols), f32),
            pltpu.VMEM((length, cols), bf16),
            pltpu.VMEM((length, cols), bf16),
        ],
        compiler_params=pltpu.CompilerParams(vmem_limit_bytes=48 * 2**20),
        cost_estimate=pl.CostEstimate(
            flops=10 * 10**9, bytes_accessed=8 * 10**6, transcendentals=2 * 10**6
        ),
        name="back",
    )(bounds, control, *args)
    return results[0], results[1], results[2:]


def late_kernel(place_ref, hidden_ref, down_ref, d_qkv_ref, weight_ref, mine_ref, other_ref):
    store_split(place_ref, mine_ref, other_ref, 0, dot32(hidden_ref[...], down_ref[...], 1, 1))
    store_split(place_ref, mine_ref, other_ref, 1, dot32(d_qkv_ref[...], weight_ref[...], 1, 1))


def late_sums(place, hidden, wide_w, d_qkv, weight, count):
    length, cols = d_qkv.shape
    width = weight.shape[0]
    pad = hidden.shape[1]
    down = wide_w[:, wide_w.shape[1] - pad :]
    chips = count // 2
    half = length // count
    step = 2
    rows = step * 2 * half
    split_specs, split_shapes = split_out(chips, step, 2, half, width)
    return pl.pallas_call(
        late_kernel,
        grid_spec=pltpu.PrefetchScalarGridSpec(
            num_scalar_prefetch=1,
            grid=(chips // step,),
            in_specs=[
                pl.BlockSpec((rows, pad), lambda i, place: (i, 0)),
                pl.BlockSpec(down.shape, lambda i, place: (0, 0)),
                pl.BlockSpec((rows, cols), lambda i, place: (i, 0)),
                pl.BlockSpec(weight.shape, lambda i, place: (0, 0)),
            ],
            out_specs=split_specs,
        ),
        out_shape=split_shapes,
        compiler_params=pltpu.CompilerParams(vmem_limit_bytes=48 * 2**20),
        cost_estimate=pl.CostEstimate(
            flops=2 * 10**9, bytes_accessed=16 * 10**6, transcendentals=0
        ),
        name="late_sums",
    )(place, hidden, down, d_qkv, weight)


def picked_kernel(pick_ref, momentum_ref, out_ref):
    count, rows, pad = out_ref.shape
    cols = momentum_ref.shape[2] // count
    for turn in range(count):
        value = momentum_ref[0, :, pl.ds(turn * cols, cols)] * momentum_decay
        out_ref[turn, :, pl.ds(0, cols)] = value
        if pad > cols:
            out_ref[turn, :, pl.ds(cols, pad - cols)] = jnp.zeros((rows, pad - cols), f32)


def picked(momentum, pick, count):
    rows, width = momentum.shape[1:]
    pad = -(-(width // count) // 128) * 128
    step = min(64, rows)
    return pl.pallas_call(
        picked_kernel,
        grid_spec=pltpu.PrefetchScalarGridSpec(
            num_scalar_prefetch=1,
            grid=(rows // step,),
            in_specs=[pl.BlockSpec((1, step, width), lambda i, pick: (pick[0], i, 0))],
            out_specs=pl.BlockSpec((count, step, pad), lambda i, pick: (0, i, 0)),
        ),
        out_shape=jax.ShapeDtypeStruct((count, rows, pad), f32),
        compiler_params=pltpu.CompilerParams(vmem_limit_bytes=40 * 2**20),
        cost_estimate=pl.CostEstimate(
            flops=rows * width, bytes_accessed=8 * rows * width, transcendentals=0
        ),
        name="picked",
    )(pick, momentum)


def squares_kernel(order_ref, attn_ref, mlp_ref, out_ref):
    @pl.when(pl.program_id(0) == 0)
    def _():
        out_ref[...] = jnp.zeros_like(out_ref)

    at = 0
    for ref in (attn_ref, mlp_ref):
        for index in range(ref.shape[0]):
            value = ref[index].astype(bf16).astype(f32)
            total = jnp.sum(jnp.sum(value * value, axis=0, keepdims=True), axis=1, keepdims=True)
            out_ref[pl.ds(at, 1), :] += jnp.broadcast_to(total, (1, out_ref.shape[1]))
            at += 1


def sums_of_squares(order, attn, mlp):
    rows = attn.shape[1]
    step = min(64, rows)
    return pl.pallas_call(
        squares_kernel,
        grid=(rows // step,),
        in_specs=[
            smem_spec(),
            pl.BlockSpec((attn.shape[0], step, attn.shape[2]), lambda i: (0, i, 0)),
            pl.BlockSpec((mlp.shape[0], step, mlp.shape[2]), lambda i: (0, i, 0)),
        ],
        out_specs=pl.BlockSpec((8, 128), lambda i: (0, 0)),
        out_shape=jax.ShapeDtypeStruct((8, 128), f32),
        compiler_params=pltpu.CompilerParams(vmem_limit_bytes=40 * 2**20),
        cost_estimate=pl.CostEstimate(
            flops=2 * (attn.size + mlp.size),
            bytes_accessed=4 * (attn.size + mlp.size),
            transcendentals=0,
        ),
        name="sums_of_squares",
    )(order, attn, mlp)


def assemble_kernel(places, wt_ref, *refs):
    pieces, out_ref, arrived = refs[: len(places)], refs[-2], refs[-1]
    copies = []
    for at, (bits, first, rows) in enumerate(places):
        start = pl.multiple_of((wt_ref[0] ^ bits) * rows + first, 16)
        target = out_ref.at[pl.ds(start, pieces[at].shape[0]), :]
        copies.append(pltpu.make_async_copy(pieces[at], target, arrived.at[at]))
    for copy in copies:
        copy.start()
    for copy in copies:
        copy.wait()


def assemble(wt_index, pieces, places, rows):
    size = rows * pieces[0].shape[1]
    return pl.pallas_call(
        functools.partial(assemble_kernel, places),
        in_specs=[smem_spec()] + any_specs(len(pieces)),
        out_specs=vmem_specs(1)[0],
        out_shape=jax.ShapeDtypeStruct((rows, pieces[0].shape[1]), pieces[0].dtype),
        scratch_shapes=[pltpu.SemaphoreType.DMA((len(pieces),))],
        compiler_params=pltpu.CompilerParams(vmem_limit_bytes=24 * 2**20),
        cost_estimate=pl.CostEstimate(flops=0, bytes_accessed=4 * size, transcendentals=0),
        name="assemble",
    )(wt_index.reshape(1), *pieces)


def norm_backward(d_normed, values, inverse, gain_row):
    scaled = d_normed * gain_row
    gain_part = jnp.sum(d_normed * values * inverse, axis=0)
    d_values = inverse * scaled - values * inverse**3 * jnp.mean(
        scaled * values, axis=-1, keepdims=True
    )
    return (d_values, gain_part)


def ortho_kernel(parts, count, extra, control_ref, *refs):
    blocks = refs[:parts]
    refs = refs[extra:]
    outs = refs[parts : parts + count]
    whole, gram, prod, gram_low, prod_low, poly_low, rows, arrived = refs[parts + count :]
    shard, pad = outs[0].shape
    width = gram.shape[0]
    tiles = width // tile

    def upper(j):
        return pl.ds(0, (j + 1) * tile), pl.ds(j * tile, tile)

    def mirror(low):
        for j in range(1, tiles):
            for i in range(j):
                here, there = pl.ds(i * tile, tile), pl.ds(j * tile, tile)
                low[there, here] = low[here, there].T

    @pl.when(control_ref[0] == 1)
    def _():
        copies = [
            [
                pltpu.make_async_copy(
                    blocks[part].at[turn],
                    whole.at[pl.ds(part * shard, shard), pl.ds(turn * pad, pad)],
                    arrived.at[part, turn],
                )
                for turn in range(count)
            ]
            for part in range(parts)
        ]
        for part in range(parts):
            for copy in copies[part]:
                copy.start()
        diagonal = lax.broadcasted_iota(jnp.int32, (tile, tile), 0) == lax.broadcasted_iota(
            jnp.int32, (tile, tile), 1
        )
        squares = jnp.zeros((1, 1), f32)
        for j in range(tiles):
            for part in range(j * tile // shard, (j + 1) * tile // shard):
                for copy in copies[part]:
                    copy.wait()
            up, at = upper(j)
            gram[up, at] = dot32(whole[up, :], whole[at, :], 1, 1)
            entries = jnp.where(diagonal, gram[at, at], 0.0)
            squares = squares + jnp.sum(
                jnp.sum(entries, axis=1, keepdims=True), axis=0, keepdims=True
            )
        inverse = 1.0 / (jnp.sqrt(squares) + ortho_eps)
        for j in range(tiles):
            up, at = upper(j)
            scaled = gram[up, at] * (inverse * inverse)
            gram[up, at] = scaled
            gram_low[up, at] = scaled.astype(bf16)
        mirror(gram_low)

        def step(index, carry):
            poly = poly_low.at[index]
            for j in range(tiles):
                up, at = upper(j)
                poly[up, at] = (
                    coef_b * gram[up, at] + coef_c * dot32(gram_low[up, :], gram_low[:, at], 1, 0)
                ).astype(bf16)
            mirror(poly)
            for j in range(tiles):
                up, at = upper(j)
                value = coef_a * gram[up, at] + dot32(poly[up, :], gram_low[:, at], 1, 0)
                prod[up, at] = value
                prod_low[up, at] = value.astype(bf16)
            mirror(prod_low)
            for j in range(tiles):
                up, at = upper(j)
                value = coef_a * prod[up, at] + dot32(prod_low[up, :], poly[:, at], 1, 0)
                gram[up, at] = value
                gram_low[up, at] = value.astype(bf16)
            mirror(gram_low)
            return carry

        lax.fori_loop(0, NS_STEPS - 1, step, 0)
        unit = lax.broadcasted_iota(jnp.int32, (shard, width), 0) == lax.broadcasted_iota(
            jnp.int32, (shard, width), 1
        )
        rows[...] = (
            coef_a * unit.astype(f32)
            + coef_b * gram[pl.ds(0, shard), :]
            + coef_c * dot32(gram_low[pl.ds(0, shard), :], gram_low[...], 1, 0)
        )

        def apply(index, carry):
            value = rows[...]
            rows[...] = coef_a * value + dot32(
                value.astype(bf16), poly_low[NS_STEPS - 2 - index], 1, 0
            )
            return carry

        lax.fori_loop(0, NS_STEPS - 1, apply, 0)
        scaled = (rows[...] * inverse).astype(bf16)
        for turn in range(count):
            place = lax.rem(control_ref[1] + turn, count)
            lanes = pl.ds(pl.multiple_of(place * pad, 128), pad)
            outs[turn][...] = dot32(scaled, whole[:, lanes], 1, 0).astype(bf16)


def orthogonalize(control, blocks, after):
    count, shard, pad = blocks[0].shape
    parts = len(blocks)
    width = shard * parts
    return pl.pallas_call(
        functools.partial(ortho_kernel, parts, count, len(after)),
        out_shape=[jax.ShapeDtypeStruct((shard, pad), bf16)] * count,
        in_specs=[smem_spec()] + any_specs(parts + len(after)),
        out_specs=vmem_specs(count),
        scratch_shapes=[
            pltpu.VMEM((width, count * pad), bf16),
            pltpu.VMEM((width, width), f32),
            pltpu.VMEM((width, width), f32),
            pltpu.VMEM((width, width), bf16),
            pltpu.VMEM((width, width), bf16),
            pltpu.VMEM((NS_STEPS - 1, width, width), bf16),
            pltpu.VMEM((shard, width), f32),
            pltpu.SemaphoreType.DMA((parts, count)),
        ],
        compiler_params=pltpu.CompilerParams(vmem_limit_bytes=56 * 2**20),
        cost_estimate=pl.CostEstimate(
            flops=30 * 10**9, bytes_accessed=4 * count * shard * pad, transcendentals=0
        ),
        name="orthogonalize",
    )(control, *blocks, *after)


def update_kernel(owners, control_ref, rate_ref, own_ref, *refs):
    arrived, out_ref = refs[:-1], refs[-1]
    count, cols = len(arrived), own_ref.shape[2]
    for index, owner in enumerate(owners):
        turn = lax.rem(control_ref[1] - owner + count, count)
        for at in range(count):

            @pl.when(turn == at)
            def _():
                out_ref[index] = (
                    own_ref[index] * (1.0 - matrix_rate * decay_rate)
                    - rate_ref[index] * arrived[at][:, pl.ds(0, cols)].astype(f32)
                )


def update(control, rate, own, arrived, owners):
    return pl.pallas_call(
        functools.partial(update_kernel, owners),
        grid=(1,),
        in_specs=[smem_spec()] * 2 + whole_specs((own, *arrived)),
        out_specs=whole_spec(own.shape),
        out_shape=jax.ShapeDtypeStruct(own.shape, f32),
        compiler_params=pltpu.CompilerParams(vmem_limit_bytes=40 * 2**20),
        name="update",
    )(control, rate, own, *arrived)


def finish_kernel(share_ref, momentum_ref, grad_ref, new_ref):
    count, matrices = share_ref.shape[:2]
    cols = grad_ref.shape[2] // count
    for index in range(matrices):
        for turn in range(count):
            at = pl.ds(turn * cols, cols)
            grad = share_ref[turn, index].astype(f32)[:, :cols]
            grad_ref[index, :, at] = grad
            new_ref[index, :, at] = momentum_decay * momentum_ref[index, :, at] + grad


def finish(share, momentum):
    count, matrices, shard, pad = share.shape
    width = momentum.shape[2]
    step = min(64, shard)
    whole = pl.BlockSpec((matrices, step, width), lambda i: (0, i, 0))
    size = matrices * shard * width
    return pl.pallas_call(
        finish_kernel,
        grid=(shard // step,),
        in_specs=[pl.BlockSpec((count, matrices, step, pad), lambda i: (0, 0, i, 0)), whole],
        out_specs=[whole, whole],
        out_shape=[jax.ShapeDtypeStruct(momentum.shape, f32)] * 2,
        compiler_params=pltpu.CompilerParams(vmem_limit_bytes=40 * 2**20),
        cost_estimate=pl.CostEstimate(
            flops=2 * size, bytes_accessed=14 * size, transcendentals=0
        ),
        name="finish",
    )(share, momentum)


def adam_update(parameter, gradient, first_state, second_state):
    first_new = first_decay * first_state + (1.0 - first_decay) * gradient
    second_new = second_decay * second_state + (1.0 - second_decay) * gradient * gradient
    first_hat = first_new / (1.0 - first_decay**STEP)
    second_hat = second_new / (1.0 - second_decay**STEP)
    return (parameter - vector_rate * first_hat / (jnp.sqrt(second_hat) + adam_eps), second_new)


def swap(value, axis, bits, count):
    return lax.ppermute(value, axis, [(i, i ^ bits) for i in range(count)])


def sum_all(value, axis, count):
    bits = 1
    while bits < count:
        value = value + swap(value, axis, bits, count)
        bits *= 2
    return value


def near_wt(block, wt_count):
    return [swap(block, "wt", bits, wt_count) for bits in range(1, min(wt_count, 3))]


def gather_wt(block, near, wt_index, wt_count):
    rows = block.shape[0]
    pieces = [block] + near
    places = [(bits, 0, rows) for bits in range(len(pieces))]
    if wt_count == 4:
        half = rows // 2
        pieces.append(swap(near[0][:half], "wt", 2, wt_count))
        pieces.append(swap(near[1][half:], "wt", 1, wt_count))
        places += [(3, 0, rows), (3, half, rows)]
    else:
        for bits in range(3, wt_count):
            pieces.append(swap(block, "wt", bits, wt_count))
            places.append((bits, 0, rows))
    return assemble(wt_index, pieces, places, rows * wt_count)


def sum_wt(parts, wt_count):
    total = parts[0].astype(f32)
    for bits in range(1, wt_count):
        total = total + swap(parts[bits], "wt", bits, wt_count).astype(f32)
    return total.astype(bf16)


def send_chips(sums, seq_count):
    return [swap(value, "seq", 2 * bits, seq_count) for bits, value in enumerate(sums) if bits]


def gather_owned(block, owners, wt_count):
    blocks = [block]
    for bits in range(1, wt_count):
        pairs = [
            (owner * wt_count + w, owner * wt_count + (w ^ bits))
            for owner in owners
            for w in range(wt_count)
        ]
        blocks.append(lax.ppermute(block, ("seq", "wt"), pairs))
    return blocks


def spread_owned(blocks, owners, seq_count):
    return [blocks[0]] + [
        lax.ppermute(
            blocks[turn], "seq", [(owner, (owner + turn) % seq_count) for owner in owners]
        )
        for turn in range(1, seq_count)
    ]


def per_device(
    tokens,
    cotangent,
    doc_bounds,
    attn_master,
    mlp_master,
    attn_momentum,
    mlp_momentum,
    gains,
    gain_first,
    gain_second,
    qkv_bias,
    bias_first,
    bias_second,
):
    seq_count = lax.axis_size("seq")
    wt_count = lax.axis_size("wt")
    seq_index = lax.axis_index("seq")
    wt_index = lax.axis_index("wt")
    row_count = tokens.shape[1]
    width = tokens.shape[2]
    ff = mlp_master.shape[2]
    shard = attn_master.shape[1]
    length = row_count * seq_count
    head_cols = width // seq_count
    ff_cols = ff // seq_count

    place = jnp.stack([seq_index // 2, seq_index % 2])

    x_same = jnp.stack(
        [tokens[0]]
        + [swap(tokens[0], "seq", 2 * bits, seq_count) for bits in range(1, seq_count // 2)]
    )
    x_other = swap(x_same, "seq", 1, seq_count)
    dy_low = lax.all_gather(cotangent[0], "seq", axis=0, tiled=True)

    attn_own = lax.dynamic_slice_in_dim(attn_master, seq_index * head_cols, head_cols, 2)
    mlp_own = lax.dynamic_slice_in_dim(mlp_master, seq_index * ff_cols, ff_cols, 2)
    vectors = jnp.pad(jnp.concatenate([gains, qkv_bias], 0), ((0, 11), (0, 3 * head_cols - shard)))
    qkv_w = jnp.concatenate([attn_own[0], attn_own[1], attn_own[2]], 1)
    qkv_w = jnp.concatenate([qkv_w, vectors], 0).astype(bf16)
    qkv_w = lax.all_gather(qkv_w, "wt", axis=0)
    vectors = jnp.moveaxis(qkv_w[:, shard : shard + 5, :shard], 0, 1).reshape(5, width).astype(f32)
    qkv_w = qkv_w[:, :shard].reshape(width, 3 * head_cols)
    ff_pad = -(-ff_cols // 128) * 128
    wide_w = jnp.pad(mlp_own, ((0, 0), (0, 0), (0, ff_pad - ff_cols)))
    wide_w = jnp.concatenate([attn_master[3], wide_w[0], wide_w[1], wide_w[2]], 1).astype(bf16)
    wide_near = near_wt(wide_w, wt_count)
    x_other, wide_near = lax.optimization_barrier((x_other, wide_near))
    wide_w = gather_wt(wide_w, wide_near, wt_index, wt_count)

    bias_own = lax.dynamic_slice_in_dim(vectors[2:5], seq_index * head_cols, head_cols, 1)
    _, position = doc_layout(doc_bounds[0], length)
    cosine, sine = rope_tables(position, head_cols)
    x_low, normed_one, query, key, value, attended, log_total = front(
        doc_bounds,
        place,
        x_same,
        x_other,
        qkv_w,
        vectors[0:1],
        bias_own.reshape(1, 3 * head_cols),
        cosine,
        sine,
    )
    attended, dy_low = lax.optimization_barrier((attended, dy_low))
    attn_all = lax.all_gather(attended, "seq", axis=0)

    mlp_pick = jnp.minimum(seq_index // 2, 2).reshape(1)
    attn_pick = jnp.minimum(seq_index // 2, 3).reshape(1)
    mlp_pick, attn_pick, wide_w, attended = lax.optimization_barrier(
        (mlp_pick, attn_pick, wide_w, attended)
    )
    squares = sums_of_squares(mlp_pick, attn_master, mlp_master)
    mlp_old = picked(mlp_momentum, mlp_pick, seq_count)
    attn_old = picked(attn_momentum, attn_pick, seq_count)
    attn_all, squares, mlp_old, attn_old = lax.optimization_barrier(
        (attn_all, squares, mlp_old, attn_old)
    )

    normed_two, d_gate, d_up, hidden, d_mine, d_other, resid_own = middle(
        place, attn_all, x_low, dy_low, wide_w, vectors[1:2]
    )

    control = jnp.stack([jnp.zeros_like(seq_index), seq_index, wt_index])
    sums = pair_sums(d_mine, swap(d_other, "seq", 1, seq_count))
    sums, normed_two = lax.optimization_barrier((sums, normed_two))
    arrived = send_chips(sums, seq_count)
    mlp_share = sum_wt(
        mlp_grads(control, normed_two, dy_low, d_gate, d_up, hidden, wt_count), wt_count
    )
    pair, d_resid, gain_part_two = post(
        sums[0], arrived, resid_own, cotangent[0], vectors[1:2], wide_w, seq_count
    )
    pair, mlp_share = lax.optimization_barrier((pair, mlp_share))
    pair = lax.all_to_all(pair, "seq", split_axis=0, concat_axis=0)
    pair, mlp_share = lax.optimization_barrier((pair, mlp_share))
    mlp_share = lax.all_gather(mlp_share, "seq", axis=0)

    d_qkv, bias_part, attn_part = back(
        doc_bounds,
        control,
        query,
        key,
        value,
        log_total,
        pair,
        normed_one,
        attn_all,
        cosine,
        sine,
        wt_count,
    )

    def new_block(share, old, pick):
        grad = lax.dynamic_index_in_dim(share, pick[0], 1, keepdims=False).astype(f32)
        return (old + grad).astype(bf16)

    def control_of(owners):
        active = functools.reduce(jnp.logical_or, [seq_index == owner for owner in owners])
        return jnp.stack([active.astype(jnp.int32), seq_index, wt_index])

    attn_share = sum_wt(attn_part, wt_count)
    attn_share, hidden = lax.optimization_barrier((attn_share, hidden))
    attn_share = lax.all_gather(attn_share, "seq", axis=0)
    mlp_block = new_block(mlp_share, mlp_old, mlp_pick)
    mlp_gathered = gather_owned(mlp_block, MLP_OWNERS, wt_count)

    mine, other = late_sums(place, hidden, wide_w, d_qkv, qkv_w, seq_count)
    sums = pair_sums(mine, swap(other, "seq", 1, seq_count))

    mlp_grad, mlp_mom = finish(mlp_share, mlp_momentum)
    mlp_blocks = orthogonalize(control_of(MLP_OWNERS), mlp_gathered, [mlp_grad, sums[0]])

    attn_block = new_block(attn_share, attn_old, attn_pick)
    attn_block, mlp_blocks, sums = lax.optimization_barrier((attn_block, mlp_blocks, sums))
    attn_gathered = gather_owned(attn_block, ATTN_OWNERS, wt_count)
    arrived = send_chips(sums, seq_count)
    attn_grad, attn_mom = finish(attn_share, attn_momentum)
    attn_blocks = orthogonalize(control_of(ATTN_OWNERS), attn_gathered, [attn_grad])
    mlp_blocks, attn_blocks = lax.optimization_barrier((mlp_blocks, attn_blocks))

    squares = sum_all(squares, "wt", wt_count)[:, 0]
    attn_rate = matrix_rate * math.sqrt(width) * jnp.sqrt(squares[:4] / (width * width))
    mlp_rate = matrix_rate * math.sqrt(ff) * jnp.sqrt(squares[4:7] / (width * ff))
    mlp_new = update(
        control, mlp_rate, mlp_own, spread_owned(mlp_blocks, MLP_OWNERS, seq_count), MLP_OWNERS
    )
    attn_new = update(
        control,
        attn_rate,
        attn_own,
        spread_owned(attn_blocks, ATTN_OWNERS, seq_count),
        ATTN_OWNERS,
    )

    total = sums[0]
    for value in arrived:
        total = total + value.astype(f32)
    layer_out = (resid_own + total[0]).astype(bf16)
    x_own = tokens[0].astype(f32)
    inverse_own = lax.rsqrt(jnp.mean(x_own * x_own, axis=-1, keepdims=True) + norm_eps)
    d_input_norm, gain_part_one = norm_backward(total[1], x_own, inverse_own, vectors[0])
    tokens_grad = d_resid + d_input_norm

    bias_wide = lax.dynamic_update_slice(
        jnp.zeros((3, width), f32), bias_part.reshape(3, head_cols), (0, seq_index * head_cols)
    )
    small = jnp.concatenate(
        [gain_part_one[None], gain_part_two, bias_wide, jnp.zeros((3, width), f32)], 0
    )
    small = sum_all(sum_all(small, "seq", seq_count), "wt", wt_count)
    small = lax.dynamic_slice_in_dim(small, wt_index * shard, shard, 1)
    gain_grad = small[:2]
    bias_grad = small[2:5]
    gain_new, gain_second_new = adam_update(gains, gain_grad, gain_first, gain_second)
    bias_new, bias_second_new = adam_update(qkv_bias, bias_grad, bias_first, bias_second)
    return (
        layer_out[None],
        tokens_grad[None],
        attn_grad,
        mlp_grad,
        attn_mom,
        mlp_mom,
        attn_new,
        mlp_new,
        gain_grad,
        gain_second_new,
        gain_new,
        bias_grad,
        bias_second_new,
        bias_new,
    )


def solution(mesh):
    return jax.shard_map(
        per_device,
        mesh=mesh,
        in_specs=(
            P("wt", "seq", None),
            P("wt", "seq", None),
            P("wt", None),
            P(None, "wt", None),
            P(None, "wt", None),
            P(None, "wt", None),
            P(None, "wt", None),
            P(None, "wt"),
            P(None, "wt"),
            P(None, "wt"),
            P(None, "wt"),
            P(None, "wt"),
            P(None, "wt"),
        ),
        out_specs=(
            P("wt", "seq", None),
            P("wt", "seq", None),
            P(None, "wt", None),
            P(None, "wt", None),
            P(None, "wt", None),
            P(None, "wt", None),
            P(None, "wt", "seq"),
            P(None, "wt", "seq"),
            P(None, "wt"),
            P(None, "wt"),
            P(None, "wt"),
            P(None, "wt"),
            P(None, "wt"),
            P(None, "wt"),
        ),
        check_vma=False,
    )
```

```python
import functools
import math

import jax
import jax.numpy as jnp
from jax import lax
from jax.experimental import pallas as pl
from jax.experimental.pallas import tpu as pltpu
from jax.sharding import PartitionSpec as P

HEAD_DIM = 64
NS_STEPS = 5
STEP = 10

norm_eps = 1e-06
rope_base = 1000000.0
coef_a = 3.4445
coef_b = -4.775
coef_c = 2.0315
momentum_decay = 0.95
matrix_rate = 0.5
decay_rate = 0.01
first_decay = 0.9
second_decay = 0.95
vector_rate = 0.25
adam_eps = 1e-08
ortho_eps = 1e-07
masked_score = -1e30
tile = 256
vmem_limit = 62 * 2**20

MLP_OWNERS = (0, 2, 4)
ATTN_OWNERS = (1, 3, 5, 6)

f32 = jnp.float32
bf16 = jnp.bfloat16


def dot32(a, b, ca, cb):
    return lax.dot_general(a, b, (((ca,), (cb,)), ((), ())), preferred_element_type=f32)


def doc_layout(bounds, length):
    places = jnp.arange(length, dtype=jnp.int32)
    first_bound = bounds[0]
    second_bound = bounds[1]
    doc_index = (places >= first_bound).astype(jnp.int32) + (places >= second_bound).astype(
        jnp.int32
    )
    doc_start = jnp.where(
        places < first_bound, 0, jnp.where(places < second_bound, first_bound, second_bound)
    )
    return (doc_index, (places - doc_start).astype(f32))


def rope_tables(position, cols):
    half_dim = HEAD_DIM // 2
    lane = jnp.arange(cols, dtype=jnp.int32) % HEAD_DIM
    frequency = rope_base ** (-2.0 * jnp.arange(half_dim, dtype=f32) / HEAD_DIM)
    angles = position[:, None] * frequency[None, :]
    repeat = cols // half_dim
    cosine = jnp.concatenate([jnp.cos(angles)] * repeat, 1)
    sine = jnp.concatenate([jnp.sin(angles)] * repeat, 1)
    return cosine, jnp.where(lane < half_dim, -1.0, 1.0)[None, :] * sine


def swap_halves(values):
    half_dim = HEAD_DIM // 2
    parts = []
    for first in range(0, values.shape[1], HEAD_DIM):
        parts.append(values[:, first + half_dim : first + HEAD_DIM])
        parts.append(values[:, first : first + half_dim])
    return jnp.concatenate(parts, axis=1)


def visible(bounds_ref, first, rows, length):
    query = first + lax.broadcasted_iota(jnp.int32, (rows, length), 0)
    key = lax.broadcasted_iota(jnp.int32, (rows, length), 1)
    one, two = bounds_ref[0, 0], bounds_ref[0, 1]
    start = jnp.where(query < one, 0, jnp.where(query < two, one, two))
    return (key <= query) & (key >= start)


def slot_of(chips, value):
    slot, bits = 0, chips
    while bits > 1:
        slot = slot * 2 + (value & 1)
        value = value >> 1
        bits //= 2
    return slot


def front_kernel(
    bounds_ref,
    place_ref,
    same_ref,
    other_ref,
    weight_ref,
    gain_ref,
    bias_ref,
    cosine_ref,
    sine_ref,
    x_ref,
    normed_ref,
    query_ref,
    key_ref,
    value_ref,
    attended_ref,
    log_ref,
):
    length = x_ref.shape[0]
    cols = query_ref.shape[1]
    chips, rows, _ = same_ref.shape
    for chip in range(chips):
        at = pl.ds(chip * 2 * rows, 2 * rows)
        slot = slot_of(chips, place_ref[0] ^ chip)
        low = pl.ds(chip * 2 * rows + place_ref[1] * rows, rows)
        high = pl.ds(chip * 2 * rows + (1 - place_ref[1]) * rows, rows)
        x_ref[low, :] = same_ref[slot]
        x_ref[high, :] = other_ref[slot]
        x = x_ref[at, :].astype(f32)
        inverse = lax.rsqrt(jnp.mean(x * x, axis=-1, keepdims=True) + norm_eps)
        normed = (x * inverse * gain_ref[...]).astype(bf16)
        normed_ref[at, :] = normed
        projected = (dot32(normed, weight_ref[...], 1, 0) + bias_ref[...]).astype(bf16).astype(f32)
        cosine, sine = cosine_ref[at, :], sine_ref[at, :]
        query = projected[:, :cols]
        key = projected[:, cols : 2 * cols]
        query_ref[at, :] = (query * cosine + swap_halves(query) * sine).astype(bf16)
        key_ref[at, :] = (key * cosine + swap_halves(key) * sine).astype(bf16)
        value_ref[at, :] = projected[:, 2 * cols :].astype(bf16)
    for first in range(0, length, tile):
        at, keys = pl.ds(first, tile), pl.ds(0, first + tile)
        allowed = visible(bounds_ref, first, tile, first + tile)
        attended = []
        for head in range(cols // HEAD_DIM):
            lanes = pl.ds(head * HEAD_DIM, HEAD_DIM)
            scores = dot32(query_ref[at, lanes], key_ref[keys, lanes], 1, 1)
            scores = jnp.where(allowed, scores * HEAD_DIM ** (-0.5), masked_score)
            peak = jnp.max(scores, axis=-1, keepdims=True)
            exponent = jnp.exp(scores - peak)
            total = jnp.sum(exponent, axis=-1, keepdims=True)
            weights = (exponent * (1.0 / total)).astype(bf16)
            attended.append(dot32(weights, value_ref[keys, lanes], 1, 0))
            log_ref[at, pl.ds(head, 1)] = peak + jnp.log(total)
        attended_ref[at, :] = jnp.concatenate(attended, axis=1).astype(bf16)


def vmem_specs(count):
    return [pl.BlockSpec(memory_space=pltpu.VMEM)] * count


def whole_spec(shape):
    return pl.BlockSpec(shape, lambda i: (0,) * len(shape))


def whole_specs(arrays):
    return [whole_spec(value.shape) for value in arrays]


def any_specs(count):
    return [pl.BlockSpec(memory_space=pl.ANY)] * count


def smem_spec():
    return pl.BlockSpec(memory_space=pltpu.SMEM)


def front(bounds, place, same, other, weight, gain, bias, cosine, sine):
    chips, rows, width = same.shape
    length, cols = cosine.shape
    part = jax.ShapeDtypeStruct((length, cols), bf16)
    shapes = [
        jax.ShapeDtypeStruct((length, width), bf16),
        jax.ShapeDtypeStruct((length, width), bf16),
        part,
        part,
        part,
        part,
        jax.ShapeDtypeStruct((length, cols // HEAD_DIM), f32),
    ]
    args = (same, other, weight, gain, bias, cosine, sine)
    return pl.pallas_call(
        front_kernel,
        grid=(1,),
        in_specs=[smem_spec()] * 2 + whole_specs(args),
        out_specs=whole_specs(shapes),
        out_shape=shapes,
        compiler_params=pltpu.CompilerParams(vmem_limit_bytes=vmem_limit),
        cost_estimate=pl.CostEstimate(
            flops=8 * 10**9, bytes_accessed=8 * 10**6, transcendentals=2 * 10**6
        ),
        name="front",
    )(bounds, place, *args)


def store_split(place_ref, mine_ref, other_ref, index, value):
    rows = value.shape[0] // 2
    core = place_ref[1]
    top, low = value[:rows], value[rows:]
    mine_ref[0, index] = jnp.where(core == 0, top, low)
    other_ref[0, index] = jnp.where(core == 0, low, top).astype(bf16)


def split_out(chips, sums, rows, width):
    spec = pl.BlockSpec(
        (1, sums, rows, width), lambda i, place: (slot_of(chips, i ^ place[0]), 0, 0, 0)
    )
    shape = (chips, sums, rows, width)
    return [spec, spec], [jax.ShapeDtypeStruct(shape, f32), jax.ShapeDtypeStruct(shape, bf16)]


def middle_kernel(
    place_ref,
    same_ref,
    other_ref,
    x_ref,
    dy_ref,
    weight_ref,
    gain_ref,
    normed_ref,
    d_gate_ref,
    d_up_ref,
    hidden_ref,
    d_mine_ref,
    d_other_ref,
    resid_ref,
    gain_part_ref,
):
    width = x_ref.shape[1]
    cols = d_gate_ref.shape[1]
    rows = resid_ref.shape[0]
    gate_w = weight_ref.at[:, pl.ds(width, cols)]
    up_w = weight_ref.at[:, pl.ds(width + cols, cols)]
    down_w = weight_ref.at[:, pl.ds(width + 2 * cols, cols)]
    attended = []
    for chip in range(same_ref.shape[0]):
        slot = slot_of(same_ref.shape[0], place_ref[0] ^ chip)
        same, other = same_ref[slot], other_ref[slot]
        attended.append(jnp.where(place_ref[1] == 0, same, other))
        attended.append(jnp.where(place_ref[1] == 0, other, same))
    attended = jnp.concatenate(attended, axis=1)
    resid = x_ref[...].astype(f32) + dot32(attended, weight_ref[:, pl.ds(0, width)], 1, 0)

    @pl.when(pl.program_id(0) == place_ref[0])
    def _():
        resid_ref[...] = jnp.where(place_ref[1] == 0, resid[:rows], resid[rows:])

    inverse = lax.rsqrt(jnp.mean(resid * resid, axis=-1, keepdims=True) + norm_eps)
    normed = (resid * inverse * gain_ref[...]).astype(bf16)
    normed_ref[...] = normed
    gate = dot32(normed, gate_w[...], 1, 0)
    up = dot32(normed, up_w[...], 1, 0)
    d_hidden = dot32(dy_ref[...], down_w[...], 1, 0)
    sigmoid = jax.nn.sigmoid(gate)
    silu = gate * sigmoid
    hidden = (silu * up).astype(bf16)
    hidden_ref[...] = hidden
    d_gate = (d_hidden * up * (sigmoid * (1.0 + gate * (1.0 - sigmoid)))).astype(bf16)
    d_up = (d_hidden * silu).astype(bf16)
    d_gate_ref[...] = d_gate
    d_up_ref[...] = d_up
    d_normed = dot32(d_gate, gate_w[...], 1, 1) + dot32(d_up, up_w[...], 1, 1)
    store_split(place_ref, d_mine_ref, d_other_ref, 0, d_normed)

    @pl.when(pl.program_id(0) == 0)
    def _():
        gain_part_ref[...] = jnp.zeros_like(gain_part_ref)

    gain_part_ref[...] += jnp.sum(d_normed * resid * inverse, axis=0, keepdims=True)


def middle(place, same, other, x, dy, weight, gain):
    chips, length, head_cols = same.shape
    count = 2 * chips
    width = x.shape[1]
    cols = (weight.shape[1] - width) // 3
    half = length // count
    rows = 2 * half

    def block(size):
        return pl.BlockSpec((rows, size), lambda i, place: (i, 0))

    def whole(shape):
        return pl.BlockSpec(shape, lambda i, place: (0,) * len(shape))

    split_specs, split_shapes = split_out(chips, 1, half, width)
    wide = jax.ShapeDtypeStruct((length, cols), bf16)
    return pl.pallas_call(
        middle_kernel,
        grid_spec=pltpu.PrefetchScalarGridSpec(
            num_scalar_prefetch=1,
            grid=(chips,),
            in_specs=[
                pl.BlockSpec((chips, rows, head_cols), lambda i, place: (0, i, 0)),
                pl.BlockSpec((chips, rows, head_cols), lambda i, place: (0, i, 0)),
                block(width),
                block(width),
                whole(weight.shape),
                whole(gain.shape),
            ],
            out_specs=[
                block(width),
                block(cols),
                block(cols),
                block(cols),
                *split_specs,
                whole((half, width)),
                whole((1, width)),
            ],
        ),
        out_shape=[
            jax.ShapeDtypeStruct((length, width), bf16),
            wide,
            wide,
            wide,
            *split_shapes,
            jax.ShapeDtypeStruct((half, width), f32),
            jax.ShapeDtypeStruct((1, width), f32),
        ],
        compiler_params=pltpu.CompilerParams(vmem_limit_bytes=vmem_limit),
        cost_estimate=pl.CostEstimate(
            flops=10 * 10**9, bytes_accessed=20 * 10**6, transcendentals=10**6
        ),
        name="middle",
    )(place, same, other, x, dy, weight, gain)


def pair_kernel(kept, mine_ref, got_ref, keep_ref, *sends):
    for slot in range(kept):
        keep_ref[slot] = mine_ref[slot] + got_ref[slot].astype(f32)
    for slot in range(kept, mine_ref.shape[0]):
        value = (mine_ref[slot] + got_ref[slot].astype(f32)).astype(bf16)
        if len(sends) == 1:
            sends[0][slot - kept] = value
        else:
            sends[slot - kept][0] = value


def pair_sums(mine, got, kept, together):
    slots, sums, rows, width = mine.shape
    step = 32

    def spec(count):
        return pl.BlockSpec((count, sums, step, width), lambda i: (0, 0, i, 0))

    counts = [slots - kept] if together else [1] * (slots - kept)
    return pl.pallas_call(
        functools.partial(pair_kernel, kept),
        grid=(rows // step,),
        in_specs=[spec(slots)] * 2,
        out_specs=[spec(kept)] + [spec(count) for count in counts],
        out_shape=[jax.ShapeDtypeStruct((kept, sums, rows, width), f32)]
        + [jax.ShapeDtypeStruct((count, sums, rows, width), bf16) for count in counts],
        compiler_params=pltpu.CompilerParams(vmem_limit_bytes=vmem_limit),
        name="pair_sums",
    )(mine, got)


def post_kernel(extra, own_ref, resid_ref, dy_ref, gain_ref, weight_ref, *refs):
    arrived, (pair_ref, d_resid_ref) = refs[: -2 - extra], refs[-2:]
    d_normed = own_ref[0, 0]
    for ref in arrived:
        d_normed = d_normed + ref[0, 0].astype(f32)
    resid = resid_ref[...]
    inverse = lax.rsqrt(jnp.mean(resid * resid, axis=-1, keepdims=True) + norm_eps)
    scaled = d_normed * gain_ref[...]
    d_resid = (
        dy_ref[...].astype(f32)
        + inverse * scaled
        - resid * (inverse * inverse * inverse) * jnp.mean(scaled * resid, axis=-1, keepdims=True)
    )
    d_resid_ref[...] = d_resid
    low = d_resid.astype(bf16)
    d_attn = dot32(low, weight_ref[...], 1, 1).astype(bf16)
    cols = pair_ref.shape[3]
    for part in range(pair_ref.shape[0]):
        pair_ref[part, 0] = d_attn[:, part * cols : (part + 1) * cols]
        pair_ref[part, 1] = low[:, part * cols : (part + 1) * cols]


def post(own, arrived, resid, dy, gain, weight, count, after):
    rows, width = resid.shape
    cols = width // count

    def whole(shape):
        return pl.BlockSpec(shape, lambda i: (0,) * len(shape))

    return pl.pallas_call(
        functools.partial(post_kernel, len(after)),
        grid=(1,),
        in_specs=[whole(own.shape), whole(resid.shape), whole(dy.shape), whole(gain.shape)]
        + [whole((width, width))]
        + [whole(value.shape) for value in arrived]
        + any_specs(len(after)),
        out_specs=[whole((count, 2, rows, cols)), whole((rows, width))],
        out_shape=[
            jax.ShapeDtypeStruct((count, 2, rows, cols), bf16),
            jax.ShapeDtypeStruct((rows, width), f32),
        ],
        compiler_params=pltpu.CompilerParams(vmem_limit_bytes=vmem_limit),
        name="post",
    )(own, resid, dy, gain, weight, *arrived, *after)


def mlp_grads_kernel(
    parts, extra, control_ref, normed_ref, dy_ref, d_gate_ref, d_up_ref, hidden_ref, *refs
):
    outs = refs[extra:]
    shard = outs[0].shape[0] // 3
    for part in range(parts):
        at = pl.ds(pl.multiple_of((control_ref[2] ^ part) * shard, 128), shard)
        normed = normed_ref[:, at]
        pairs = [(normed, d_gate_ref), (normed, d_up_ref), (dy_ref[:, at], hidden_ref)]
        for index, (left, right_ref) in enumerate(pairs):
            outs[part][pl.ds(index * shard, shard), :] = dot32(left, right_ref[...], 0, 0).astype(
                bf16
            )


def mlp_grads(control, normed, dy, d_gate, d_up, hidden, parts, after):
    length, width = normed.shape
    cols = hidden.shape[1]
    args = (normed, dy, d_gate, d_up, hidden)
    shapes = [jax.ShapeDtypeStruct((3 * width // parts, cols), bf16)] * parts
    return pl.pallas_call(
        functools.partial(mlp_grads_kernel, parts, len(after)),
        grid=(1,),
        in_specs=[smem_spec()] + whole_specs(args) + any_specs(len(after)),
        out_specs=whole_specs(shapes),
        out_shape=shapes,
        compiler_params=pltpu.CompilerParams(vmem_limit_bytes=vmem_limit),
        cost_estimate=pl.CostEstimate(
            flops=3 * 10**9, bytes_accessed=9 * 10**6, transcendentals=0
        ),
        name="mlp_grads",
    )(control, *args, *after)


def back_kernel(
    parts,
    bounds_ref,
    control_ref,
    query_ref,
    key_ref,
    value_ref,
    log_ref,
    arrived_ref,
    normed_ref,
    same_ref,
    other_ref,
    cosine_ref,
    sine_ref,
    weight_ref,
    gain_ref,
    gain_two_ref,
    squares_ref,
    d_qkv_ref,
    *refs,
):
    grads_refs, (d_key_ref, d_value_ref, d_attn_ref, d_resid_ref) = refs[:parts], refs[parts:]
    length, cols = query_ref.shape
    count, _, rows, _ = arrived_ref.shape
    scale = HEAD_DIM ** (-0.5)
    for part in range(count):
        d_attn_ref[pl.ds(part * rows, rows), :] = arrived_ref[part, 0]
        d_resid_ref[pl.ds(part * rows, rows), :] = arrived_ref[part, 1]
    d_key_ref[...] = jnp.zeros_like(d_key_ref)
    d_value_ref[...] = jnp.zeros_like(d_value_ref)

    def undo(values, at):
        return values * cosine_ref[at, :] - swap_halves(values) * sine_ref[at, :]

    for first in range(0, length, tile):
        at, keys = pl.ds(first, tile), pl.ds(0, first + tile)
        allowed = visible(bounds_ref, first, tile, first + tile)
        d_query, d_key, d_value = [], [], []
        for head in range(cols // HEAD_DIM):
            lanes = pl.ds(head * HEAD_DIM, HEAD_DIM)
            query, d_out = query_ref[at, lanes], d_attn_ref[at, lanes]
            key, value = key_ref[keys, lanes], value_ref[keys, lanes]
            scores = jnp.where(allowed, dot32(query, key, 1, 1) * scale, masked_score)
            weights = jnp.exp(scores - log_ref[at, pl.ds(head, 1)])
            d_value.append(dot32(weights.astype(bf16), d_out, 0, 0))
            d_weights = dot32(d_out, value, 1, 1)
            inner = jnp.sum(weights * d_weights, axis=-1, keepdims=True)
            d_scores = (weights * (d_weights - inner)).astype(bf16)
            d_query.append(dot32(d_scores, key, 1, 0) * scale)
            d_key.append(dot32(d_scores, query, 0, 0) * scale)
        d_key_ref[keys, :] += jnp.concatenate(d_key, axis=1)
        d_value_ref[keys, :] += jnp.concatenate(d_value, axis=1)
        d_qkv_ref[at, pl.ds(0, cols)] = undo(jnp.concatenate(d_query, axis=1), at).astype(bf16)
    for first in range(0, length, tile):
        at = pl.ds(first, tile)
        d_qkv_ref[at, pl.ds(cols, cols)] = undo(d_key_ref[at, :], at).astype(bf16)
        d_qkv_ref[at, pl.ds(2 * cols, cols)] = d_value_ref[at, :].astype(bf16)
    shard = gain_ref.shape[1] // parts
    pad = grads_refs[0].shape[1]
    pieces = shard // cols
    bias = jnp.sum(d_qkv_ref[...].astype(f32), axis=0, keepdims=True)
    lane = lax.broadcasted_iota(jnp.int32, squares_ref.shape, 1)
    row = lax.broadcasted_iota(jnp.int32, squares_ref.shape, 0)
    squares = jnp.sum(jnp.where(lane == row, squares_ref[...], 0.0), axis=0, keepdims=True)
    squares_high = squares.astype(bf16).astype(f32)
    rest = jnp.zeros((1, shard - squares.shape[1]), f32)

    def wide(value):
        return value if shard == 128 else jnp.concatenate([value, rest], axis=1)

    for part in range(parts):
        block = control_ref[2] ^ part
        grads_ref = grads_refs[part]
        at = pl.ds(pl.multiple_of(block * shard, 128), shard)
        grads = dot32(normed_ref[:, at], d_qkv_ref[...], 0, 0)
        gain_one = lax.dot_general(
            jnp.ones((8, 3 * cols), f32),
            grads * weight_ref[at, :].astype(f32),
            (((1,), (1,)), ((), ())),
            precision=lax.Precision.HIGHEST,
            preferred_element_type=f32,
        )[0:1]
        grads = grads.astype(bf16)
        for index in range(3):
            grads_ref[pl.ds(index * shard, shard), pl.ds(0, cols)] = grads[
                :, index * cols : (index + 1) * cols
            ]
        for piece in range(pieces):
            place = block * pieces + piece
            slot = slot_of(same_ref.shape[0], (place >> 1) ^ (control_ref[1] >> 1))
            near = ((place ^ control_ref[1]) & 1) == 0
            attended = jnp.where(near, same_ref[slot], other_ref[slot])
            grads_ref[pl.ds(3 * shard + piece * cols, cols), pl.ds(0, cols)] = dot32(
                attended, d_resid_ref[...], 0, 0
            ).astype(bf16)
        if pad > cols:
            grads_ref[pl.ds(0, 4 * shard), pl.ds(cols, pad - cols)] = jnp.zeros(
                (4 * shard, pad - cols), bf16
            )
        small = [gain_one / gain_ref[:, at], gain_two_ref[:, at]]
        for index in range(3):
            own = bias[:, index * cols : (index + 1) * cols]
            small.append(
                jnp.concatenate(
                    [
                        jnp.where(block * pieces + piece == control_ref[1], own, 0.0)
                        for piece in range(pieces)
                    ],
                    axis=1,
                )
            )
        small += [wide(squares_high), wide(squares - squares_high), jnp.zeros((1, shard), f32)]
        small = jnp.concatenate(small, axis=0)
        small = [small[:, first : first + 128] for first in range(0, shard, 128)]
        small += [jnp.zeros((8, 128), f32)] * (2 - len(small))
        grads_ref[pl.ds(4 * shard, 16), :] = jnp.concatenate(small, axis=0).astype(bf16)


def back(bounds, control, args, parts):
    query, normed = args[0], args[5]
    length, cols = query.shape
    width = normed.shape[1]
    pad = -(-cols // 128) * 128
    shapes = [jax.ShapeDtypeStruct((length, 3 * cols), bf16)]
    shapes += [jax.ShapeDtypeStruct((4 * width // parts + 16, pad), bf16)] * parts
    results = pl.pallas_call(
        functools.partial(back_kernel, parts),
        grid=(1,),
        in_specs=[smem_spec()] * 2 + whole_specs(args),
        out_specs=whole_specs(shapes),
        out_shape=shapes,
        scratch_shapes=[
            pltpu.VMEM((length, cols), f32),
            pltpu.VMEM((length, cols), f32),
            pltpu.VMEM((length, cols), bf16),
            pltpu.VMEM((length, cols), bf16),
        ],
        compiler_params=pltpu.CompilerParams(vmem_limit_bytes=vmem_limit),
        cost_estimate=pl.CostEstimate(
            flops=10 * 10**9, bytes_accessed=8 * 10**6, transcendentals=2 * 10**6
        ),
        name="back",
    )(bounds, control, *args)
    return results[0], results[1:]


def late_kernel(place_ref, hidden_ref, down_ref, d_qkv_ref, weight_ref, mine_ref, other_ref):
    store_split(place_ref, mine_ref, other_ref, 0, dot32(hidden_ref[...], down_ref[...], 1, 1))
    store_split(place_ref, mine_ref, other_ref, 1, dot32(d_qkv_ref[...], weight_ref[...], 1, 1))


def late_sums(place, hidden, down, d_qkv, weight, count):
    length, cols = d_qkv.shape
    width = weight.shape[0]
    chips = count // 2
    half = length // count
    rows = 2 * half

    def block(size):
        return pl.BlockSpec((rows, size), lambda i, place: (i, 0))

    def whole(shape):
        return pl.BlockSpec(shape, lambda i, place: (0, 0))

    split_specs, split_shapes = split_out(chips, 2, half, width)
    return pl.pallas_call(
        late_kernel,
        grid_spec=pltpu.PrefetchScalarGridSpec(
            num_scalar_prefetch=1,
            grid=(chips,),
            in_specs=[
                block(hidden.shape[1]),
                whole(down.shape),
                block(cols),
                whole(weight.shape),
            ],
            out_specs=split_specs,
        ),
        out_shape=split_shapes,
        compiler_params=pltpu.CompilerParams(vmem_limit_bytes=vmem_limit),
        cost_estimate=pl.CostEstimate(
            flops=2 * 10**9, bytes_accessed=16 * 10**6, transcendentals=0
        ),
        name="late_sums",
    )(place, hidden, down, d_qkv, weight)


def picked_kernel(pick_ref, momentum_ref, out_ref):
    count, rows, pad = out_ref.shape
    cols = momentum_ref.shape[2] // count
    for turn in range(count):
        value = momentum_ref[0, :, pl.ds(turn * cols, cols)] * momentum_decay
        out_ref[turn, :, pl.ds(0, cols)] = value
        if pad > cols:
            out_ref[turn, :, pl.ds(cols, pad - cols)] = jnp.zeros((rows, pad - cols), f32)


def picked(momentum, pick, count):
    rows, width = momentum.shape[1:]
    pad = -(-(width // count) // 128) * 128
    step = min(64, rows)
    return pl.pallas_call(
        picked_kernel,
        grid_spec=pltpu.PrefetchScalarGridSpec(
            num_scalar_prefetch=1,
            grid=(rows // step,),
            in_specs=[pl.BlockSpec((1, step, width), lambda i, pick: (pick[0], i, 0))],
            out_specs=pl.BlockSpec((count, step, pad), lambda i, pick: (0, i, 0)),
        ),
        out_shape=jax.ShapeDtypeStruct((count, rows, pad), f32),
        compiler_params=pltpu.CompilerParams(vmem_limit_bytes=vmem_limit),
        cost_estimate=pl.CostEstimate(
            flops=rows * width, bytes_accessed=8 * rows * width, transcendentals=0
        ),
        name="picked",
    )(pick, momentum)


def squares_kernel(order_ref, attn_ref, mlp_ref, out_ref):
    @pl.when(pl.program_id(0) == 0)
    def _():
        out_ref[...] = jnp.zeros_like(out_ref)

    at = 0
    for ref in (attn_ref, mlp_ref):
        for index in range(ref.shape[0]):
            value = ref[index].astype(bf16).astype(f32)
            total = jnp.sum(jnp.sum(value * value, axis=0, keepdims=True), axis=1, keepdims=True)
            out_ref[pl.ds(at, 1), :] += jnp.broadcast_to(total, (1, out_ref.shape[1]))
            at += 1


def block_kernel(extra, pick_ref, share_ref, old_ref, *refs):
    refs[extra][...] = (old_ref[...] + share_ref[...].astype(f32)).astype(bf16)


def new_block(share, old, pick, after):
    count, shard, pad = old.shape
    step = 2
    return pl.pallas_call(
        functools.partial(block_kernel, len(after)),
        grid_spec=pltpu.PrefetchScalarGridSpec(
            num_scalar_prefetch=1,
            grid=(count // step,),
            in_specs=[
                pl.BlockSpec((step, shard, pad), lambda i, pick: (i, pick[0], 0)),
                pl.BlockSpec((step, shard, pad), lambda i, pick: (i, 0, 0)),
            ]
            + any_specs(len(after)),
            out_specs=pl.BlockSpec((step, shard, pad), lambda i, pick: (i, 0, 0)),
        ),
        out_shape=jax.ShapeDtypeStruct(old.shape, bf16),
        compiler_params=pltpu.CompilerParams(vmem_limit_bytes=vmem_limit),
        cost_estimate=pl.CostEstimate(
            flops=old.size, bytes_accessed=8 * old.size, transcendentals=0
        ),
        name="new_block",
    )(pick, share, old, *after)


def sums_of_squares(order, attn, mlp):
    rows = attn.shape[1]
    step = min(64, rows)
    return pl.pallas_call(
        squares_kernel,
        grid=(rows // step,),
        in_specs=[
            smem_spec(),
            pl.BlockSpec((attn.shape[0], step, attn.shape[2]), lambda i: (0, i, 0)),
            pl.BlockSpec((mlp.shape[0], step, mlp.shape[2]), lambda i: (0, i, 0)),
        ],
        out_specs=pl.BlockSpec((8, 128), lambda i: (0, 0)),
        out_shape=jax.ShapeDtypeStruct((8, 128), f32),
        compiler_params=pltpu.CompilerParams(vmem_limit_bytes=vmem_limit),
        cost_estimate=pl.CostEstimate(
            flops=2 * (attn.size + mlp.size),
            bytes_accessed=4 * (attn.size + mlp.size),
            transcendentals=0,
        ),
        name="sums_of_squares",
    )(order, attn, mlp)


def pack_kernel(place_ref, master_ref, vectors_ref, *refs):
    out_ref = refs[-1]
    shard = master_ref.shape[1]
    cols = out_ref.shape[1] // 3
    for index in range(3):
        value = master_ref[index].astype(bf16)
        part = value[:, :cols]
        for at in range(1, value.shape[1] // cols):
            part = jnp.where(place_ref[1] == at, value[:, at * cols : (at + 1) * cols], part)
        out_ref[pl.ds(0, shard), pl.ds(index * cols, cols)] = part
    out_ref[pl.ds(shard, 16), :] = vectors_ref[...].astype(bf16)


def pack(seq_index, master, vectors, cols, after):
    shard = master.shape[1]
    lanes = max(cols, 128)
    place = jnp.stack([seq_index // (lanes // cols), seq_index % (lanes // cols)])
    shape = (shard + 16, 3 * cols)
    return pl.pallas_call(
        pack_kernel,
        grid_spec=pltpu.PrefetchScalarGridSpec(
            num_scalar_prefetch=1,
            grid=(1,),
            in_specs=[
                pl.BlockSpec((3, shard, lanes), lambda i, place: (0, 0, place[0])),
                pl.BlockSpec(vectors.shape, lambda i, place: (0, 0)),
            ]
            + any_specs(len(after)),
            out_specs=pl.BlockSpec(shape, lambda i, place: (0, 0)),
        ),
        out_shape=jax.ShapeDtypeStruct(shape, bf16),
        compiler_params=pltpu.CompilerParams(vmem_limit_bytes=vmem_limit),
        name="pack",
    )(place, master, vectors, *after)


def assemble_kernel(places, wt_ref, *refs):
    pieces, out_ref, arrived = refs[: len(places)], refs[-2], refs[-1]
    copies = []
    for at, (bits, first, rows) in enumerate(places):
        start = pl.multiple_of((wt_ref[0] ^ bits) * rows + first, 16)
        target = out_ref.at[pl.ds(start, pieces[at].shape[0]), :]
        copies.append(pltpu.make_async_copy(pieces[at], target, arrived.at[at]))
    for copy in copies:
        copy.start()
    for copy in copies:
        copy.wait()


def assemble(wt_index, pieces, places, rows):
    size = rows * pieces[0].shape[1]
    return pl.pallas_call(
        functools.partial(assemble_kernel, places),
        in_specs=[smem_spec()] + any_specs(len(pieces)),
        out_specs=vmem_specs(1)[0],
        out_shape=jax.ShapeDtypeStruct((rows, pieces[0].shape[1]), pieces[0].dtype),
        scratch_shapes=[pltpu.SemaphoreType.DMA((len(pieces),))],
        compiler_params=pltpu.CompilerParams(vmem_limit_bytes=vmem_limit),
        cost_estimate=pl.CostEstimate(flops=0, bytes_accessed=4 * size, transcendentals=0),
        name="assemble",
    )(wt_index.reshape(1), *pieces)


def norm_backward(d_normed, values, inverse, gain_row):
    scaled = d_normed * gain_row
    return inverse * scaled - values * inverse**3 * jnp.mean(
        scaled * values, axis=-1, keepdims=True
    )


def ortho_kernel(places, extra, control_ref, *refs):
    pieces, outs = refs[: len(places)], refs[len(places) + extra : -8]
    whole, gram, prod, gram_low, prod_low, poly_low, rows, arrived = refs[-8:]
    parts, count = arrived.shape
    shard, pad = outs[0].shape[1:]
    width = gram.shape[0]
    tiles = width // tile

    def upper(j):
        return pl.ds(j * tile, tile), pl.ds(j * tile, width - j * tile)

    def mirror(low):
        for j in range(1, tiles):
            for i in range(j):
                here, there = pl.ds(i * tile, tile), pl.ds(j * tile, tile)
                low[there, here] = low[here, there].T

    @pl.when(control_ref[0] == 1)
    def _():
        copies = [[] for _ in range(parts)]
        for (part, first), piece in zip(places, pieces):
            for turn in range(first, first + piece.shape[0]):
                copies[part].append(
                    pltpu.make_async_copy(
                        piece.at[turn - first],
                        whole.at[pl.ds(part * shard, shard), pl.ds(turn * pad, pad)],
                        arrived.at[part, turn],
                    )
                )
        for part in range(parts):
            for copy in copies[part]:
                copy.start()
        for part in range(parts):
            for copy in copies[part]:
                copy.wait()
        diagonal = lax.broadcasted_iota(jnp.int32, (tile, tile), 0) == lax.broadcasted_iota(
            jnp.int32, (tile, tile), 1
        )
        squares = jnp.zeros((1, 1), f32)
        for j in range(tiles):
            up, at = upper(j)
            gram[up, at] = dot32(whole[up, :], whole[at, :], 1, 1)
            entries = jnp.where(diagonal, gram[up, up], 0.0)
            squares = squares + jnp.sum(
                jnp.sum(entries, axis=1, keepdims=True), axis=0, keepdims=True
            )
        inverse = 1.0 / (jnp.sqrt(squares) + ortho_eps)
        for j in range(tiles):
            up, at = upper(j)
            scaled = gram[up, at] * (inverse * inverse)
            gram[up, at] = scaled
            gram_low[up, at] = scaled.astype(bf16)
        mirror(gram_low)

        def step(index, carry):
            poly = poly_low.at[index]
            for j in range(tiles):
                up, at = upper(j)
                poly[up, at] = (
                    coef_b * gram[up, at] + coef_c * dot32(gram_low[up, :], gram_low[:, at], 1, 0)
                ).astype(bf16)
            mirror(poly)
            for j in range(tiles):
                up, at = upper(j)
                value = coef_a * gram[up, at] + dot32(poly[up, :], gram_low[:, at], 1, 0)
                prod[up, at] = value
                prod_low[up, at] = value.astype(bf16)
            mirror(prod_low)
            for j in range(tiles):
                up, at = upper(j)
                value = coef_a * prod[up, at] + dot32(prod_low[up, :], poly[:, at], 1, 0)
                gram[up, at] = value
                gram_low[up, at] = value.astype(bf16)
            mirror(gram_low)
            return carry

        lax.fori_loop(0, NS_STEPS - 1, step, 0)
        unit = lax.broadcasted_iota(jnp.int32, (shard, width), 0) == lax.broadcasted_iota(
            jnp.int32, (shard, width), 1
        )
        rows[...] = (
            coef_a * unit.astype(f32)
            + coef_b * gram[pl.ds(0, shard), :]
            + coef_c * dot32(gram_low[pl.ds(0, shard), :], gram_low[...], 1, 0)
        )

        def apply(index, carry):
            value = rows[...]
            rows[...] = coef_a * value + dot32(
                value.astype(bf16), poly_low[NS_STEPS - 2 - index], 1, 0
            )
            return carry

        lax.fori_loop(0, NS_STEPS - 1, apply, 0)
        scaled = (rows[...] * inverse).astype(bf16)
        for turn in range(count // 2):
            chip = lax.rem((control_ref[1] >> 1) + turn, count // 2)
            for core in range(2):
                lanes = pl.ds(pl.multiple_of((2 * chip + core) * pad, 128), pad)
                outs[turn][core] = dot32(scaled, whole[:, lanes], 1, 0).astype(bf16)


def orthogonalize(control, pieces, places, parts, after):
    count, shard, pad = pieces[0].shape
    width = shard * parts
    return pl.pallas_call(
        functools.partial(ortho_kernel, places, len(after)),
        out_shape=[jax.ShapeDtypeStruct((2, shard, pad), bf16)] * (count // 2),
        in_specs=[smem_spec()] + any_specs(len(pieces) + len(after)),
        out_specs=vmem_specs(count // 2),
        scratch_shapes=[
            pltpu.VMEM((width, count * pad), bf16),
            pltpu.VMEM((width, width), f32),
            pltpu.VMEM((width, width), f32),
            pltpu.VMEM((width, width), bf16),
            pltpu.VMEM((width, width), bf16),
            pltpu.VMEM((NS_STEPS - 1, width, width), bf16),
            pltpu.VMEM((shard, width), f32),
            pltpu.SemaphoreType.DMA((parts, count)),
        ],
        compiler_params=pltpu.CompilerParams(vmem_limit_bytes=vmem_limit),
        cost_estimate=pl.CostEstimate(
            flops=30 * 10**9, bytes_accessed=4 * count * shard * pad, transcendentals=0
        ),
        name="orthogonalize",
    )(control, *pieces, *after)


def update_kernel(owners, control_ref, rate_ref, own_ref, *refs):
    arrived, other_ref, out_ref = refs[:-2], refs[-2], refs[-1]
    chips, cols = len(arrived), own_ref.shape[2]
    chip, core = control_ref[1] >> 1, control_ref[1] & 1
    for index, owner in enumerate(owners):
        turn = lax.rem(chip - owner // 2 + chips, chips)
        for at in range(chips):

            @pl.when(turn == at)
            def _():
                step = jnp.where(core == owner % 2, arrived[at][core], other_ref[at])
                out_ref[index] = (
                    own_ref[index] * (1.0 - matrix_rate * decay_rate)
                    - rate_ref[index] * step[:, :cols].astype(f32)
                )


def update(control, rate, own, arrived, other, owners):
    return pl.pallas_call(
        functools.partial(update_kernel, owners),
        grid=(1,),
        in_specs=[smem_spec()] * 2 + whole_specs((own, *arrived, other)),
        out_specs=whole_spec(own.shape),
        out_shape=jax.ShapeDtypeStruct(own.shape, f32),
        compiler_params=pltpu.CompilerParams(vmem_limit_bytes=vmem_limit),
        name="update",
    )(control, rate, own, *arrived, other)


def finish_kernel(matrices, *refs):
    shares, momentum_ref, (grad_ref, new_ref) = refs[:matrices], refs[matrices], refs[-2:]
    count = shares[0].shape[0]
    cols = grad_ref.shape[2] // count
    for index in range(matrices):
        for turn in range(count):
            at = pl.ds(turn * cols, cols)
            grad = shares[index][turn].astype(f32)[:, :cols]
            grad_ref[index, :, at] = grad
            new_ref[index, :, at] = momentum_decay * momentum_ref[index, :, at] + grad


def finish(share, momentum, after):
    count, _, pad = share.shape
    matrices, shard, width = momentum.shape
    step = min(64, shard)
    steps = shard // step
    whole = pl.BlockSpec((matrices, step, width), lambda i: (0, i, 0))
    parts = [
        pl.BlockSpec((count, step, pad), lambda i, index=index: (0, index * steps + i, 0))
        for index in range(matrices)
    ]
    size = matrices * shard * width
    return pl.pallas_call(
        functools.partial(finish_kernel, matrices),
        grid=(steps,),
        in_specs=parts + [whole] + any_specs(len(after)),
        out_specs=[whole, whole],
        out_shape=[jax.ShapeDtypeStruct(momentum.shape, f32)] * 2,
        compiler_params=pltpu.CompilerParams(vmem_limit_bytes=vmem_limit),
        cost_estimate=pl.CostEstimate(
            flops=2 * size, bytes_accessed=14 * size, transcendentals=0
        ),
        name="finish",
    )(*[share] * matrices, momentum, *after)


def adam_update(parameter, gradient, first_state, second_state):
    first_new = first_decay * first_state + (1.0 - first_decay) * gradient
    second_new = second_decay * second_state + (1.0 - second_decay) * gradient * gradient
    first_hat = first_new / (1.0 - first_decay**STEP)
    second_hat = second_new / (1.0 - second_decay**STEP)
    return (parameter - vector_rate * first_hat / (jnp.sqrt(second_hat) + adam_eps), second_new)


def swap(value, axis, bits, count):
    return lax.ppermute(value, axis, [(i, i ^ bits) for i in range(count)])


def sum_all(value, axis, count):
    bits = 1
    while bits < count:
        value = value + swap(value, axis, bits, count)
        bits *= 2
    return value


def near_wt(block, wt_count):
    return [swap(block, "wt", bits, wt_count) for bits in range(1, min(wt_count, 3))]


def far_wt(block, near, wt_count):
    rows = block.shape[0]
    if wt_count == 4:
        half = rows // 2
        pieces = [swap(near[0][:half], "wt", 2, wt_count), swap(near[1][half:], "wt", 1, wt_count)]
        return pieces, [(3, 0), (3, half)]
    places = [(bits, 0) for bits in range(1 + len(near), wt_count)]
    return [swap(block, "wt", bits, wt_count) for bits, _ in places], places


def sum_wt(parts, wt_count):
    total = parts[0].astype(f32)
    for bits in range(1, wt_count):
        total = total + swap(parts[bits], "wt", bits, wt_count).astype(f32)
    return total


def chip_order(seq_count):
    chips = seq_count // 2
    return [slot_of(chips, slot) for slot in range(chips)]


def gather_chips(block, seq_count):
    return [block] + [swap(block, "seq", 2 * bits, seq_count) for bits in chip_order(seq_count)[1:]]


def both_cores(blocks, seq_count):
    same = jnp.stack(blocks)
    return same, swap(same, "seq", 1, seq_count)


def send_chips(sends, seq_count):
    return [
        swap(value, "seq", 2 * bits, seq_count)
        for bits, value in zip(chip_order(seq_count)[1:], sends)
    ]


def send_owned(value, bits, owners, wt_count):
    pairs = [
        (owner * wt_count + w, owner * wt_count + (w ^ bits))
        for owner in owners
        for w in range(wt_count)
    ]
    return lax.ppermute(value, ("seq", "wt"), pairs)


def near_owned(block, owners, wt_count):
    return [send_owned(block, bits, owners, wt_count) for bits in range(1, min(wt_count, 3))]


def gather_owned(block, near, owners, wt_count):
    pieces = [block] + near
    places = [(part, 0) for part in range(len(pieces))]
    if wt_count == 4:
        half = block.shape[0] // 2
        pieces.append(send_owned(near[0][:half], 2, owners, wt_count))
        pieces.append(send_owned(near[1][half:], 1, owners, wt_count))
        return pieces, places + [(3, 0), (3, half)]
    for bits in range(len(pieces), wt_count):
        pieces.append(send_owned(block, bits, owners, wt_count))
        places.append((bits, 0))
    return pieces, places


def spread_chips(blocks, owners, seq_count):
    chips = seq_count // 2
    return [blocks[0]] + [
        lax.ppermute(
            blocks[turn],
            "seq",
            [(owner, (owner // 2 + turn) % chips * 2 + owner % 2) for owner in owners],
        )
        for turn in range(1, chips)
    ]


def spread_cores(arrived, core, seq_count):
    sent = [lax.dynamic_index_in_dim(value, 1 - core, 0, keepdims=False) for value in arrived]
    return swap(jnp.stack(sent), "seq", 1, seq_count)


def per_device(
    tokens,
    cotangent,
    doc_bounds,
    attn_master,
    mlp_master,
    attn_momentum,
    mlp_momentum,
    gains,
    gain_first,
    gain_second,
    qkv_bias,
    bias_first,
    bias_second,
):
    seq_count = lax.axis_size("seq")
    wt_count = lax.axis_size("wt")
    seq_index = lax.axis_index("seq")
    wt_index = lax.axis_index("wt")
    row_count = tokens.shape[1]
    width = tokens.shape[2]
    ff = mlp_master.shape[2]
    shard = attn_master.shape[1]
    length = row_count * seq_count
    head_cols = width // seq_count
    ff_cols = ff // seq_count

    place = jnp.stack([seq_index // 2, seq_index % 2])

    x_same, x_other = both_cores(gather_chips(tokens[0], seq_count), seq_count)
    own_dy, x_same = lax.optimization_barrier((cotangent[0], x_same))
    dy_low = lax.all_gather(own_dy, "seq", axis=0, tiled=True)

    vectors = jnp.pad(jnp.concatenate([gains, qkv_bias], 0), ((0, 11), (0, 3 * head_cols - shard)))
    _, position = doc_layout(doc_bounds[0], length)
    cosine, sine = rope_tables(position, head_cols)
    qkv_w = pack(seq_index, attn_master, vectors, head_cols, [cosine, sine])
    qkv_w = lax.all_gather(qkv_w, "wt", axis=0)
    place_own, qkv_w = lax.optimization_barrier((seq_index, qkv_w))
    attn_own = lax.dynamic_slice_in_dim(attn_master, place_own * head_cols, head_cols, 2)
    mlp_own = lax.dynamic_slice_in_dim(mlp_master, place_own * ff_cols, ff_cols, 2)
    ff_pad = -(-ff_cols // 128) * 128
    wide_own = jnp.pad(mlp_own, ((0, 0), (0, 0), (0, ff_pad - ff_cols)))
    wide_own = jnp.concatenate([attn_master[3], wide_own[0], wide_own[1], wide_own[2]], 1)
    wide_own = wide_own.astype(bf16)
    wide_near = near_wt(wide_own, wt_count)
    vectors = jnp.moveaxis(qkv_w[:, shard : shard + 5, :shard], 0, 1).reshape(5, width).astype(f32)
    qkv_w = qkv_w[:, :shard].reshape(width, 3 * head_cols)

    bias_own = lax.dynamic_slice_in_dim(vectors[2:5], seq_index * head_cols, head_cols, 1)
    x_low, normed_one, query, key, value, attended, log_total = front(
        doc_bounds,
        place,
        x_same,
        x_other,
        qkv_w,
        vectors[0:1],
        bias_own.reshape(1, 3 * head_cols),
        cosine,
        sine,
    )
    a_blocks = gather_chips(attended, seq_count)

    mlp_pick = jnp.minimum(seq_index // 2, 2).reshape(1)
    attn_pick = jnp.minimum(seq_index // 2, 3).reshape(1)
    mlp_pick, attn_pick, attended = lax.optimization_barrier((mlp_pick, attn_pick, attended))
    squares = sums_of_squares(mlp_pick, attn_master, mlp_master)
    wide_near, squares = lax.optimization_barrier((wide_near, squares))
    wide_far, far_places = far_wt(wide_own, wide_near, wt_count)
    mlp_old = picked(mlp_momentum, mlp_pick, seq_count)
    attn_old = picked(attn_momentum, attn_pick, seq_count)
    near_places = [(bits, 0) for bits in range(1 + len(wide_near))]
    wide_w = assemble(
        wt_index,
        [wide_own] + wide_near + wide_far,
        [(bits, first, shard) for bits, first in near_places + far_places],
        width,
    )
    a_blocks, wide_w, squares, mlp_old, attn_old = lax.optimization_barrier(
        (a_blocks, wide_w, squares, mlp_old, attn_old)
    )
    a_same, a_other = both_cores(a_blocks, seq_count)

    normed_two, d_gate, d_up, hidden, d_mine, d_other, resid_own, gain_part_two = middle(
        place, a_same, a_other, x_low, dy_low, wide_w, vectors[1:2]
    )

    control = jnp.stack([jnp.zeros_like(seq_index), seq_index, wt_index])
    own, *sends = pair_sums(d_mine, swap(d_other, "seq", 1, seq_count), 1, False)
    arrived = send_chips(sends, seq_count)
    mlp_part = mlp_grads(
        control, normed_two, dy_low, d_gate, d_up, hidden, wt_count, arrived[1:2]
    )
    mlp_share = sum_wt(mlp_part, wt_count).astype(bf16)
    pair, d_resid = post(
        own, arrived, resid_own, cotangent[0], vectors[1:2], wide_w, seq_count, mlp_part[:1]
    )
    pair = lax.all_to_all(pair, "seq", split_axis=0, concat_axis=0)
    pair, mlp_share = lax.optimization_barrier((pair, mlp_share))
    mlp_share = lax.all_gather(mlp_share, "seq", axis=0)

    args = (query, key, value, log_total, pair, normed_one, a_same, a_other, cosine, sine)
    args += (qkv_w, vectors[0:1], gain_part_two, squares)
    d_qkv, attn_part = back(doc_bounds, control, args, wt_count)

    def control_of(owners):
        active = functools.reduce(jnp.logical_or, [seq_index == owner for owner in owners])
        return jnp.stack([active.astype(jnp.int32), seq_index, wt_index])

    attn_share = sum_wt(attn_part, wt_count)
    squares = jnp.sum(attn_share[4 * shard + 5 : 4 * shard + 7, :7], axis=0)
    attn_share = attn_share.astype(bf16)
    attn_share = lax.all_gather(attn_share, "seq", axis=0)

    mine, other = late_sums(
        place, hidden, wide_w[:, width + 2 * ff_pad :], d_qkv, qkv_w, seq_count
    )
    late, *sends = pair_sums(mine, swap(other, "seq", 1, seq_count), 1, False)

    mlp_block = new_block(mlp_share, mlp_old, mlp_pick, [late])
    mlp_near = near_owned(mlp_block, MLP_OWNERS, wt_count)
    mlp_grad, mlp_mom = finish(mlp_share, mlp_momentum, [mlp_block])
    mlp_near, done = lax.optimization_barrier((mlp_near, mlp_grad[0, :8, :128]))
    mlp_pieces, mlp_places = gather_owned(mlp_block, mlp_near, MLP_OWNERS, wt_count)
    sends, attn_share = lax.optimization_barrier((sends, attn_share))
    late_arrived = send_chips(sends, seq_count)
    attn_block = new_block(attn_share, attn_old, attn_pick, [mlp_grad, done])
    attn_near = near_owned(attn_block, ATTN_OWNERS, wt_count)
    attn_pieces, attn_places = gather_owned(attn_block, attn_near, ATTN_OWNERS, wt_count)
    mlp_blocks = orthogonalize(
        control_of(MLP_OWNERS), mlp_pieces, mlp_places, wt_count, [done, *attn_pieces[1:]]
    )
    attn_blocks = orthogonalize(
        control_of(ATTN_OWNERS), attn_pieces, attn_places, wt_count, [mlp_blocks[0]]
    )
    mlp_blocks, attn_blocks = lax.optimization_barrier((mlp_blocks, attn_blocks))
    attn_grad, attn_mom = finish(attn_share, attn_momentum, attn_blocks[:1])

    attn_rate = matrix_rate * math.sqrt(width) * jnp.sqrt(squares[:4] / (width * width))
    mlp_rate = matrix_rate * math.sqrt(ff) * jnp.sqrt(squares[4:] / (width * ff))
    core = seq_index % 2
    mlp_arrived = spread_chips(mlp_blocks, MLP_OWNERS, seq_count)
    attn_arrived = spread_chips(attn_blocks, ATTN_OWNERS, seq_count)
    mlp_other = spread_cores(mlp_arrived, core, seq_count)
    attn_other = spread_cores(attn_arrived, core, seq_count)
    mlp_new = update(control, mlp_rate, mlp_own, mlp_arrived, mlp_other, MLP_OWNERS)
    attn_new = update(control, attn_rate, attn_own, attn_arrived, attn_other, ATTN_OWNERS)
    late_arrived, attn_grad = lax.optimization_barrier((late_arrived, attn_grad))

    total = late[0]
    for value in late_arrived:
        total = total + value[0].astype(f32)
    layer_out = (resid_own + total[0]).astype(bf16)
    x_own = tokens[0].astype(f32)
    inverse_own = lax.rsqrt(jnp.mean(x_own * x_own, axis=-1, keepdims=True) + norm_eps)
    d_input_norm = norm_backward(total[1], x_own, inverse_own, vectors[0])
    tokens_grad = d_resid + d_input_norm

    small = jnp.sum(attn_share[:, 4 * shard :].astype(f32), axis=0).reshape(2, 8, 128)
    small = jnp.moveaxis(small[: shard // 128], 0, 1).reshape(8, shard)
    gain_grad = small[:2]
    bias_grad = small[2:5]
    gain_new, gain_second_new = adam_update(gains, gain_grad, gain_first, gain_second)
    bias_new, bias_second_new = adam_update(qkv_bias, bias_grad, bias_first, bias_second)
    return (
        layer_out[None],
        tokens_grad[None],
        attn_grad,
        mlp_grad,
        attn_mom,
        mlp_mom,
        attn_new,
        mlp_new,
        gain_grad,
        gain_second_new,
        gain_new,
        bias_grad,
        bias_second_new,
        bias_new,
    )


def solution(mesh):
    return jax.shard_map(
        per_device,
        mesh=mesh,
        in_specs=(
            P("wt", "seq", None),
            P("wt", "seq", None),
            P("wt", None),
            P(None, "wt", None),
            P(None, "wt", None),
            P(None, "wt", None),
            P(None, "wt", None),
            P(None, "wt"),
            P(None, "wt"),
            P(None, "wt"),
            P(None, "wt"),
            P(None, "wt"),
            P(None, "wt"),
        ),
        out_specs=(
            P("wt", "seq", None),
            P("wt", "seq", None),
            P(None, "wt", None),
            P(None, "wt", None),
            P(None, "wt", None),
            P(None, "wt", None),
            P(None, "wt", "seq"),
            P(None, "wt", "seq"),
            P(None, "wt"),
            P(None, "wt"),
            P(None, "wt"),
            P(None, "wt"),
            P(None, "wt"),
            P(None, "wt"),
        ),
        check_vma=False,
    )
```

```python
import functools
import math

import jax
import jax.numpy as jnp
from jax import lax
from jax.experimental import pallas as pl
from jax.experimental.pallas import tpu as pltpu
from jax.sharding import PartitionSpec as P

HEAD_DIM = 64
NS_STEPS = 5
STEP = 10

norm_eps = 1e-06
rope_base = 1000000.0
coef_a = 3.4445
coef_b = -4.775
coef_c = 2.0315
momentum_decay = 0.95
matrix_rate = 0.5
decay_rate = 0.01
first_decay = 0.9
second_decay = 0.95
vector_rate = 0.25
adam_eps = 1e-08
ortho_eps = 1e-07
masked_score = -1e30
tile = 256
vmem_limit = 62 * 2**20

MLP_OWNERS = (0, 2, 4)
ATTN_OWNERS = (1, 3, 5, 6)

f32 = jnp.float32
bf16 = jnp.bfloat16


def dot32(a, b, ca, cb):
    return lax.dot_general(a, b, (((ca,), (cb,)), ((), ())), preferred_element_type=f32)


def doc_layout(bounds, length):
    places = jnp.arange(length, dtype=jnp.int32)
    first_bound = bounds[0]
    second_bound = bounds[1]
    doc_index = (places >= first_bound).astype(jnp.int32) + (places >= second_bound).astype(
        jnp.int32
    )
    doc_start = jnp.where(
        places < first_bound, 0, jnp.where(places < second_bound, first_bound, second_bound)
    )
    return (doc_index, (places - doc_start).astype(f32))


def rope_tables(position, cols):
    half_dim = HEAD_DIM // 2
    lane = jnp.arange(cols, dtype=jnp.int32) % HEAD_DIM
    frequency = rope_base ** (-2.0 * jnp.arange(half_dim, dtype=f32) / HEAD_DIM)
    angles = position[:, None] * frequency[None, :]
    repeat = cols // half_dim
    cosine = jnp.concatenate([jnp.cos(angles)] * repeat, 1)
    sine = jnp.concatenate([jnp.sin(angles)] * repeat, 1)
    return cosine, jnp.where(lane < half_dim, -1.0, 1.0)[None, :] * sine


def swap_halves(values):
    half_dim = HEAD_DIM // 2
    parts = []
    for first in range(0, values.shape[1], HEAD_DIM):
        parts.append(values[:, first + half_dim : first + HEAD_DIM])
        parts.append(values[:, first : first + half_dim])
    return jnp.concatenate(parts, axis=1)


def visible(bounds_ref, first, rows, length):
    query = first + lax.broadcasted_iota(jnp.int32, (rows, length), 0)
    key = lax.broadcasted_iota(jnp.int32, (rows, length), 1)
    one, two = bounds_ref[0, 0], bounds_ref[0, 1]
    start = jnp.where(query < one, 0, jnp.where(query < two, one, two))
    return (key <= query) & (key >= start)


def slot_of(chips, value):
    slot, bits = 0, chips
    while bits > 1:
        slot = slot * 2 + (value & 1)
        value = value >> 1
        bits //= 2
    return slot


def front_kernel(
    bounds_ref,
    place_ref,
    same_ref,
    other_ref,
    weight_ref,
    gain_ref,
    bias_ref,
    cosine_ref,
    sine_ref,
    x_ref,
    normed_ref,
    query_ref,
    key_ref,
    value_ref,
    attended_ref,
    log_ref,
):
    length = x_ref.shape[0]
    cols = query_ref.shape[1]
    chips, rows, _ = same_ref.shape
    for chip in range(chips):
        at = pl.ds(chip * 2 * rows, 2 * rows)
        slot = slot_of(chips, place_ref[0] ^ chip)
        low = pl.ds(chip * 2 * rows + place_ref[1] * rows, rows)
        high = pl.ds(chip * 2 * rows + (1 - place_ref[1]) * rows, rows)
        x_ref[low, :] = same_ref[slot]
        x_ref[high, :] = other_ref[slot]
        x = x_ref[at, :].astype(f32)
        inverse = lax.rsqrt(jnp.mean(x * x, axis=-1, keepdims=True) + norm_eps)
        normed = (x * inverse * gain_ref[...]).astype(bf16)
        normed_ref[at, :] = normed
        projected = (dot32(normed, weight_ref[...], 1, 0) + bias_ref[...]).astype(bf16).astype(f32)
        cosine, sine = cosine_ref[at, :], sine_ref[at, :]
        query = projected[:, :cols]
        key = projected[:, cols : 2 * cols]
        query_ref[at, :] = (query * cosine + swap_halves(query) * sine).astype(bf16)
        key_ref[at, :] = (key * cosine + swap_halves(key) * sine).astype(bf16)
        value_ref[at, :] = projected[:, 2 * cols :].astype(bf16)
    for first in range(0, length, tile):
        at, keys = pl.ds(first, tile), pl.ds(0, first + tile)
        allowed = visible(bounds_ref, first, tile, first + tile)
        attended = []
        for head in range(cols // HEAD_DIM):
            lanes = pl.ds(head * HEAD_DIM, HEAD_DIM)
            scores = dot32(query_ref[at, lanes], key_ref[keys, lanes], 1, 1)
            scores = jnp.where(allowed, scores * HEAD_DIM ** (-0.5), masked_score)
            peak = jnp.max(scores, axis=-1, keepdims=True)
            exponent = jnp.exp(scores - peak)
            total = jnp.sum(exponent, axis=-1, keepdims=True)
            weights = (exponent * (1.0 / total)).astype(bf16)
            attended.append(dot32(weights, value_ref[keys, lanes], 1, 0))
            log_ref[at, pl.ds(head, 1)] = peak + jnp.log(total)
        attended_ref[at, :] = jnp.concatenate(attended, axis=1).astype(bf16)


def vmem_specs(count):
    return [pl.BlockSpec(memory_space=pltpu.VMEM)] * count


def whole_spec(shape):
    return pl.BlockSpec(shape, lambda i: (0,) * len(shape))


def whole_specs(arrays):
    return [whole_spec(value.shape) for value in arrays]


def any_specs(count):
    return [pl.BlockSpec(memory_space=pl.ANY)] * count


def smem_spec():
    return pl.BlockSpec(memory_space=pltpu.SMEM)


def front(bounds, place, same, other, weight, gain, bias, cosine, sine):
    chips, rows, width = same.shape
    length, cols = cosine.shape
    part = jax.ShapeDtypeStruct((length, cols), bf16)
    shapes = [
        jax.ShapeDtypeStruct((length, width), bf16),
        jax.ShapeDtypeStruct((length, width), bf16),
        part,
        part,
        part,
        part,
        jax.ShapeDtypeStruct((length, cols // HEAD_DIM), f32),
    ]
    args = (same, other, weight, gain, bias, cosine, sine)
    return pl.pallas_call(
        front_kernel,
        grid=(1,),
        in_specs=[smem_spec()] * 2 + whole_specs(args),
        out_specs=whole_specs(shapes),
        out_shape=shapes,
        compiler_params=pltpu.CompilerParams(vmem_limit_bytes=vmem_limit),
        cost_estimate=pl.CostEstimate(
            flops=8 * 10**9, bytes_accessed=8 * 10**6, transcendentals=2 * 10**6
        ),
        name="front",
    )(bounds, place, *args)


def store_split(place_ref, mine_ref, other_ref, index, value):
    rows = value.shape[0] // 2
    core = place_ref[1]
    top, low = value[:rows], value[rows:]
    mine_ref[0, index] = jnp.where(core == 0, top, low)
    other_ref[0, index] = jnp.where(core == 0, low, top).astype(bf16)


def split_out(chips, sums, rows, width):
    spec = pl.BlockSpec(
        (1, sums, rows, width), lambda i, place: (slot_of(chips, i ^ place[0]), 0, 0, 0)
    )
    shape = (chips, sums, rows, width)
    return [spec, spec], [jax.ShapeDtypeStruct(shape, f32), jax.ShapeDtypeStruct(shape, bf16)]


def middle_kernel(
    place_ref,
    same_ref,
    other_ref,
    x_ref,
    dy_ref,
    weight_ref,
    gain_ref,
    normed_ref,
    d_gate_ref,
    d_up_ref,
    hidden_ref,
    d_mine_ref,
    d_other_ref,
    resid_ref,
    gain_part_ref,
):
    width = x_ref.shape[1]
    cols = d_gate_ref.shape[1]
    rows = resid_ref.shape[0]
    gate_w = weight_ref.at[:, pl.ds(width, cols)]
    up_w = weight_ref.at[:, pl.ds(width + cols, cols)]
    down_w = weight_ref.at[:, pl.ds(width + 2 * cols, cols)]
    attended = []
    for chip in range(same_ref.shape[0]):
        slot = slot_of(same_ref.shape[0], place_ref[0] ^ chip)
        same, other = same_ref[slot], other_ref[slot]
        attended.append(jnp.where(place_ref[1] == 0, same, other))
        attended.append(jnp.where(place_ref[1] == 0, other, same))
    attended = jnp.concatenate(attended, axis=1)
    resid = x_ref[...].astype(f32) + dot32(attended, weight_ref[:, pl.ds(0, width)], 1, 0)

    @pl.when(pl.program_id(0) == place_ref[0])
    def _():
        resid_ref[...] = jnp.where(place_ref[1] == 0, resid[:rows], resid[rows:])

    inverse = lax.rsqrt(jnp.mean(resid * resid, axis=-1, keepdims=True) + norm_eps)
    normed = (resid * inverse * gain_ref[...]).astype(bf16)
    normed_ref[...] = normed
    gate = dot32(normed, gate_w[...], 1, 0)
    up = dot32(normed, up_w[...], 1, 0)
    d_hidden = dot32(dy_ref[...], down_w[...], 1, 0)
    sigmoid = jax.nn.sigmoid(gate)
    silu = gate * sigmoid
    hidden = (silu * up).astype(bf16)
    hidden_ref[...] = hidden
    d_gate = (d_hidden * up * (sigmoid * (1.0 + gate * (1.0 - sigmoid)))).astype(bf16)
    d_up = (d_hidden * silu).astype(bf16)
    d_gate_ref[...] = d_gate
    d_up_ref[...] = d_up
    d_normed = dot32(d_gate, gate_w[...], 1, 1) + dot32(d_up, up_w[...], 1, 1)
    store_split(place_ref, d_mine_ref, d_other_ref, 0, d_normed)

    @pl.when(pl.program_id(0) == 0)
    def _():
        gain_part_ref[...] = jnp.zeros_like(gain_part_ref)

    gain_part_ref[...] += jnp.sum(d_normed * resid * inverse, axis=0, keepdims=True)


def middle(place, same, other, x, dy, weight, gain):
    chips, length, head_cols = same.shape
    count = 2 * chips
    width = x.shape[1]
    cols = (weight.shape[1] - width) // 3
    half = length // count
    rows = 2 * half

    def block(size):
        return pl.BlockSpec((rows, size), lambda i, place: (i, 0))

    def whole(shape):
        return pl.BlockSpec(shape, lambda i, place: (0,) * len(shape))

    split_specs, split_shapes = split_out(chips, 1, half, width)
    wide = jax.ShapeDtypeStruct((length, cols), bf16)
    return pl.pallas_call(
        middle_kernel,
        grid_spec=pltpu.PrefetchScalarGridSpec(
            num_scalar_prefetch=1,
            grid=(chips,),
            in_specs=[
                pl.BlockSpec((chips, rows, head_cols), lambda i, place: (0, i, 0)),
                pl.BlockSpec((chips, rows, head_cols), lambda i, place: (0, i, 0)),
                block(width),
                block(width),
                whole(weight.shape),
                whole(gain.shape),
            ],
            out_specs=[
                block(width),
                block(cols),
                block(cols),
                block(cols),
                *split_specs,
                whole((half, width)),
                whole((1, width)),
            ],
        ),
        out_shape=[
            jax.ShapeDtypeStruct((length, width), bf16),
            wide,
            wide,
            wide,
            *split_shapes,
            jax.ShapeDtypeStruct((half, width), f32),
            jax.ShapeDtypeStruct((1, width), f32),
        ],
        compiler_params=pltpu.CompilerParams(vmem_limit_bytes=vmem_limit),
        cost_estimate=pl.CostEstimate(
            flops=10 * 10**9, bytes_accessed=20 * 10**6, transcendentals=10**6
        ),
        name="middle",
    )(place, same, other, x, dy, weight, gain)


def pair_kernel(kept, extra, mine_ref, got_ref, *refs):
    keep_ref, sends = refs[extra], refs[extra + 1 :]
    for slot in range(kept):
        keep_ref[slot] = mine_ref[slot] + got_ref[slot].astype(f32)
    for slot in range(kept, mine_ref.shape[0]):
        value = (mine_ref[slot] + got_ref[slot].astype(f32)).astype(bf16)
        if len(sends) == 1:
            sends[0][slot - kept] = value
        else:
            sends[slot - kept][0] = value


def pair_sums(mine, got, kept, together, after):
    slots, sums, rows, width = mine.shape
    step = 32

    def spec(count):
        return pl.BlockSpec((count, sums, step, width), lambda i: (0, 0, i, 0))

    counts = [slots - kept] if together else [1] * (slots - kept)
    return pl.pallas_call(
        functools.partial(pair_kernel, kept, len(after)),
        grid=(rows // step,),
        in_specs=[spec(slots)] * 2 + any_specs(len(after)),
        out_specs=[spec(kept)] + [spec(count) for count in counts],
        out_shape=[jax.ShapeDtypeStruct((kept, sums, rows, width), f32)]
        + [jax.ShapeDtypeStruct((count, sums, rows, width), bf16) for count in counts],
        compiler_params=pltpu.CompilerParams(vmem_limit_bytes=vmem_limit),
        name="pair_sums",
    )(mine, got, *after)


def post_kernel(extra, own_ref, resid_ref, dy_ref, gain_ref, weight_ref, *refs):
    arrived, (pair_ref, d_resid_ref) = refs[: -2 - extra], refs[-2:]
    d_normed = own_ref[0, 0]
    for ref in arrived:
        d_normed = d_normed + ref[0, 0].astype(f32)
    resid = resid_ref[...]
    inverse = lax.rsqrt(jnp.mean(resid * resid, axis=-1, keepdims=True) + norm_eps)
    scaled = d_normed * gain_ref[...]
    d_resid = (
        dy_ref[...].astype(f32)
        + inverse * scaled
        - resid * (inverse * inverse * inverse) * jnp.mean(scaled * resid, axis=-1, keepdims=True)
    )
    d_resid_ref[...] = d_resid
    low = d_resid.astype(bf16)
    d_attn = dot32(low, weight_ref[...], 1, 1).astype(bf16)
    cols = pair_ref.shape[3]
    for part in range(pair_ref.shape[0]):
        pair_ref[part, 0] = d_attn[:, part * cols : (part + 1) * cols]
        pair_ref[part, 1] = low[:, part * cols : (part + 1) * cols]


def post(own, arrived, resid, dy, gain, weight, count, after):
    rows, width = resid.shape
    cols = width // count

    def whole(shape):
        return pl.BlockSpec(shape, lambda i: (0,) * len(shape))

    return pl.pallas_call(
        functools.partial(post_kernel, len(after)),
        grid=(1,),
        in_specs=[whole(own.shape), whole(resid.shape), whole(dy.shape), whole(gain.shape)]
        + [whole((width, width))]
        + [whole(value.shape) for value in arrived]
        + any_specs(len(after)),
        out_specs=[whole((count, 2, rows, cols)), whole((rows, width))],
        out_shape=[
            jax.ShapeDtypeStruct((count, 2, rows, cols), bf16),
            jax.ShapeDtypeStruct((rows, width), f32),
        ],
        compiler_params=pltpu.CompilerParams(vmem_limit_bytes=vmem_limit),
        name="post",
    )(own, resid, dy, gain, weight, *arrived, *after)


def mlp_grads_kernel(
    parts, extra, normed_ref, dy_ref, d_gate_ref, d_up_ref, hidden_ref, *refs
):
    out_ref = refs[extra]
    shard = out_ref.shape[0] // (3 * parts)
    for part in range(parts):
        at = pl.ds(part * shard, shard)
        normed = normed_ref[:, at]
        pairs = [(normed, d_gate_ref), (normed, d_up_ref), (dy_ref[:, at], hidden_ref)]
        for index, (left, right_ref) in enumerate(pairs):
            out_ref[pl.ds((3 * part + index) * shard, shard), :] = dot32(
                left, right_ref[...], 0, 0
            ).astype(bf16)


def mlp_grads(normed, dy, d_gate, d_up, hidden, parts, after):
    width = normed.shape[1]
    args = (normed, dy, d_gate, d_up, hidden)
    shape = jax.ShapeDtypeStruct((3 * width, hidden.shape[1]), bf16)
    return pl.pallas_call(
        functools.partial(mlp_grads_kernel, parts, len(after)),
        grid=(1,),
        in_specs=whole_specs(args) + any_specs(len(after)),
        out_specs=whole_spec(shape.shape),
        out_shape=shape,
        compiler_params=pltpu.CompilerParams(vmem_limit_bytes=vmem_limit),
        cost_estimate=pl.CostEstimate(
            flops=3 * 10**9, bytes_accessed=9 * 10**6, transcendentals=0
        ),
        name="mlp_grads",
    )(*args, *after)


def back_kernel(
    parts,
    bounds_ref,
    control_ref,
    query_ref,
    key_ref,
    value_ref,
    log_ref,
    arrived_ref,
    normed_ref,
    same_ref,
    other_ref,
    cosine_ref,
    sine_ref,
    weight_ref,
    gain_ref,
    gain_two_ref,
    squares_ref,
    d_qkv_ref,
    *refs,
):
    grads_refs, (d_key_ref, d_value_ref, d_attn_ref, d_resid_ref) = refs[:parts], refs[parts:]
    length, cols = query_ref.shape
    count, _, rows, _ = arrived_ref.shape
    scale = HEAD_DIM ** (-0.5)
    for part in range(count):
        d_attn_ref[pl.ds(part * rows, rows), :] = arrived_ref[part, 0]
        d_resid_ref[pl.ds(part * rows, rows), :] = arrived_ref[part, 1]
    d_key_ref[...] = jnp.zeros_like(d_key_ref)
    d_value_ref[...] = jnp.zeros_like(d_value_ref)

    def undo(values, at):
        return values * cosine_ref[at, :] - swap_halves(values) * sine_ref[at, :]

    for first in range(0, length, tile):
        at, keys = pl.ds(first, tile), pl.ds(0, first + tile)
        allowed = visible(bounds_ref, first, tile, first + tile)
        d_query, d_key, d_value = [], [], []
        for head in range(cols // HEAD_DIM):
            lanes = pl.ds(head * HEAD_DIM, HEAD_DIM)
            query, d_out = query_ref[at, lanes], d_attn_ref[at, lanes]
            key, value = key_ref[keys, lanes], value_ref[keys, lanes]
            scores = jnp.where(allowed, dot32(query, key, 1, 1) * scale, masked_score)
            weights = jnp.exp(scores - log_ref[at, pl.ds(head, 1)])
            d_value.append(dot32(weights.astype(bf16), d_out, 0, 0))
            d_weights = dot32(d_out, value, 1, 1)
            inner = jnp.sum(weights * d_weights, axis=-1, keepdims=True)
            d_scores = (weights * (d_weights - inner)).astype(bf16)
            d_query.append(dot32(d_scores, key, 1, 0) * scale)
            d_key.append(dot32(d_scores, query, 0, 0) * scale)
        d_key_ref[keys, :] += jnp.concatenate(d_key, axis=1)
        d_value_ref[keys, :] += jnp.concatenate(d_value, axis=1)
        d_qkv_ref[at, pl.ds(0, cols)] = undo(jnp.concatenate(d_query, axis=1), at).astype(bf16)
    for first in range(0, length, tile):
        at = pl.ds(first, tile)
        d_qkv_ref[at, pl.ds(cols, cols)] = undo(d_key_ref[at, :], at).astype(bf16)
        d_qkv_ref[at, pl.ds(2 * cols, cols)] = d_value_ref[at, :].astype(bf16)
    shard = gain_ref.shape[1] // parts
    pad = grads_refs[0].shape[1]
    pieces = shard // cols
    bias = jnp.sum(d_qkv_ref[...].astype(f32), axis=0, keepdims=True)
    lane = lax.broadcasted_iota(jnp.int32, squares_ref.shape, 1)
    row = lax.broadcasted_iota(jnp.int32, squares_ref.shape, 0)
    squares = jnp.sum(jnp.where(lane == row, squares_ref[...], 0.0), axis=0, keepdims=True)
    squares_high = squares.astype(bf16).astype(f32)
    rest = jnp.zeros((1, shard - squares.shape[1]), f32)

    def wide(value):
        return value if shard == 128 else jnp.concatenate([value, rest], axis=1)

    for part in range(parts):
        block = control_ref[2] ^ part
        grads_ref = grads_refs[part]
        at = pl.ds(pl.multiple_of(block * shard, 128), shard)
        grads = dot32(normed_ref[:, at], d_qkv_ref[...], 0, 0)
        gain_one = lax.dot_general(
            jnp.ones((8, 3 * cols), f32),
            grads * weight_ref[at, :].astype(f32),
            (((1,), (1,)), ((), ())),
            precision=lax.Precision.HIGHEST,
            preferred_element_type=f32,
        )[0:1]
        grads = grads.astype(bf16)
        for index in range(3):
            grads_ref[pl.ds(index * shard, shard), pl.ds(0, cols)] = grads[
                :, index * cols : (index + 1) * cols
            ]
        for piece in range(pieces):
            place = block * pieces + piece
            slot = slot_of(same_ref.shape[0], (place >> 1) ^ (control_ref[1] >> 1))
            near = ((place ^ control_ref[1]) & 1) == 0
            attended = jnp.where(near, same_ref[slot], other_ref[slot])
            grads_ref[pl.ds(3 * shard + piece * cols, cols), pl.ds(0, cols)] = dot32(
                attended, d_resid_ref[...], 0, 0
            ).astype(bf16)
        if pad > cols:
            grads_ref[pl.ds(0, 4 * shard), pl.ds(cols, pad - cols)] = jnp.zeros(
                (4 * shard, pad - cols), bf16
            )
        small = [gain_one / gain_ref[:, at], gain_two_ref[:, at]]
        for index in range(3):
            own = bias[:, index * cols : (index + 1) * cols]
            small.append(
                jnp.concatenate(
                    [
                        jnp.where(block * pieces + piece == control_ref[1], own, 0.0)
                        for piece in range(pieces)
                    ],
                    axis=1,
                )
            )
        small += [wide(squares_high), wide(squares - squares_high), jnp.zeros((1, shard), f32)]
        small = jnp.concatenate(small, axis=0)
        small = [small[:, first : first + 128] for first in range(0, shard, 128)]
        small += [jnp.zeros((8, 128), f32)] * (2 - len(small))
        grads_ref[pl.ds(4 * shard, 16), :] = jnp.concatenate(small, axis=0).astype(bf16)


def back(bounds, control, args, parts):
    query, normed = args[0], args[5]
    length, cols = query.shape
    width = normed.shape[1]
    pad = -(-cols // 128) * 128
    shapes = [jax.ShapeDtypeStruct((length, 3 * cols), bf16)]
    shapes += [jax.ShapeDtypeStruct((4 * width // parts + 16, pad), bf16)] * parts
    results = pl.pallas_call(
        functools.partial(back_kernel, parts),
        grid=(1,),
        in_specs=[smem_spec()] * 2 + whole_specs(args),
        out_specs=whole_specs(shapes),
        out_shape=shapes,
        scratch_shapes=[
            pltpu.VMEM((length, cols), f32),
            pltpu.VMEM((length, cols), f32),
            pltpu.VMEM((length, cols), bf16),
            pltpu.VMEM((length, cols), bf16),
        ],
        compiler_params=pltpu.CompilerParams(vmem_limit_bytes=vmem_limit),
        cost_estimate=pl.CostEstimate(
            flops=10 * 10**9, bytes_accessed=8 * 10**6, transcendentals=2 * 10**6
        ),
        name="back",
    )(bounds, control, *args)
    return results[0], results[1:]


def late_kernel(place_ref, hidden_ref, down_ref, d_qkv_ref, weight_ref, mine_ref, other_ref):
    store_split(place_ref, mine_ref, other_ref, 0, dot32(hidden_ref[...], down_ref[...], 1, 1))
    store_split(place_ref, mine_ref, other_ref, 1, dot32(d_qkv_ref[...], weight_ref[...], 1, 1))


def late_sums(place, hidden, down, d_qkv, weight, count):
    length, cols = d_qkv.shape
    width = weight.shape[0]
    chips = count // 2
    half = length // count
    rows = 2 * half

    def block(size):
        return pl.BlockSpec((rows, size), lambda i, place: (i, 0))

    def whole(shape):
        return pl.BlockSpec(shape, lambda i, place: (0, 0))

    split_specs, split_shapes = split_out(chips, 2, half, width)
    return pl.pallas_call(
        late_kernel,
        grid_spec=pltpu.PrefetchScalarGridSpec(
            num_scalar_prefetch=1,
            grid=(chips,),
            in_specs=[
                block(hidden.shape[1]),
                whole(down.shape),
                block(cols),
                whole(weight.shape),
            ],
            out_specs=split_specs,
        ),
        out_shape=split_shapes,
        compiler_params=pltpu.CompilerParams(vmem_limit_bytes=vmem_limit),
        cost_estimate=pl.CostEstimate(
            flops=2 * 10**9, bytes_accessed=16 * 10**6, transcendentals=0
        ),
        name="late_sums",
    )(place, hidden, down, d_qkv, weight)


def picked_kernel(pick_ref, momentum_ref, out_ref):
    count, rows, pad = out_ref.shape
    cols = momentum_ref.shape[2] // count
    for turn in range(count):
        value = momentum_ref[0, :, pl.ds(turn * cols, cols)] * momentum_decay
        out_ref[turn, :, pl.ds(0, cols)] = value
        if pad > cols:
            out_ref[turn, :, pl.ds(cols, pad - cols)] = jnp.zeros((rows, pad - cols), f32)


def picked(momentum, pick, count):
    rows, width = momentum.shape[1:]
    pad = -(-(width // count) // 128) * 128
    step = min(64, rows)
    return pl.pallas_call(
        picked_kernel,
        grid_spec=pltpu.PrefetchScalarGridSpec(
            num_scalar_prefetch=1,
            grid=(rows // step,),
            in_specs=[pl.BlockSpec((1, step, width), lambda i, pick: (pick[0], i, 0))],
            out_specs=pl.BlockSpec((count, step, pad), lambda i, pick: (0, i, 0)),
        ),
        out_shape=jax.ShapeDtypeStruct((count, rows, pad), f32),
        compiler_params=pltpu.CompilerParams(vmem_limit_bytes=vmem_limit),
        cost_estimate=pl.CostEstimate(
            flops=rows * width, bytes_accessed=8 * rows * width, transcendentals=0
        ),
        name="picked",
    )(pick, momentum)


def squares_kernel(order_ref, attn_ref, mlp_ref, out_ref):
    @pl.when(pl.program_id(0) == 0)
    def _():
        out_ref[...] = jnp.zeros_like(out_ref)

    at = 0
    for ref in (attn_ref, mlp_ref):
        for index in range(ref.shape[0]):
            value = ref[index].astype(bf16).astype(f32)
            total = jnp.sum(jnp.sum(value * value, axis=0, keepdims=True), axis=1, keepdims=True)
            out_ref[pl.ds(at, 1), :] += jnp.broadcast_to(total, (1, out_ref.shape[1]))
            at += 1


def block_kernel(extra, pick_ref, share_ref, old_ref, *refs):
    refs[extra][...] = (old_ref[...] + share_ref[...].astype(f32)).astype(bf16)


def new_block(share, old, pick, after):
    count, shard, pad = old.shape
    step = 2
    return pl.pallas_call(
        functools.partial(block_kernel, len(after)),
        grid_spec=pltpu.PrefetchScalarGridSpec(
            num_scalar_prefetch=1,
            grid=(count // step,),
            in_specs=[
                pl.BlockSpec((step, shard, pad), lambda i, pick: (i, pick[0], 0)),
                pl.BlockSpec((step, shard, pad), lambda i, pick: (i, 0, 0)),
            ]
            + any_specs(len(after)),
            out_specs=pl.BlockSpec((step, shard, pad), lambda i, pick: (i, 0, 0)),
        ),
        out_shape=jax.ShapeDtypeStruct(old.shape, bf16),
        compiler_params=pltpu.CompilerParams(vmem_limit_bytes=vmem_limit),
        cost_estimate=pl.CostEstimate(
            flops=old.size, bytes_accessed=8 * old.size, transcendentals=0
        ),
        name="new_block",
    )(pick, share, old, *after)


def sums_of_squares(order, attn, mlp):
    rows = attn.shape[1]
    step = min(64, rows)
    return pl.pallas_call(
        squares_kernel,
        grid=(rows // step,),
        in_specs=[
            smem_spec(),
            pl.BlockSpec((attn.shape[0], step, attn.shape[2]), lambda i: (0, i, 0)),
            pl.BlockSpec((mlp.shape[0], step, mlp.shape[2]), lambda i: (0, i, 0)),
        ],
        out_specs=pl.BlockSpec((8, 128), lambda i: (0, 0)),
        out_shape=jax.ShapeDtypeStruct((8, 128), f32),
        compiler_params=pltpu.CompilerParams(vmem_limit_bytes=vmem_limit),
        cost_estimate=pl.CostEstimate(
            flops=2 * (attn.size + mlp.size),
            bytes_accessed=4 * (attn.size + mlp.size),
            transcendentals=0,
        ),
        name="sums_of_squares",
    )(order, attn, mlp)


def pack_kernel(place_ref, master_ref, vectors_ref, *refs):
    out_ref = refs[-1]
    shard = master_ref.shape[1]
    cols = out_ref.shape[1] // 3
    for index in range(3):
        value = master_ref[index].astype(bf16)
        part = value[:, :cols]
        for at in range(1, value.shape[1] // cols):
            part = jnp.where(place_ref[1] == at, value[:, at * cols : (at + 1) * cols], part)
        out_ref[pl.ds(0, shard), pl.ds(index * cols, cols)] = part
    out_ref[pl.ds(shard, 16), :] = vectors_ref[...].astype(bf16)


def pack(seq_index, master, vectors, cols, after):
    shard = master.shape[1]
    lanes = max(cols, 128)
    place = jnp.stack([seq_index // (lanes // cols), seq_index % (lanes // cols)])
    shape = (shard + 16, 3 * cols)
    return pl.pallas_call(
        pack_kernel,
        grid_spec=pltpu.PrefetchScalarGridSpec(
            num_scalar_prefetch=1,
            grid=(1,),
            in_specs=[
                pl.BlockSpec((3, shard, lanes), lambda i, place: (0, 0, place[0])),
                pl.BlockSpec(vectors.shape, lambda i, place: (0, 0)),
            ]
            + any_specs(len(after)),
            out_specs=pl.BlockSpec(shape, lambda i, place: (0, 0)),
        ),
        out_shape=jax.ShapeDtypeStruct(shape, bf16),
        compiler_params=pltpu.CompilerParams(vmem_limit_bytes=vmem_limit),
        name="pack",
    )(place, master, vectors, *after)


def assemble_kernel(places, wt_ref, *refs):
    pieces, out_ref, arrived = refs[: len(places)], refs[-2], refs[-1]
    copies = []
    for at, (bits, first, rows) in enumerate(places):
        start = pl.multiple_of((wt_ref[0] ^ bits) * rows + first, 16)
        target = out_ref.at[pl.ds(start, pieces[at].shape[0]), :]
        copies.append(pltpu.make_async_copy(pieces[at], target, arrived.at[at]))
    for copy in copies:
        copy.start()
    for copy in copies:
        copy.wait()


def assemble(wt_index, pieces, places, rows):
    size = rows * pieces[0].shape[1]
    return pl.pallas_call(
        functools.partial(assemble_kernel, places),
        in_specs=[smem_spec()] + any_specs(len(pieces)),
        out_specs=vmem_specs(1)[0],
        out_shape=jax.ShapeDtypeStruct((rows, pieces[0].shape[1]), pieces[0].dtype),
        scratch_shapes=[pltpu.SemaphoreType.DMA((len(pieces),))],
        compiler_params=pltpu.CompilerParams(vmem_limit_bytes=vmem_limit),
        cost_estimate=pl.CostEstimate(flops=0, bytes_accessed=4 * size, transcendentals=0),
        name="assemble",
    )(wt_index.reshape(1), *pieces)


def norm_backward(d_normed, values, inverse, gain_row):
    scaled = d_normed * gain_row
    return inverse * scaled - values * inverse**3 * jnp.mean(
        scaled * values, axis=-1, keepdims=True
    )


def ortho_kernel(places, extra, control_ref, *refs):
    pieces, outs = refs[: len(places)], refs[len(places) + extra : -8]
    whole, gram, prod, gram_low, prod_low, poly_low, rows, arrived = refs[-8:]
    parts, count = arrived.shape
    shard, pad = outs[0].shape[1:]
    width = gram.shape[0]
    tiles = width // tile

    def upper(j):
        return pl.ds(j * tile, tile), pl.ds(j * tile, width - j * tile)

    def mirror(low):
        for j in range(1, tiles):
            for i in range(j):
                here, there = pl.ds(i * tile, tile), pl.ds(j * tile, tile)
                low[there, here] = low[here, there].T

    @pl.when(control_ref[0] == 1)
    def _():
        copies = [[] for _ in range(parts)]
        for (part, first), piece in zip(places, pieces):
            for turn in range(first, first + piece.shape[0]):
                copies[part].append(
                    pltpu.make_async_copy(
                        piece.at[turn - first],
                        whole.at[pl.ds(part * shard, shard), pl.ds(turn * pad, pad)],
                        arrived.at[part, turn],
                    )
                )
        for part in range(parts):
            for copy in copies[part]:
                copy.start()
        for part in range(parts):
            for copy in copies[part]:
                copy.wait()
        diagonal = lax.broadcasted_iota(jnp.int32, (tile, tile), 0) == lax.broadcasted_iota(
            jnp.int32, (tile, tile), 1
        )
        squares = jnp.zeros((1, 1), f32)
        for j in range(tiles):
            up, at = upper(j)
            gram[up, at] = dot32(whole[up, :], whole[at, :], 1, 1)
            entries = jnp.where(diagonal, gram[up, up], 0.0)
            squares = squares + jnp.sum(
                jnp.sum(entries, axis=1, keepdims=True), axis=0, keepdims=True
            )
        inverse = 1.0 / (jnp.sqrt(squares) + ortho_eps)
        for j in range(tiles):
            up, at = upper(j)
            scaled = gram[up, at] * (inverse * inverse)
            gram[up, at] = scaled
            gram_low[up, at] = scaled.astype(bf16)
        mirror(gram_low)

        def step(index, carry):
            poly = poly_low.at[index]
            for j in range(tiles):
                up, at = upper(j)
                poly[up, at] = (
                    coef_b * gram[up, at] + coef_c * dot32(gram_low[up, :], gram_low[:, at], 1, 0)
                ).astype(bf16)
            mirror(poly)
            for j in range(tiles):
                up, at = upper(j)
                value = coef_a * gram[up, at] + dot32(poly[up, :], gram_low[:, at], 1, 0)
                prod[up, at] = value
                prod_low[up, at] = value.astype(bf16)
            mirror(prod_low)
            for j in range(tiles):
                up, at = upper(j)
                value = coef_a * prod[up, at] + dot32(prod_low[up, :], poly[:, at], 1, 0)
                gram[up, at] = value
                gram_low[up, at] = value.astype(bf16)
            mirror(gram_low)
            return carry

        lax.fori_loop(0, NS_STEPS - 1, step, 0)
        unit = lax.broadcasted_iota(jnp.int32, (shard, width), 0) == lax.broadcasted_iota(
            jnp.int32, (shard, width), 1
        )
        rows[...] = (
            coef_a * unit.astype(f32)
            + coef_b * gram[pl.ds(0, shard), :]
            + coef_c * dot32(gram_low[pl.ds(0, shard), :], gram_low[...], 1, 0)
        )

        def apply(index, carry):
            value = rows[...]
            rows[...] = coef_a * value + dot32(
                value.astype(bf16), poly_low[NS_STEPS - 2 - index], 1, 0
            )
            return carry

        lax.fori_loop(0, NS_STEPS - 1, apply, 0)
        scaled = (rows[...] * inverse).astype(bf16)
        for turn in range(count // 2):
            chip = lax.rem((control_ref[1] >> 1) + turn, count // 2)
            for core in range(2):
                lanes = pl.ds(pl.multiple_of((2 * chip + core) * pad, 128), pad)
                outs[turn][core] = dot32(scaled, whole[:, lanes], 1, 0).astype(bf16)


def orthogonalize(control, pieces, places, parts, after):
    count, shard, pad = pieces[0].shape
    width = shard * parts
    return pl.pallas_call(
        functools.partial(ortho_kernel, places, len(after)),
        out_shape=[jax.ShapeDtypeStruct((2, shard, pad), bf16)] * (count // 2),
        in_specs=[smem_spec()] + any_specs(len(pieces) + len(after)),
        out_specs=vmem_specs(count // 2),
        scratch_shapes=[
            pltpu.VMEM((width, count * pad), bf16),
            pltpu.VMEM((width, width), f32),
            pltpu.VMEM((width, width), f32),
            pltpu.VMEM((width, width), bf16),
            pltpu.VMEM((width, width), bf16),
            pltpu.VMEM((NS_STEPS - 1, width, width), bf16),
            pltpu.VMEM((shard, width), f32),
            pltpu.SemaphoreType.DMA((parts, count)),
        ],
        compiler_params=pltpu.CompilerParams(vmem_limit_bytes=vmem_limit),
        cost_estimate=pl.CostEstimate(
            flops=30 * 10**9, bytes_accessed=4 * count * shard * pad, transcendentals=0
        ),
        name="orthogonalize",
    )(control, *pieces, *after)


def update_kernel(owners, control_ref, rate_ref, own_ref, *refs):
    arrived, other_ref, out_ref = refs[:-2], refs[-2], refs[-1]
    chips, cols = len(arrived), own_ref.shape[2]
    chip, core = control_ref[1] >> 1, control_ref[1] & 1
    for index, owner in enumerate(owners):
        turn = lax.rem(chip - owner // 2 + chips, chips)
        for at in range(chips):

            @pl.when(turn == at)
            def _():
                step = jnp.where(core == owner % 2, arrived[at][core], other_ref[at])
                out_ref[index] = (
                    own_ref[index] * (1.0 - matrix_rate * decay_rate)
                    - rate_ref[index] * step[:, :cols].astype(f32)
                )


def update(control, rate, own, arrived, other, owners):
    return pl.pallas_call(
        functools.partial(update_kernel, owners),
        grid=(1,),
        in_specs=[smem_spec()] * 2 + whole_specs((own, *arrived, other)),
        out_specs=whole_spec(own.shape),
        out_shape=jax.ShapeDtypeStruct(own.shape, f32),
        compiler_params=pltpu.CompilerParams(vmem_limit_bytes=vmem_limit),
        name="update",
    )(control, rate, own, *arrived, other)


def finish_kernel(matrices, *refs):
    shares, momentum_ref, (grad_ref, new_ref) = refs[:matrices], refs[matrices], refs[-2:]
    count = shares[0].shape[0]
    cols = grad_ref.shape[2] // count
    for index in range(matrices):
        for turn in range(count):
            at = pl.ds(turn * cols, cols)
            grad = shares[index][turn].astype(f32)[:, :cols]
            grad_ref[index, :, at] = grad
            new_ref[index, :, at] = momentum_decay * momentum_ref[index, :, at] + grad


def finish(share, momentum, after):
    count, _, pad = share.shape
    matrices, shard, width = momentum.shape
    step = min(64, shard)
    steps = shard // step
    whole = pl.BlockSpec((matrices, step, width), lambda i: (0, i, 0))
    parts = [
        pl.BlockSpec((count, step, pad), lambda i, index=index: (0, index * steps + i, 0))
        for index in range(matrices)
    ]
    size = matrices * shard * width
    return pl.pallas_call(
        functools.partial(finish_kernel, matrices),
        grid=(steps,),
        in_specs=parts + [whole] + any_specs(len(after)),
        out_specs=[whole, whole],
        out_shape=[jax.ShapeDtypeStruct(momentum.shape, f32)] * 2,
        compiler_params=pltpu.CompilerParams(vmem_limit_bytes=vmem_limit),
        cost_estimate=pl.CostEstimate(
            flops=2 * size, bytes_accessed=14 * size, transcendentals=0
        ),
        name="finish",
    )(*[share] * matrices, momentum, *after)


def adam_update(parameter, gradient, first_state, second_state):
    first_new = first_decay * first_state + (1.0 - first_decay) * gradient
    second_new = second_decay * second_state + (1.0 - second_decay) * gradient * gradient
    first_hat = first_new / (1.0 - first_decay**STEP)
    second_hat = second_new / (1.0 - second_decay**STEP)
    return (parameter - vector_rate * first_hat / (jnp.sqrt(second_hat) + adam_eps), second_new)


def swap(value, axis, bits, count):
    return lax.ppermute(value, axis, [(i, i ^ bits) for i in range(count)])


def sum_all(value, axis, count):
    bits = 1
    while bits < count:
        value = value + swap(value, axis, bits, count)
        bits *= 2
    return value


def near_wt(block, wt_count):
    return [swap(block, "wt", bits, wt_count) for bits in range(1, min(wt_count, 3))]


def far_wt(block, near, wt_count):
    rows = block.shape[0]
    if wt_count == 4:
        half = rows // 2
        pieces = [swap(near[0][:half], "wt", 2, wt_count), swap(near[1][half:], "wt", 1, wt_count)]
        return pieces, [(3, 0), (3, half)]
    places = [(bits, 0) for bits in range(1 + len(near), wt_count)]
    return [swap(block, "wt", bits, wt_count) for bits, _ in places], places


def sum_wt(parts, wt_count):
    total = parts[0].astype(f32)
    for bits in range(1, wt_count):
        total = total + swap(parts[bits], "wt", bits, wt_count).astype(f32)
    return total


def chip_order(seq_count):
    chips = seq_count // 2
    return [slot_of(chips, slot) for slot in range(chips)]


def gather_chips(block, seq_count):
    return [block] + [swap(block, "seq", 2 * bits, seq_count) for bits in chip_order(seq_count)[1:]]


def both_cores(blocks, seq_count):
    same = jnp.stack(blocks)
    return same, swap(same, "seq", 1, seq_count)


def send_chips(sends, seq_count):
    return [
        swap(value, "seq", 2 * bits, seq_count)
        for bits, value in zip(chip_order(seq_count)[1:], sends)
    ]


def send_owned(value, bits, owners, wt_count):
    pairs = [
        (owner * wt_count + w, owner * wt_count + (w ^ bits))
        for owner in owners
        for w in range(wt_count)
    ]
    return lax.ppermute(value, ("seq", "wt"), pairs)


def near_owned(block, owners, wt_count):
    return [send_owned(block, bits, owners, wt_count) for bits in range(1, min(wt_count, 3))]


def gather_owned(block, near, owners, wt_count):
    pieces = [block] + near
    places = [(part, 0) for part in range(len(pieces))]
    if wt_count == 4:
        half = block.shape[0] // 2
        pieces.append(send_owned(near[0][:half], 2, owners, wt_count))
        pieces.append(send_owned(near[1][half:], 1, owners, wt_count))
        return pieces, places + [(3, 0), (3, half)]
    for bits in range(len(pieces), wt_count):
        pieces.append(send_owned(block, bits, owners, wt_count))
        places.append((bits, 0))
    return pieces, places


def direct_owned(block, owners, wt_count):
    pieces = [block] + [send_owned(block, bits, owners, wt_count) for bits in range(1, wt_count)]
    return pieces, [(part, 0) for part in range(wt_count)]


def spread_chips(blocks, owners, seq_count):
    chips = seq_count // 2
    return [blocks[0]] + [
        lax.ppermute(
            blocks[turn],
            "seq",
            [(owner, (owner // 2 + turn) % chips * 2 + owner % 2) for owner in owners],
        )
        for turn in range(1, chips)
    ]


def spread_cores(arrived, core, seq_count):
    sent = [lax.dynamic_index_in_dim(value, 1 - core, 0, keepdims=False) for value in arrived]
    return swap(jnp.stack(sent), "seq", 1, seq_count)


def per_device(
    tokens,
    cotangent,
    doc_bounds,
    attn_master,
    mlp_master,
    attn_momentum,
    mlp_momentum,
    gains,
    gain_first,
    gain_second,
    qkv_bias,
    bias_first,
    bias_second,
):
    seq_count = lax.axis_size("seq")
    wt_count = lax.axis_size("wt")
    seq_index = lax.axis_index("seq")
    wt_index = lax.axis_index("wt")
    row_count = tokens.shape[1]
    width = tokens.shape[2]
    ff = mlp_master.shape[2]
    shard = attn_master.shape[1]
    length = row_count * seq_count
    head_cols = width // seq_count
    ff_cols = ff // seq_count

    place = jnp.stack([seq_index // 2, seq_index % 2])

    x_same, x_other = both_cores(gather_chips(tokens[0], seq_count), seq_count)
    own_dy, x_same = lax.optimization_barrier((cotangent[0], x_same))
    dy_low = lax.all_gather(own_dy, "seq", axis=0, tiled=True)

    vectors = jnp.pad(jnp.concatenate([gains, qkv_bias], 0), ((0, 11), (0, 3 * head_cols - shard)))
    _, position = doc_layout(doc_bounds[0], length)
    cosine, sine = rope_tables(position, head_cols)
    qkv_w = pack(seq_index, attn_master, vectors, head_cols, [cosine, sine])
    qkv_w = lax.all_gather(qkv_w, "wt", axis=0)
    place_own, qkv_w = lax.optimization_barrier((seq_index, qkv_w))
    attn_own = lax.dynamic_slice_in_dim(attn_master, place_own * head_cols, head_cols, 2)
    mlp_own = lax.dynamic_slice_in_dim(mlp_master, place_own * ff_cols, ff_cols, 2)
    ff_pad = -(-ff_cols // 128) * 128
    wide_own = jnp.pad(mlp_own, ((0, 0), (0, 0), (0, ff_pad - ff_cols)))
    wide_own = jnp.concatenate([attn_master[3], wide_own[0], wide_own[1], wide_own[2]], 1)
    wide_own = wide_own.astype(bf16)
    wide_near = near_wt(wide_own, wt_count)
    vectors = jnp.moveaxis(qkv_w[:, shard : shard + 5, :shard], 0, 1).reshape(5, width).astype(f32)
    qkv_w = qkv_w[:, :shard].reshape(width, 3 * head_cols)

    bias_own = lax.dynamic_slice_in_dim(vectors[2:5], seq_index * head_cols, head_cols, 1)
    x_low, normed_one, query, key, value, attended, log_total = front(
        doc_bounds,
        place,
        x_same,
        x_other,
        qkv_w,
        vectors[0:1],
        bias_own.reshape(1, 3 * head_cols),
        cosine,
        sine,
    )
    a_blocks = gather_chips(attended, seq_count)

    mlp_pick = jnp.minimum(seq_index // 2, 2).reshape(1)
    attn_pick = jnp.minimum(seq_index // 2, 3).reshape(1)
    mlp_pick, attn_pick, attended = lax.optimization_barrier((mlp_pick, attn_pick, attended))
    squares = sums_of_squares(mlp_pick, attn_master, mlp_master)
    wide_near, squares = lax.optimization_barrier((wide_near, squares))
    wide_far, far_places = far_wt(wide_own, wide_near, wt_count)
    mlp_old = picked(mlp_momentum, mlp_pick, seq_count)
    attn_old = picked(attn_momentum, attn_pick, seq_count)
    near_places = [(bits, 0) for bits in range(1 + len(wide_near))]
    wide_w = assemble(
        wt_index,
        [wide_own] + wide_near + wide_far,
        [(bits, first, shard) for bits, first in near_places + far_places],
        width,
    )
    a_blocks, wide_w, squares, mlp_old, attn_old = lax.optimization_barrier(
        (a_blocks, wide_w, squares, mlp_old, attn_old)
    )
    a_same, a_other = both_cores(a_blocks, seq_count)

    normed_two, d_gate, d_up, hidden, d_mine, d_other, resid_own, gain_part_two = middle(
        place, a_same, a_other, x_low, dy_low, wide_w, vectors[1:2]
    )

    control = jnp.stack([jnp.zeros_like(seq_index), seq_index, wt_index])
    mlp_part = mlp_grads(normed_two, dy_low, d_gate, d_up, hidden, wt_count, [])
    mlp_share = lax.psum_scatter(mlp_part, "wt", scatter_dimension=0, tiled=True)
    got = swap(d_other, "seq", 1, seq_count)
    own, *sends = pair_sums(d_mine, got, 1, False, [mlp_part])
    arrived = send_chips(sends, seq_count)
    pair, d_resid = post(
        own, arrived, resid_own, cotangent[0], vectors[1:2], wide_w, seq_count, []
    )
    pair = lax.all_to_all(pair, "seq", split_axis=0, concat_axis=0)
    pair, mlp_share = lax.optimization_barrier((pair, mlp_share))
    mlp_share = lax.all_gather(mlp_share, "seq", axis=0)

    args = (query, key, value, log_total, pair, normed_one, a_same, a_other, cosine, sine)
    args += (qkv_w, vectors[0:1], gain_part_two, squares)
    d_qkv, attn_part = back(doc_bounds, control, args, wt_count)

    def control_of(owners):
        active = functools.reduce(jnp.logical_or, [seq_index == owner for owner in owners])
        return jnp.stack([active.astype(jnp.int32), seq_index, wt_index])

    attn_share = sum_wt(attn_part, wt_count)
    squares = jnp.sum(attn_share[4 * shard + 5 : 4 * shard + 7, :7], axis=0)
    attn_share = attn_share.astype(bf16)
    attn_share = lax.all_gather(attn_share, "seq", axis=0)

    mine, other = late_sums(
        place, hidden, wide_w[:, width + 2 * ff_pad :], d_qkv, qkv_w, seq_count
    )
    late, *sends = pair_sums(mine, swap(other, "seq", 1, seq_count), 1, False, [])

    mlp_block = new_block(mlp_share, mlp_old, mlp_pick, [late])
    mlp_near = near_owned(mlp_block, MLP_OWNERS, wt_count)
    mlp_grad, mlp_mom = finish(mlp_share, mlp_momentum, [mlp_block])
    mlp_near, done = lax.optimization_barrier((mlp_near, mlp_grad[0, :8, :128]))
    mlp_pieces, mlp_places = gather_owned(mlp_block, mlp_near, MLP_OWNERS, wt_count)
    sends, attn_share = lax.optimization_barrier((sends, attn_share))
    late_arrived = send_chips(sends, seq_count)
    attn_block = new_block(attn_share, attn_old, attn_pick, [])
    attn_near = near_owned(attn_block, ATTN_OWNERS, wt_count)
    attn_near, mlp_pieces = lax.optimization_barrier((attn_near, mlp_pieces))
    attn_pieces, attn_places = gather_owned(attn_block, attn_near, ATTN_OWNERS, wt_count)
    mlp_blocks = orthogonalize(
        control_of(MLP_OWNERS), mlp_pieces, mlp_places, wt_count, [done, *attn_pieces[1:]]
    )
    attn_blocks = orthogonalize(
        control_of(ATTN_OWNERS), attn_pieces, attn_places, wt_count, [mlp_blocks[0]]
    )
    mlp_blocks, attn_blocks, late_arrived = lax.optimization_barrier(
        (mlp_blocks, attn_blocks, late_arrived)
    )
    attn_grad, attn_mom = finish(attn_share, attn_momentum, attn_blocks[:1])

    attn_rate = matrix_rate * math.sqrt(width) * jnp.sqrt(squares[:4] / (width * width))
    mlp_rate = matrix_rate * math.sqrt(ff) * jnp.sqrt(squares[4:] / (width * ff))
    core = seq_index % 2
    mlp_arrived = spread_chips(mlp_blocks, MLP_OWNERS, seq_count)
    attn_arrived = spread_chips(attn_blocks, ATTN_OWNERS, seq_count)
    mlp_other = spread_cores(mlp_arrived, core, seq_count)
    attn_other = spread_cores(attn_arrived, core, seq_count)
    mlp_new = update(control, mlp_rate, mlp_own, mlp_arrived, mlp_other, MLP_OWNERS)
    attn_new = update(control, attn_rate, attn_own, attn_arrived, attn_other, ATTN_OWNERS)
    total = late[0]
    for value in late_arrived:
        total = total + value[0].astype(f32)
    layer_out = (resid_own + total[0]).astype(bf16)
    x_own = tokens[0].astype(f32)
    inverse_own = lax.rsqrt(jnp.mean(x_own * x_own, axis=-1, keepdims=True) + norm_eps)
    d_input_norm = norm_backward(total[1], x_own, inverse_own, vectors[0])
    tokens_grad = d_resid + d_input_norm

    small = jnp.sum(attn_share[:, 4 * shard :].astype(f32), axis=0).reshape(2, 8, 128)
    small = jnp.moveaxis(small[: shard // 128], 0, 1).reshape(8, shard)
    gain_grad = small[:2]
    bias_grad = small[2:5]
    gain_new, gain_second_new = adam_update(gains, gain_grad, gain_first, gain_second)
    bias_new, bias_second_new = adam_update(qkv_bias, bias_grad, bias_first, bias_second)
    return (
        layer_out[None],
        tokens_grad[None],
        attn_grad,
        mlp_grad,
        attn_mom,
        mlp_mom,
        attn_new,
        mlp_new,
        gain_grad,
        gain_second_new,
        gain_new,
        bias_grad,
        bias_second_new,
        bias_new,
    )


def solution(mesh):
    return jax.shard_map(
        per_device,
        mesh=mesh,
        in_specs=(
            P("wt", "seq", None),
            P("wt", "seq", None),
            P("wt", None),
            P(None, "wt", None),
            P(None, "wt", None),
            P(None, "wt", None),
            P(None, "wt", None),
            P(None, "wt"),
            P(None, "wt"),
            P(None, "wt"),
            P(None, "wt"),
            P(None, "wt"),
            P(None, "wt"),
        ),
        out_specs=(
            P("wt", "seq", None),
            P("wt", "seq", None),
            P(None, "wt", None),
            P(None, "wt", None),
            P(None, "wt", None),
            P(None, "wt", None),
            P(None, "wt", "seq"),
            P(None, "wt", "seq"),
            P(None, "wt"),
            P(None, "wt"),
            P(None, "wt"),
            P(None, "wt"),
            P(None, "wt"),
            P(None, "wt"),
        ),
        check_vma=False,
    )
```

```python
import functools
import math

import jax
import jax.numpy as jnp
from jax import lax
from jax.experimental import pallas as pl
from jax.experimental.pallas import tpu as pltpu
from jax.sharding import PartitionSpec as P

HEAD_DIM = 64
NS_STEPS = 5
STEP = 10

norm_eps = 1e-06
rope_base = 1000000.0
coef_a = 3.4445
coef_b = -4.775
coef_c = 2.0315
momentum_decay = 0.95
matrix_rate = 0.5
decay_rate = 0.01
first_decay = 0.9
second_decay = 0.95
vector_rate = 0.25
adam_eps = 1e-08
ortho_eps = 1e-07
masked_score = -1e30
tile = 256
vmem_limit = 62 * 2**20

MLP_OWNERS = (0, 2, 4)
ATTN_OWNERS = (1, 3, 5, 6)

f32 = jnp.float32
bf16 = jnp.bfloat16


def dot32(a, b, ca, cb):
    return lax.dot_general(a, b, (((ca,), (cb,)), ((), ())), preferred_element_type=f32)


def doc_layout(bounds, length):
    places = jnp.arange(length, dtype=jnp.int32)
    first_bound = bounds[0]
    second_bound = bounds[1]
    doc_index = (places >= first_bound).astype(jnp.int32) + (places >= second_bound).astype(
        jnp.int32
    )
    doc_start = jnp.where(
        places < first_bound, 0, jnp.where(places < second_bound, first_bound, second_bound)
    )
    return (doc_index, (places - doc_start).astype(f32))


def rope_tables(position, cols):
    half_dim = HEAD_DIM // 2
    lane = jnp.arange(cols, dtype=jnp.int32) % HEAD_DIM
    frequency = rope_base ** (-2.0 * jnp.arange(half_dim, dtype=f32) / HEAD_DIM)
    angles = position[:, None] * frequency[None, :]
    repeat = cols // half_dim
    cosine = jnp.concatenate([jnp.cos(angles)] * repeat, 1)
    sine = jnp.concatenate([jnp.sin(angles)] * repeat, 1)
    return cosine, jnp.where(lane < half_dim, -1.0, 1.0)[None, :] * sine


def swap_halves(values):
    half_dim = HEAD_DIM // 2
    parts = []
    for first in range(0, values.shape[1], HEAD_DIM):
        parts.append(values[:, first + half_dim : first + HEAD_DIM])
        parts.append(values[:, first : first + half_dim])
    return jnp.concatenate(parts, axis=1)


def visible(bounds_ref, first, rows, length):
    query = first + lax.broadcasted_iota(jnp.int32, (rows, length), 0)
    key = lax.broadcasted_iota(jnp.int32, (rows, length), 1)
    one, two = bounds_ref[0, 0], bounds_ref[0, 1]
    start = jnp.where(query < one, 0, jnp.where(query < two, one, two))
    return (key <= query) & (key >= start)


def slot_of(chips, value):
    slot, bits = 0, chips
    while bits > 1:
        slot = slot * 2 + (value & 1)
        value = value >> 1
        bits //= 2
    return slot


def front_kernel(
    bounds_ref,
    place_ref,
    same_ref,
    other_ref,
    weight_ref,
    gain_ref,
    bias_ref,
    cosine_ref,
    sine_ref,
    x_ref,
    normed_ref,
    query_ref,
    key_ref,
    value_ref,
    attended_ref,
    log_ref,
):
    length = x_ref.shape[0]
    cols = query_ref.shape[1]
    chips, rows, _ = same_ref.shape
    for chip in range(chips):
        at = pl.ds(chip * 2 * rows, 2 * rows)
        slot = slot_of(chips, place_ref[0] ^ chip)
        low = pl.ds(chip * 2 * rows + place_ref[1] * rows, rows)
        high = pl.ds(chip * 2 * rows + (1 - place_ref[1]) * rows, rows)
        x_ref[low, :] = same_ref[slot]
        x_ref[high, :] = other_ref[slot]
        x = x_ref[at, :].astype(f32)
        inverse = lax.rsqrt(jnp.mean(x * x, axis=-1, keepdims=True) + norm_eps)
        normed = (x * inverse * gain_ref[...]).astype(bf16)
        normed_ref[at, :] = normed
        projected = (dot32(normed, weight_ref[...], 1, 0) + bias_ref[...]).astype(bf16).astype(f32)
        cosine, sine = cosine_ref[at, :], sine_ref[at, :]
        query = projected[:, :cols]
        key = projected[:, cols : 2 * cols]
        query_ref[at, :] = (query * cosine + swap_halves(query) * sine).astype(bf16)
        key_ref[at, :] = (key * cosine + swap_halves(key) * sine).astype(bf16)
        value_ref[at, :] = projected[:, 2 * cols :].astype(bf16)
    for first in range(0, length, tile):
        at, keys = pl.ds(first, tile), pl.ds(0, first + tile)
        allowed = visible(bounds_ref, first, tile, first + tile)
        attended = []
        for head in range(cols // HEAD_DIM):
            lanes = pl.ds(head * HEAD_DIM, HEAD_DIM)
            scores = dot32(query_ref[at, lanes], key_ref[keys, lanes], 1, 1)
            scores = jnp.where(allowed, scores * HEAD_DIM ** (-0.5), masked_score)
            peak = jnp.max(scores, axis=-1, keepdims=True)
            exponent = jnp.exp(scores - peak)
            total = jnp.sum(exponent, axis=-1, keepdims=True)
            weights = (exponent * (1.0 / total)).astype(bf16)
            attended.append(dot32(weights, value_ref[keys, lanes], 1, 0))
            log_ref[at, pl.ds(head, 1)] = peak + jnp.log(total)
        attended_ref[at, :] = jnp.concatenate(attended, axis=1).astype(bf16)


def vmem_specs(count):
    return [pl.BlockSpec(memory_space=pltpu.VMEM)] * count


def whole_spec(shape):
    return pl.BlockSpec(shape, lambda i: (0,) * len(shape))


def whole_specs(arrays):
    return [whole_spec(value.shape) for value in arrays]


def any_specs(count):
    return [pl.BlockSpec(memory_space=pl.ANY)] * count


def smem_spec():
    return pl.BlockSpec(memory_space=pltpu.SMEM)


def front(bounds, place, same, other, weight, gain, bias, cosine, sine):
    chips, rows, width = same.shape
    length, cols = cosine.shape
    part = jax.ShapeDtypeStruct((length, cols), bf16)
    shapes = [
        jax.ShapeDtypeStruct((length, width), bf16),
        jax.ShapeDtypeStruct((length, width), bf16),
        part,
        part,
        part,
        part,
        jax.ShapeDtypeStruct((length, cols // HEAD_DIM), f32),
    ]
    args = (same, other, weight, gain, bias, cosine, sine)
    return pl.pallas_call(
        front_kernel,
        grid=(1,),
        in_specs=[smem_spec()] * 2 + whole_specs(args),
        out_specs=whole_specs(shapes),
        out_shape=shapes,
        compiler_params=pltpu.CompilerParams(vmem_limit_bytes=vmem_limit),
        cost_estimate=pl.CostEstimate(
            flops=8 * 10**9, bytes_accessed=8 * 10**6, transcendentals=2 * 10**6
        ),
        name="front",
    )(bounds, place, *args)


def store_split(place_ref, mine_ref, other_ref, index, value):
    rows = value.shape[0] // 2
    core = place_ref[1]
    top, low = value[:rows], value[rows:]
    mine_ref[0, index] = jnp.where(core == 0, top, low)
    other_ref[0, index] = jnp.where(core == 0, low, top).astype(bf16)


def split_out(chips, sums, rows, width):
    spec = pl.BlockSpec(
        (1, sums, rows, width), lambda i, place: (slot_of(chips, i ^ place[0]), 0, 0, 0)
    )
    shape = (chips, sums, rows, width)
    return [spec, spec], [jax.ShapeDtypeStruct(shape, f32), jax.ShapeDtypeStruct(shape, bf16)]


def middle_kernel(
    place_ref,
    same_ref,
    other_ref,
    x_ref,
    dy_ref,
    weight_ref,
    gain_ref,
    normed_ref,
    d_gate_ref,
    d_up_ref,
    hidden_ref,
    d_mine_ref,
    d_other_ref,
    resid_ref,
    gain_part_ref,
):
    width = x_ref.shape[1]
    cols = d_gate_ref.shape[1]
    rows = resid_ref.shape[0]
    gate_w = weight_ref.at[:, pl.ds(width, cols)]
    up_w = weight_ref.at[:, pl.ds(width + cols, cols)]
    down_w = weight_ref.at[:, pl.ds(width + 2 * cols, cols)]
    attended = []
    for chip in range(same_ref.shape[0]):
        slot = slot_of(same_ref.shape[0], place_ref[0] ^ chip)
        same, other = same_ref[slot], other_ref[slot]
        attended.append(jnp.where(place_ref[1] == 0, same, other))
        attended.append(jnp.where(place_ref[1] == 0, other, same))
    attended = jnp.concatenate(attended, axis=1)
    resid = x_ref[...].astype(f32) + dot32(attended, weight_ref[:, pl.ds(0, width)], 1, 0)

    @pl.when(pl.program_id(0) == place_ref[0])
    def _():
        resid_ref[...] = jnp.where(place_ref[1] == 0, resid[:rows], resid[rows:])

    inverse = lax.rsqrt(jnp.mean(resid * resid, axis=-1, keepdims=True) + norm_eps)
    normed = (resid * inverse * gain_ref[...]).astype(bf16)
    normed_ref[...] = normed
    gate = dot32(normed, gate_w[...], 1, 0)
    up = dot32(normed, up_w[...], 1, 0)
    d_hidden = dot32(dy_ref[...], down_w[...], 1, 0)
    sigmoid = jax.nn.sigmoid(gate)
    silu = gate * sigmoid
    hidden = (silu * up).astype(bf16)
    hidden_ref[...] = hidden
    d_gate = (d_hidden * up * (sigmoid * (1.0 + gate * (1.0 - sigmoid)))).astype(bf16)
    d_up = (d_hidden * silu).astype(bf16)
    d_gate_ref[...] = d_gate
    d_up_ref[...] = d_up
    d_normed = dot32(d_gate, gate_w[...], 1, 1) + dot32(d_up, up_w[...], 1, 1)
    store_split(place_ref, d_mine_ref, d_other_ref, 0, d_normed)

    @pl.when(pl.program_id(0) == 0)
    def _():
        gain_part_ref[...] = jnp.zeros_like(gain_part_ref)

    gain_part_ref[...] += jnp.sum(d_normed * resid * inverse, axis=0, keepdims=True)


def middle(place, same, other, x, dy, weight, gain):
    chips, length, head_cols = same.shape
    count = 2 * chips
    width = x.shape[1]
    cols = (weight.shape[1] - width) // 3
    half = length // count
    rows = 2 * half

    def block(size):
        return pl.BlockSpec((rows, size), lambda i, place: (i, 0))

    def whole(shape):
        return pl.BlockSpec(shape, lambda i, place: (0,) * len(shape))

    split_specs, split_shapes = split_out(chips, 1, half, width)
    wide = jax.ShapeDtypeStruct((length, cols), bf16)
    return pl.pallas_call(
        middle_kernel,
        grid_spec=pltpu.PrefetchScalarGridSpec(
            num_scalar_prefetch=1,
            grid=(chips,),
            in_specs=[
                pl.BlockSpec((chips, rows, head_cols), lambda i, place: (0, i, 0)),
                pl.BlockSpec((chips, rows, head_cols), lambda i, place: (0, i, 0)),
                block(width),
                block(width),
                whole(weight.shape),
                whole(gain.shape),
            ],
            out_specs=[
                block(width),
                block(cols),
                block(cols),
                block(cols),
                *split_specs,
                whole((half, width)),
                whole((1, width)),
            ],
        ),
        out_shape=[
            jax.ShapeDtypeStruct((length, width), bf16),
            wide,
            wide,
            wide,
            *split_shapes,
            jax.ShapeDtypeStruct((half, width), f32),
            jax.ShapeDtypeStruct((1, width), f32),
        ],
        compiler_params=pltpu.CompilerParams(vmem_limit_bytes=vmem_limit),
        cost_estimate=pl.CostEstimate(
            flops=10 * 10**9, bytes_accessed=20 * 10**6, transcendentals=10**6
        ),
        name="middle",
    )(place, same, other, x, dy, weight, gain)


def pair_kernel(kept, extra, mine_ref, got_ref, *refs):
    keep_ref, sends = refs[extra], refs[extra + 1 :]
    for slot in range(kept):
        keep_ref[slot] = mine_ref[slot] + got_ref[slot].astype(f32)
    for slot in range(kept, mine_ref.shape[0]):
        value = (mine_ref[slot] + got_ref[slot].astype(f32)).astype(bf16)
        if len(sends) == 1:
            sends[0][slot - kept] = value
        else:
            sends[slot - kept][0] = value


def pair_sums(mine, got, kept, together, after):
    slots, sums, rows, width = mine.shape
    step = 32

    def spec(count):
        return pl.BlockSpec((count, sums, step, width), lambda i: (0, 0, i, 0))

    counts = [slots - kept] if together else [1] * (slots - kept)
    return pl.pallas_call(
        functools.partial(pair_kernel, kept, len(after)),
        grid=(rows // step,),
        in_specs=[spec(slots)] * 2 + any_specs(len(after)),
        out_specs=[spec(kept)] + [spec(count) for count in counts],
        out_shape=[jax.ShapeDtypeStruct((kept, sums, rows, width), f32)]
        + [jax.ShapeDtypeStruct((count, sums, rows, width), bf16) for count in counts],
        compiler_params=pltpu.CompilerParams(vmem_limit_bytes=vmem_limit),
        name="pair_sums",
    )(mine, got, *after)


def post_kernel(extra, own_ref, resid_ref, dy_ref, gain_ref, weight_ref, *refs):
    arrived, (pair_ref, d_resid_ref) = refs[: -2 - extra], refs[-2:]
    d_normed = own_ref[0, 0]
    for ref in arrived:
        d_normed = d_normed + ref[0, 0].astype(f32)
    resid = resid_ref[...]
    inverse = lax.rsqrt(jnp.mean(resid * resid, axis=-1, keepdims=True) + norm_eps)
    scaled = d_normed * gain_ref[...]
    d_resid = (
        dy_ref[...].astype(f32)
        + inverse * scaled
        - resid * (inverse * inverse * inverse) * jnp.mean(scaled * resid, axis=-1, keepdims=True)
    )
    d_resid_ref[...] = d_resid
    low = d_resid.astype(bf16)
    d_attn = dot32(low, weight_ref[...], 1, 1).astype(bf16)
    cols = pair_ref.shape[3]
    for part in range(pair_ref.shape[0]):
        pair_ref[part, 0] = d_attn[:, part * cols : (part + 1) * cols]
        pair_ref[part, 1] = low[:, part * cols : (part + 1) * cols]


def post(own, arrived, resid, dy, gain, weight, count, after):
    rows, width = resid.shape
    cols = width // count

    def whole(shape):
        return pl.BlockSpec(shape, lambda i: (0,) * len(shape))

    return pl.pallas_call(
        functools.partial(post_kernel, len(after)),
        grid=(1,),
        in_specs=[whole(own.shape), whole(resid.shape), whole(dy.shape), whole(gain.shape)]
        + [whole((width, width))]
        + [whole(value.shape) for value in arrived]
        + any_specs(len(after)),
        out_specs=[whole((count, 2, rows, cols)), whole((rows, width))],
        out_shape=[
            jax.ShapeDtypeStruct((count, 2, rows, cols), bf16),
            jax.ShapeDtypeStruct((rows, width), f32),
        ],
        compiler_params=pltpu.CompilerParams(vmem_limit_bytes=vmem_limit),
        name="post",
    )(own, resid, dy, gain, weight, *arrived, *after)


def mlp_grads_kernel(
    parts, extra, normed_ref, dy_ref, d_gate_ref, d_up_ref, hidden_ref, *refs
):
    out_ref = refs[extra]
    shard = out_ref.shape[0] // (3 * parts)
    for part in range(parts):
        at = pl.ds(part * shard, shard)
        normed = normed_ref[:, at]
        pairs = [(normed, d_gate_ref), (normed, d_up_ref), (dy_ref[:, at], hidden_ref)]
        for index, (left, right_ref) in enumerate(pairs):
            out_ref[pl.ds((3 * part + index) * shard, shard), :] = dot32(
                left, right_ref[...], 0, 0
            ).astype(bf16)


def mlp_grads(normed, dy, d_gate, d_up, hidden, parts, after):
    width = normed.shape[1]
    args = (normed, dy, d_gate, d_up, hidden)
    shape = jax.ShapeDtypeStruct((3 * width, hidden.shape[1]), bf16)
    return pl.pallas_call(
        functools.partial(mlp_grads_kernel, parts, len(after)),
        grid=(1,),
        in_specs=whole_specs(args) + any_specs(len(after)),
        out_specs=whole_spec(shape.shape),
        out_shape=shape,
        compiler_params=pltpu.CompilerParams(vmem_limit_bytes=vmem_limit),
        cost_estimate=pl.CostEstimate(
            flops=3 * 10**9, bytes_accessed=9 * 10**6, transcendentals=0
        ),
        name="mlp_grads",
    )(*args, *after)


def back_kernel(
    parts,
    bounds_ref,
    control_ref,
    query_ref,
    key_ref,
    value_ref,
    log_ref,
    arrived_ref,
    normed_ref,
    same_ref,
    other_ref,
    cosine_ref,
    sine_ref,
    weight_ref,
    gain_ref,
    gain_two_ref,
    squares_ref,
    d_qkv_ref,
    *refs,
):
    grads_refs, (d_key_ref, d_value_ref, d_attn_ref, d_resid_ref) = refs[:parts], refs[parts:]
    length, cols = query_ref.shape
    count, _, rows, _ = arrived_ref.shape
    scale = HEAD_DIM ** (-0.5)
    for part in range(count):
        d_attn_ref[pl.ds(part * rows, rows), :] = arrived_ref[part, 0]
        d_resid_ref[pl.ds(part * rows, rows), :] = arrived_ref[part, 1]
    d_key_ref[...] = jnp.zeros_like(d_key_ref)
    d_value_ref[...] = jnp.zeros_like(d_value_ref)

    def undo(values, at):
        return values * cosine_ref[at, :] - swap_halves(values) * sine_ref[at, :]

    for first in range(0, length, tile):
        at, keys = pl.ds(first, tile), pl.ds(0, first + tile)
        allowed = visible(bounds_ref, first, tile, first + tile)
        d_query, d_key, d_value = [], [], []
        for head in range(cols // HEAD_DIM):
            lanes = pl.ds(head * HEAD_DIM, HEAD_DIM)
            query, d_out = query_ref[at, lanes], d_attn_ref[at, lanes]
            key, value = key_ref[keys, lanes], value_ref[keys, lanes]
            scores = jnp.where(allowed, dot32(query, key, 1, 1) * scale, masked_score)
            weights = jnp.exp(scores - log_ref[at, pl.ds(head, 1)])
            d_value.append(dot32(weights.astype(bf16), d_out, 0, 0))
            d_weights = dot32(d_out, value, 1, 1)
            inner = jnp.sum(weights * d_weights, axis=-1, keepdims=True)
            d_scores = (weights * (d_weights - inner)).astype(bf16)
            d_query.append(dot32(d_scores, key, 1, 0) * scale)
            d_key.append(dot32(d_scores, query, 0, 0) * scale)
        d_key_ref[keys, :] += jnp.concatenate(d_key, axis=1)
        d_value_ref[keys, :] += jnp.concatenate(d_value, axis=1)
        d_qkv_ref[at, pl.ds(0, cols)] = undo(jnp.concatenate(d_query, axis=1), at).astype(bf16)
    for first in range(0, length, tile):
        at = pl.ds(first, tile)
        d_qkv_ref[at, pl.ds(cols, cols)] = undo(d_key_ref[at, :], at).astype(bf16)
        d_qkv_ref[at, pl.ds(2 * cols, cols)] = d_value_ref[at, :].astype(bf16)
    shard = gain_ref.shape[1] // parts
    pad = grads_refs[0].shape[1]
    pieces = shard // cols
    bias = jnp.sum(d_qkv_ref[...].astype(f32), axis=0, keepdims=True)
    lane = lax.broadcasted_iota(jnp.int32, squares_ref.shape, 1)
    row = lax.broadcasted_iota(jnp.int32, squares_ref.shape, 0)
    squares = jnp.sum(jnp.where(lane == row, squares_ref[...], 0.0), axis=0, keepdims=True)
    squares_high = squares.astype(bf16).astype(f32)
    rest = jnp.zeros((1, shard - squares.shape[1]), f32)

    def wide(value):
        return value if shard == 128 else jnp.concatenate([value, rest], axis=1)

    for part in range(parts):
        block = control_ref[2] ^ part
        grads_ref = grads_refs[part]
        at = pl.ds(pl.multiple_of(block * shard, 128), shard)
        grads = dot32(normed_ref[:, at], d_qkv_ref[...], 0, 0)
        gain_one = lax.dot_general(
            jnp.ones((8, 3 * cols), f32),
            grads * weight_ref[at, :].astype(f32),
            (((1,), (1,)), ((), ())),
            precision=lax.Precision.HIGHEST,
            preferred_element_type=f32,
        )[0:1]
        grads = grads.astype(bf16)
        for index in range(3):
            grads_ref[pl.ds(index * shard, shard), pl.ds(0, cols)] = grads[
                :, index * cols : (index + 1) * cols
            ]
        for piece in range(pieces):
            place = block * pieces + piece
            slot = slot_of(same_ref.shape[0], (place >> 1) ^ (control_ref[1] >> 1))
            near = ((place ^ control_ref[1]) & 1) == 0
            attended = jnp.where(near, same_ref[slot], other_ref[slot])
            grads_ref[pl.ds(3 * shard + piece * cols, cols), pl.ds(0, cols)] = dot32(
                attended, d_resid_ref[...], 0, 0
            ).astype(bf16)
        if pad > cols:
            grads_ref[pl.ds(0, 4 * shard), pl.ds(cols, pad - cols)] = jnp.zeros(
                (4 * shard, pad - cols), bf16
            )
        small = [gain_one / gain_ref[:, at], gain_two_ref[:, at]]
        for index in range(3):
            own = bias[:, index * cols : (index + 1) * cols]
            small.append(
                jnp.concatenate(
                    [
                        jnp.where(block * pieces + piece == control_ref[1], own, 0.0)
                        for piece in range(pieces)
                    ],
                    axis=1,
                )
            )
        small += [wide(squares_high), wide(squares - squares_high), jnp.zeros((1, shard), f32)]
        small = jnp.concatenate(small, axis=0)
        small = [small[:, first : first + 128] for first in range(0, shard, 128)]
        small += [jnp.zeros((8, 128), f32)] * (2 - len(small))
        grads_ref[pl.ds(4 * shard, 16), :] = jnp.concatenate(small, axis=0).astype(bf16)


def back(bounds, control, args, parts):
    query, normed = args[0], args[5]
    length, cols = query.shape
    width = normed.shape[1]
    pad = -(-cols // 128) * 128
    shapes = [jax.ShapeDtypeStruct((length, 3 * cols), bf16)]
    shapes += [jax.ShapeDtypeStruct((4 * width // parts + 16, pad), bf16)] * parts
    results = pl.pallas_call(
        functools.partial(back_kernel, parts),
        grid=(1,),
        in_specs=[smem_spec()] * 2 + whole_specs(args),
        out_specs=whole_specs(shapes),
        out_shape=shapes,
        scratch_shapes=[
            pltpu.VMEM((length, cols), f32),
            pltpu.VMEM((length, cols), f32),
            pltpu.VMEM((length, cols), bf16),
            pltpu.VMEM((length, cols), bf16),
        ],
        compiler_params=pltpu.CompilerParams(vmem_limit_bytes=vmem_limit),
        cost_estimate=pl.CostEstimate(
            flops=10 * 10**9, bytes_accessed=8 * 10**6, transcendentals=2 * 10**6
        ),
        name="back",
    )(bounds, control, *args)
    return results[0], results[1:]


def late_kernel(place_ref, hidden_ref, down_ref, d_qkv_ref, weight_ref, mine_ref, other_ref):
    store_split(place_ref, mine_ref, other_ref, 0, dot32(hidden_ref[...], down_ref[...], 1, 1))
    store_split(place_ref, mine_ref, other_ref, 1, dot32(d_qkv_ref[...], weight_ref[...], 1, 1))


def late_sums(place, hidden, down, d_qkv, weight, count):
    length, cols = d_qkv.shape
    width = weight.shape[0]
    chips = count // 2
    half = length // count
    rows = 2 * half

    def block(size):
        return pl.BlockSpec((rows, size), lambda i, place: (i, 0))

    def whole(shape):
        return pl.BlockSpec(shape, lambda i, place: (0, 0))

    split_specs, split_shapes = split_out(chips, 2, half, width)
    return pl.pallas_call(
        late_kernel,
        grid_spec=pltpu.PrefetchScalarGridSpec(
            num_scalar_prefetch=1,
            grid=(chips,),
            in_specs=[
                block(hidden.shape[1]),
                whole(down.shape),
                block(cols),
                whole(weight.shape),
            ],
            out_specs=split_specs,
        ),
        out_shape=split_shapes,
        compiler_params=pltpu.CompilerParams(vmem_limit_bytes=vmem_limit),
        cost_estimate=pl.CostEstimate(
            flops=2 * 10**9, bytes_accessed=16 * 10**6, transcendentals=0
        ),
        name="late_sums",
    )(place, hidden, down, d_qkv, weight)


def picked_kernel(pick_ref, momentum_ref, out_ref):
    count, rows, pad = out_ref.shape
    cols = momentum_ref.shape[2] // count
    for turn in range(count):
        value = momentum_ref[0, :, pl.ds(turn * cols, cols)] * momentum_decay
        out_ref[turn, :, pl.ds(0, cols)] = value
        if pad > cols:
            out_ref[turn, :, pl.ds(cols, pad - cols)] = jnp.zeros((rows, pad - cols), f32)


def picked(momentum, pick, count):
    rows, width = momentum.shape[1:]
    pad = -(-(width // count) // 128) * 128
    step = min(64, rows)
    return pl.pallas_call(
        picked_kernel,
        grid_spec=pltpu.PrefetchScalarGridSpec(
            num_scalar_prefetch=1,
            grid=(rows // step,),
            in_specs=[pl.BlockSpec((1, step, width), lambda i, pick: (pick[0], i, 0))],
            out_specs=pl.BlockSpec((count, step, pad), lambda i, pick: (0, i, 0)),
        ),
        out_shape=jax.ShapeDtypeStruct((count, rows, pad), f32),
        compiler_params=pltpu.CompilerParams(vmem_limit_bytes=vmem_limit),
        cost_estimate=pl.CostEstimate(
            flops=rows * width, bytes_accessed=8 * rows * width, transcendentals=0
        ),
        name="picked",
    )(pick, momentum)


def squares_kernel(order_ref, attn_ref, mlp_ref, out_ref):
    @pl.when(pl.program_id(0) == 0)
    def _():
        out_ref[...] = jnp.zeros_like(out_ref)

    at = 0
    for ref in (attn_ref, mlp_ref):
        for index in range(ref.shape[0]):
            value = ref[index].astype(bf16).astype(f32)
            total = jnp.sum(jnp.sum(value * value, axis=0, keepdims=True), axis=1, keepdims=True)
            out_ref[pl.ds(at, 1), :] += jnp.broadcast_to(total, (1, out_ref.shape[1]))
            at += 1


def block_kernel(extra, pick_ref, share_ref, old_ref, *refs):
    refs[extra][...] = (old_ref[...] + share_ref[...].astype(f32)).astype(bf16)


def new_block(share, old, pick, after):
    count, shard, pad = old.shape
    step = 2
    return pl.pallas_call(
        functools.partial(block_kernel, len(after)),
        grid_spec=pltpu.PrefetchScalarGridSpec(
            num_scalar_prefetch=1,
            grid=(count // step,),
            in_specs=[
                pl.BlockSpec((step, shard, pad), lambda i, pick: (i, pick[0], 0)),
                pl.BlockSpec((step, shard, pad), lambda i, pick: (i, 0, 0)),
            ]
            + any_specs(len(after)),
            out_specs=pl.BlockSpec((step, shard, pad), lambda i, pick: (i, 0, 0)),
        ),
        out_shape=jax.ShapeDtypeStruct(old.shape, bf16),
        compiler_params=pltpu.CompilerParams(vmem_limit_bytes=vmem_limit),
        cost_estimate=pl.CostEstimate(
            flops=old.size, bytes_accessed=8 * old.size, transcendentals=0
        ),
        name="new_block",
    )(pick, share, old, *after)


def sums_of_squares(order, attn, mlp):
    rows = attn.shape[1]
    step = min(64, rows)
    return pl.pallas_call(
        squares_kernel,
        grid=(rows // step,),
        in_specs=[
            smem_spec(),
            pl.BlockSpec((attn.shape[0], step, attn.shape[2]), lambda i: (0, i, 0)),
            pl.BlockSpec((mlp.shape[0], step, mlp.shape[2]), lambda i: (0, i, 0)),
        ],
        out_specs=pl.BlockSpec((8, 128), lambda i: (0, 0)),
        out_shape=jax.ShapeDtypeStruct((8, 128), f32),
        compiler_params=pltpu.CompilerParams(vmem_limit_bytes=vmem_limit),
        cost_estimate=pl.CostEstimate(
            flops=2 * (attn.size + mlp.size),
            bytes_accessed=4 * (attn.size + mlp.size),
            transcendentals=0,
        ),
        name="sums_of_squares",
    )(order, attn, mlp)


def pack_kernel(place_ref, master_ref, vectors_ref, *refs):
    out_ref = refs[-1]
    shard = master_ref.shape[1]
    cols = out_ref.shape[1] // 3
    for index in range(3):
        value = master_ref[index].astype(bf16)
        part = value[:, :cols]
        for at in range(1, value.shape[1] // cols):
            part = jnp.where(place_ref[1] == at, value[:, at * cols : (at + 1) * cols], part)
        out_ref[pl.ds(0, shard), pl.ds(index * cols, cols)] = part
    out_ref[pl.ds(shard, 16), :] = vectors_ref[...].astype(bf16)


def pack(seq_index, master, vectors, cols, after):
    shard = master.shape[1]
    lanes = max(cols, 128)
    place = jnp.stack([seq_index // (lanes // cols), seq_index % (lanes // cols)])
    shape = (shard + 16, 3 * cols)
    return pl.pallas_call(
        pack_kernel,
        grid_spec=pltpu.PrefetchScalarGridSpec(
            num_scalar_prefetch=1,
            grid=(1,),
            in_specs=[
                pl.BlockSpec((3, shard, lanes), lambda i, place: (0, 0, place[0])),
                pl.BlockSpec(vectors.shape, lambda i, place: (0, 0)),
            ]
            + any_specs(len(after)),
            out_specs=pl.BlockSpec(shape, lambda i, place: (0, 0)),
        ),
        out_shape=jax.ShapeDtypeStruct(shape, bf16),
        compiler_params=pltpu.CompilerParams(vmem_limit_bytes=vmem_limit),
        name="pack",
    )(place, master, vectors, *after)


def assemble_kernel(places, wt_ref, *refs):
    pieces, out_ref, arrived = refs[: len(places)], refs[-2], refs[-1]
    copies = []
    for at, (bits, first, rows) in enumerate(places):
        start = pl.multiple_of((wt_ref[0] ^ bits) * rows + first, 16)
        target = out_ref.at[pl.ds(start, pieces[at].shape[0]), :]
        copies.append(pltpu.make_async_copy(pieces[at], target, arrived.at[at]))
    for copy in copies:
        copy.start()
    for copy in copies:
        copy.wait()


def assemble(wt_index, pieces, places, rows):
    size = rows * pieces[0].shape[1]
    return pl.pallas_call(
        functools.partial(assemble_kernel, places),
        in_specs=[smem_spec()] + any_specs(len(pieces)),
        out_specs=vmem_specs(1)[0],
        out_shape=jax.ShapeDtypeStruct((rows, pieces[0].shape[1]), pieces[0].dtype),
        scratch_shapes=[pltpu.SemaphoreType.DMA((len(pieces),))],
        compiler_params=pltpu.CompilerParams(vmem_limit_bytes=vmem_limit),
        cost_estimate=pl.CostEstimate(flops=0, bytes_accessed=4 * size, transcendentals=0),
        name="assemble",
    )(wt_index.reshape(1), *pieces)


def norm_backward(d_normed, values, inverse, gain_row):
    scaled = d_normed * gain_row
    return inverse * scaled - values * inverse**3 * jnp.mean(
        scaled * values, axis=-1, keepdims=True
    )


def ortho_kernel(places, extra, control_ref, *refs):
    pieces, outs = refs[: len(places)], refs[len(places) + extra : -8]
    whole, gram, prod, gram_low, prod_low, poly_low, rows, arrived = refs[-8:]
    parts, count = arrived.shape
    shard, pad = outs[0].shape[1:]
    width = gram.shape[0]
    tiles = width // tile

    def upper(j):
        return pl.ds(j * tile, tile), pl.ds(j * tile, width - j * tile)

    def mirror(low):
        for j in range(1, tiles):
            for i in range(j):
                here, there = pl.ds(i * tile, tile), pl.ds(j * tile, tile)
                low[there, here] = low[here, there].T

    @pl.when(control_ref[0] == 1)
    def _():
        copies = [[] for _ in range(parts)]
        for (part, first), piece in zip(places, pieces):
            for turn in range(first, first + piece.shape[0]):
                copies[part].append(
                    pltpu.make_async_copy(
                        piece.at[turn - first],
                        whole.at[pl.ds(part * shard, shard), pl.ds(turn * pad, pad)],
                        arrived.at[part, turn],
                    )
                )
        for part in range(parts):
            for copy in copies[part]:
                copy.start()
        for part in range(parts):
            for copy in copies[part]:
                copy.wait()
        diagonal = lax.broadcasted_iota(jnp.int32, (tile, tile), 0) == lax.broadcasted_iota(
            jnp.int32, (tile, tile), 1
        )
        squares = jnp.zeros((1, 1), f32)
        for j in range(tiles):
            up, at = upper(j)
            gram[up, at] = dot32(whole[up, :], whole[at, :], 1, 1)
            entries = jnp.where(diagonal, gram[up, up], 0.0)
            squares = squares + jnp.sum(
                jnp.sum(entries, axis=1, keepdims=True), axis=0, keepdims=True
            )
        inverse = 1.0 / (jnp.sqrt(squares) + ortho_eps)
        for j in range(tiles):
            up, at = upper(j)
            scaled = gram[up, at] * (inverse * inverse)
            gram[up, at] = scaled
            gram_low[up, at] = scaled.astype(bf16)
        mirror(gram_low)

        def step(index, carry):
            poly = poly_low.at[index]
            for j in range(tiles):
                up, at = upper(j)
                poly[up, at] = (
                    coef_b * gram[up, at] + coef_c * dot32(gram_low[up, :], gram_low[:, at], 1, 0)
                ).astype(bf16)
            mirror(poly)
            for j in range(tiles):
                up, at = upper(j)
                value = coef_a * gram[up, at] + dot32(poly[up, :], gram_low[:, at], 1, 0)
                prod[up, at] = value
                prod_low[up, at] = value.astype(bf16)
            mirror(prod_low)
            for j in range(tiles):
                up, at = upper(j)
                value = coef_a * prod[up, at] + dot32(prod_low[up, :], poly[:, at], 1, 0)
                gram[up, at] = value
                gram_low[up, at] = value.astype(bf16)
            mirror(gram_low)
            return carry

        lax.fori_loop(0, NS_STEPS - 1, step, 0)
        unit = lax.broadcasted_iota(jnp.int32, (shard, width), 0) == lax.broadcasted_iota(
            jnp.int32, (shard, width), 1
        )
        rows[...] = (
            coef_a * unit.astype(f32)
            + coef_b * gram[pl.ds(0, shard), :]
            + coef_c * dot32(gram_low[pl.ds(0, shard), :], gram_low[...], 1, 0)
        )

        def apply(index, carry):
            value = rows[...]
            rows[...] = coef_a * value + dot32(
                value.astype(bf16), poly_low[NS_STEPS - 2 - index], 1, 0
            )
            return carry

        lax.fori_loop(0, NS_STEPS - 1, apply, 0)
        scaled = (rows[...] * inverse).astype(bf16)
        for turn in range(count // 2):
            chip = lax.rem((control_ref[1] >> 1) + turn, count // 2)
            for core in range(2):
                lanes = pl.ds(pl.multiple_of((2 * chip + core) * pad, 128), pad)
                outs[turn][core] = dot32(scaled, whole[:, lanes], 1, 0).astype(bf16)


def orthogonalize(control, pieces, places, parts, after):
    count, shard, pad = pieces[0].shape
    width = shard * parts
    return pl.pallas_call(
        functools.partial(ortho_kernel, places, len(after)),
        out_shape=[jax.ShapeDtypeStruct((2, shard, pad), bf16)] * (count // 2),
        in_specs=[smem_spec()] + any_specs(len(pieces) + len(after)),
        out_specs=vmem_specs(count // 2),
        scratch_shapes=[
            pltpu.VMEM((width, count * pad), bf16),
            pltpu.VMEM((width, width), f32),
            pltpu.VMEM((width, width), f32),
            pltpu.VMEM((width, width), bf16),
            pltpu.VMEM((width, width), bf16),
            pltpu.VMEM((NS_STEPS - 1, width, width), bf16),
            pltpu.VMEM((shard, width), f32),
            pltpu.SemaphoreType.DMA((parts, count)),
        ],
        compiler_params=pltpu.CompilerParams(vmem_limit_bytes=vmem_limit),
        cost_estimate=pl.CostEstimate(
            flops=30 * 10**9, bytes_accessed=4 * count * shard * pad, transcendentals=0
        ),
        name="orthogonalize",
    )(control, *pieces, *after)


def update_kernel(owners, flip, extra, control_ref, rate_ref, own_ref, *refs):
    chips = len(refs) - extra - 2
    arrived, other_ref, out_ref = refs[:chips], refs[chips], refs[-1]
    cols = own_ref.shape[1 if flip else 2]
    chip, core = control_ref[1] >> 1, control_ref[1] & 1
    for index, owner in enumerate(owners):
        turn = lax.rem(chip - owner // 2 + chips, chips)
        for at in range(chips):

            @pl.when(turn == at)
            def _():
                step = jnp.where(core == owner % 2, arrived[at][core], other_ref[at])
                step = step.astype(f32)
                step = step.T[:cols] if flip else step[:, :cols]
                out_ref[index] = (
                    own_ref[index] * (1.0 - matrix_rate * decay_rate) - rate_ref[index] * step
                )


def update(control, rate, own, arrived, other, owners, flip, after):
    return pl.pallas_call(
        functools.partial(update_kernel, owners, flip, len(after)),
        grid=(1,),
        in_specs=[smem_spec()] * 2 + whole_specs((own, *arrived, other)) + any_specs(len(after)),
        out_specs=whole_spec(own.shape),
        out_shape=jax.ShapeDtypeStruct(own.shape, f32),
        compiler_params=pltpu.CompilerParams(vmem_limit_bytes=vmem_limit),
        name="update",
    )(control, rate, own, *arrived, other, *after)


def finish_kernel(matrices, *refs):
    shares, momentum_ref, (grad_ref, new_ref) = refs[:matrices], refs[matrices], refs[-2:]
    count = shares[0].shape[0]
    cols = grad_ref.shape[2] // count
    for index in range(matrices):
        for turn in range(count):
            at = pl.ds(turn * cols, cols)
            grad = shares[index][turn].astype(f32)[:, :cols]
            grad_ref[index, :, at] = grad
            new_ref[index, :, at] = momentum_decay * momentum_ref[index, :, at] + grad


def finish(share, momentum, after):
    count, _, pad = share.shape
    matrices, shard, width = momentum.shape
    step = min(64, shard)
    steps = shard // step
    whole = pl.BlockSpec((matrices, step, width), lambda i: (0, i, 0))
    parts = [
        pl.BlockSpec((count, step, pad), lambda i, index=index: (0, index * steps + i, 0))
        for index in range(matrices)
    ]
    size = matrices * shard * width
    return pl.pallas_call(
        functools.partial(finish_kernel, matrices),
        grid=(steps,),
        in_specs=parts + [whole] + any_specs(len(after)),
        out_specs=[whole, whole],
        out_shape=[jax.ShapeDtypeStruct(momentum.shape, f32)] * 2,
        compiler_params=pltpu.CompilerParams(vmem_limit_bytes=vmem_limit),
        cost_estimate=pl.CostEstimate(
            flops=2 * size, bytes_accessed=14 * size, transcendentals=0
        ),
        name="finish",
    )(*[share] * matrices, momentum, *after)


def adam_update(parameter, gradient, first_state, second_state):
    first_new = first_decay * first_state + (1.0 - first_decay) * gradient
    second_new = second_decay * second_state + (1.0 - second_decay) * gradient * gradient
    first_hat = first_new / (1.0 - first_decay**STEP)
    second_hat = second_new / (1.0 - second_decay**STEP)
    return (parameter - vector_rate * first_hat / (jnp.sqrt(second_hat) + adam_eps), second_new)


def swap(value, axis, bits, count):
    return lax.ppermute(value, axis, [(i, i ^ bits) for i in range(count)])


def sum_all(value, axis, count):
    bits = 1
    while bits < count:
        value = value + swap(value, axis, bits, count)
        bits *= 2
    return value


def near_wt(block, wt_count):
    return [swap(block, "wt", bits, wt_count) for bits in range(1, min(wt_count, 3))]


def far_wt(block, near, wt_count):
    rows = block.shape[0]
    if wt_count == 4:
        half = rows // 2
        pieces = [swap(near[0][:half], "wt", 2, wt_count), swap(near[1][half:], "wt", 1, wt_count)]
        return pieces, [(3, 0), (3, half)]
    places = [(bits, 0) for bits in range(1 + len(near), wt_count)]
    return [swap(block, "wt", bits, wt_count) for bits, _ in places], places


def sum_wt(parts, wt_count):
    total = parts[0].astype(f32)
    for bits in range(1, wt_count):
        total = total + swap(parts[bits], "wt", bits, wt_count).astype(f32)
    return total


def chip_order(seq_count):
    chips = seq_count // 2
    return [slot_of(chips, slot) for slot in range(chips)]


def gather_chips(block, seq_count):
    return [block] + [swap(block, "seq", 2 * bits, seq_count) for bits in chip_order(seq_count)[1:]]


def both_cores(blocks, seq_count):
    same = jnp.stack(blocks)
    return same, swap(same, "seq", 1, seq_count)


def send_chips(sends, seq_count):
    return [
        swap(value, "seq", 2 * bits, seq_count)
        for bits, value in zip(chip_order(seq_count)[1:], sends)
    ]


def send_owned(value, bits, owners, wt_count):
    pairs = [
        (owner * wt_count + w, owner * wt_count + (w ^ bits))
        for owner in owners
        for w in range(wt_count)
    ]
    return lax.ppermute(value, ("seq", "wt"), pairs)


def near_owned(block, owners, wt_count):
    return [send_owned(block, bits, owners, wt_count) for bits in range(1, min(wt_count, 3))]


def gather_owned(block, near, owners, wt_count):
    pieces = [block] + near
    places = [(part, 0) for part in range(len(pieces))]
    if wt_count == 4:
        half = block.shape[0] // 2
        pieces.append(send_owned(near[0][:half], 2, owners, wt_count))
        pieces.append(send_owned(near[1][half:], 1, owners, wt_count))
        return pieces, places + [(3, 0), (3, half)]
    for bits in range(len(pieces), wt_count):
        pieces.append(send_owned(block, bits, owners, wt_count))
        places.append((bits, 0))
    return pieces, places


def direct_owned(block, owners, wt_count):
    pieces = [block] + [send_owned(block, bits, owners, wt_count) for bits in range(1, wt_count)]
    return pieces, [(part, 0) for part in range(wt_count)]


def spread_chips(blocks, owners, seq_count):
    chips = seq_count // 2
    return [blocks[0]] + [
        lax.ppermute(
            blocks[turn],
            "seq",
            [(owner, (owner // 2 + turn) % chips * 2 + owner % 2) for owner in owners],
        )
        for turn in range(1, chips)
    ]


def spread_cores(arrived, core, seq_count):
    sent = [lax.dynamic_index_in_dim(value, 1 - core, 0, keepdims=False) for value in arrived]
    return swap(jnp.stack(sent), "seq", 1, seq_count)


def per_device(
    tokens,
    cotangent,
    doc_bounds,
    attn_master,
    mlp_master,
    attn_momentum,
    mlp_momentum,
    gains,
    gain_first,
    gain_second,
    qkv_bias,
    bias_first,
    bias_second,
):
    seq_count = lax.axis_size("seq")
    wt_count = lax.axis_size("wt")
    seq_index = lax.axis_index("seq")
    wt_index = lax.axis_index("wt")
    row_count = tokens.shape[1]
    width = tokens.shape[2]
    ff = mlp_master.shape[2]
    shard = attn_master.shape[1]
    length = row_count * seq_count
    head_cols = width // seq_count
    ff_cols = ff // seq_count

    place = jnp.stack([seq_index // 2, seq_index % 2])

    x_same, x_other = both_cores(gather_chips(tokens[0], seq_count), seq_count)
    own_dy, x_same = lax.optimization_barrier((cotangent[0], x_same))
    dy_low = lax.all_gather(own_dy, "seq", axis=0, tiled=True)

    vectors = jnp.pad(jnp.concatenate([gains, qkv_bias], 0), ((0, 11), (0, 3 * head_cols - shard)))
    qkv_w = pack(seq_index, attn_master, vectors, head_cols, [])
    qkv_w = lax.all_gather(qkv_w, "wt", axis=0)
    bounds, qkv_w = lax.optimization_barrier((doc_bounds, qkv_w))
    _, position = doc_layout(bounds[0], length)
    cosine, sine = rope_tables(position, head_cols)
    place_own, qkv_w = lax.optimization_barrier((seq_index, qkv_w))
    attn_own = lax.dynamic_slice_in_dim(attn_master, place_own * head_cols, head_cols, 2)
    mlp_own = lax.dynamic_slice_in_dim(mlp_master, place_own * ff_cols, ff_cols, 2)
    ff_pad = -(-ff_cols // 128) * 128
    wide_own = jnp.pad(mlp_own, ((0, 0), (0, 0), (0, ff_pad - ff_cols)))
    wide_own = jnp.concatenate([attn_master[3], wide_own[0], wide_own[1], wide_own[2]], 1)
    wide_own = wide_own.astype(bf16)
    wide_near = near_wt(wide_own, wt_count)
    vectors = jnp.moveaxis(qkv_w[:, shard : shard + 5, :shard], 0, 1).reshape(5, width).astype(f32)
    qkv_w = qkv_w[:, :shard].reshape(width, 3 * head_cols)

    bias_own = lax.dynamic_slice_in_dim(vectors[2:5], seq_index * head_cols, head_cols, 1)
    x_low, normed_one, query, key, value, attended, log_total = front(
        doc_bounds,
        place,
        x_same,
        x_other,
        qkv_w,
        vectors[0:1],
        bias_own.reshape(1, 3 * head_cols),
        cosine,
        sine,
    )
    a_blocks = gather_chips(attended, seq_count)

    mlp_pick = jnp.minimum(seq_index // 2, 2).reshape(1)
    attn_pick = jnp.minimum(seq_index // 2, 3).reshape(1)
    mlp_pick, attn_pick, attended = lax.optimization_barrier((mlp_pick, attn_pick, attended))
    squares = sums_of_squares(mlp_pick, attn_master, mlp_master)
    wide_near, squares = lax.optimization_barrier((wide_near, squares))
    wide_far, far_places = far_wt(wide_own, wide_near, wt_count)
    mlp_old = picked(mlp_momentum, mlp_pick, seq_count)
    attn_old = picked(attn_momentum, attn_pick, seq_count)
    near_places = [(bits, 0) for bits in range(1 + len(wide_near))]
    wide_w = assemble(
        wt_index,
        [wide_own] + wide_near + wide_far,
        [(bits, first, shard) for bits, first in near_places + far_places],
        width,
    )
    a_blocks, wide_w, squares, mlp_old, attn_old = lax.optimization_barrier(
        (a_blocks, wide_w, squares, mlp_old, attn_old)
    )
    a_same, a_other = both_cores(a_blocks, seq_count)

    normed_two, d_gate, d_up, hidden, d_mine, d_other, resid_own, gain_part_two = middle(
        place, a_same, a_other, x_low, dy_low, wide_w, vectors[1:2]
    )

    control = jnp.stack([jnp.zeros_like(seq_index), seq_index, wt_index])
    mlp_part = mlp_grads(normed_two, dy_low, d_gate, d_up, hidden, wt_count, [])
    mlp_share = lax.psum_scatter(mlp_part, "wt", scatter_dimension=0, tiled=True)
    got = swap(d_other, "seq", 1, seq_count)
    own, *sends = pair_sums(d_mine, got, 1, False, [mlp_part])
    arrived = send_chips(sends, seq_count)
    pair, d_resid = post(
        own, arrived, resid_own, cotangent[0], vectors[1:2], wide_w, seq_count, []
    )
    pair = lax.all_to_all(pair, "seq", split_axis=0, concat_axis=0)
    pair, mlp_share = lax.optimization_barrier((pair, mlp_share))
    mlp_share = lax.all_gather(mlp_share, "seq", axis=0)

    args = (query, key, value, log_total, pair, normed_one, a_same, a_other, cosine, sine)
    args += (qkv_w, vectors[0:1], gain_part_two, squares)
    d_qkv, attn_part = back(doc_bounds, control, args, wt_count)

    def control_of(owners):
        active = functools.reduce(jnp.logical_or, [seq_index == owner for owner in owners])
        return jnp.stack([active.astype(jnp.int32), seq_index, wt_index])

    attn_share = sum_wt(attn_part, wt_count)
    squares = jnp.sum(attn_share[4 * shard + 5 : 4 * shard + 7, :7], axis=0)
    attn_share = attn_share.astype(bf16)
    attn_share = lax.all_gather(attn_share, "seq", axis=0)

    mine, other = late_sums(
        place, hidden, wide_w[:, width + 2 * ff_pad :], d_qkv, qkv_w, seq_count
    )
    late, *sends = pair_sums(mine, swap(other, "seq", 1, seq_count), 1, False, [])

    mlp_block = new_block(mlp_share, mlp_old, mlp_pick, [late])
    mlp_near = near_owned(mlp_block, MLP_OWNERS, wt_count)
    mlp_grad, mlp_mom = finish(mlp_share, mlp_momentum, [mlp_block])
    mlp_near, done = lax.optimization_barrier((mlp_near, mlp_grad[0, :8, :128]))
    mlp_pieces, mlp_places = gather_owned(mlp_block, mlp_near, MLP_OWNERS, wt_count)
    sends, attn_share = lax.optimization_barrier((sends, attn_share))
    late_arrived = send_chips(sends, seq_count)
    attn_block = new_block(attn_share, attn_old, attn_pick, [])
    attn_near = near_owned(attn_block, ATTN_OWNERS, wt_count)
    attn_near, mlp_pieces = lax.optimization_barrier((attn_near, mlp_pieces))
    attn_pieces, attn_places = gather_owned(attn_block, attn_near, ATTN_OWNERS, wt_count)
    mlp_blocks = orthogonalize(
        control_of(MLP_OWNERS), mlp_pieces, mlp_places, wt_count, [done, *attn_pieces[1:]]
    )
    attn_blocks = orthogonalize(
        control_of(ATTN_OWNERS), attn_pieces, attn_places, wt_count, [mlp_blocks[0]]
    )
    mlp_blocks, attn_blocks, late_arrived = lax.optimization_barrier(
        (mlp_blocks, attn_blocks, late_arrived)
    )
    attn_grad, attn_mom = finish(attn_share, attn_momentum, attn_blocks[:1])

    attn_rate = matrix_rate * math.sqrt(width) * jnp.sqrt(squares[:4] / (width * width))
    mlp_rate = matrix_rate * math.sqrt(ff) * jnp.sqrt(squares[4:] / (width * ff))
    core = seq_index % 2
    mlp_arrived = spread_chips(mlp_blocks, MLP_OWNERS, seq_count)
    attn_arrived = spread_chips(attn_blocks, ATTN_OWNERS, seq_count)

    total = late[0]
    for value in late_arrived:
        total = total + value[0].astype(f32)
    layer_out = (resid_own + total[0]).astype(bf16)
    x_own = tokens[0].astype(f32)
    inverse_own = lax.rsqrt(jnp.mean(x_own * x_own, axis=-1, keepdims=True) + norm_eps)
    d_input_norm = norm_backward(total[1], x_own, inverse_own, vectors[0])
    tokens_grad = d_resid + d_input_norm

    mlp_arrived, attn_arrived, layer_out, tokens_grad, done = lax.optimization_barrier(
        (mlp_arrived, attn_arrived, layer_out, tokens_grad, attn_grad[0, :8, :128])
    )
    mlp_other = spread_cores(mlp_arrived, core, seq_count)
    attn_other = spread_cores(attn_arrived, core, seq_count)
    attn_new = update(
        control, attn_rate, attn_own, attn_arrived, attn_other, ATTN_OWNERS, False, [done]
    )
    mlp_new = update(
        control,
        mlp_rate,
        mlp_own.swapaxes(1, 2),
        mlp_arrived,
        mlp_other,
        MLP_OWNERS,
        True,
        [done],
    ).swapaxes(1, 2)

    small = jnp.sum(attn_share[:, 4 * shard :].astype(f32), axis=0).reshape(2, 8, 128)
    small = jnp.moveaxis(small[: shard // 128], 0, 1).reshape(8, shard)
    gain_grad = small[:2]
    bias_grad = small[2:5]
    gain_new, gain_second_new = adam_update(gains, gain_grad, gain_first, gain_second)
    bias_new, bias_second_new = adam_update(qkv_bias, bias_grad, bias_first, bias_second)
    return (
        layer_out[None],
        tokens_grad[None],
        attn_grad,
        mlp_grad,
        attn_mom,
        mlp_mom,
        attn_new,
        mlp_new,
        gain_grad,
        gain_second_new,
        gain_new,
        bias_grad,
        bias_second_new,
        bias_new,
    )


def solution(mesh):
    return jax.shard_map(
        per_device,
        mesh=mesh,
        in_specs=(
            P("wt", "seq", None),
            P("wt", "seq", None),
            P("wt", None),
            P(None, "wt", None),
            P(None, "wt", None),
            P(None, "wt", None),
            P(None, "wt", None),
            P(None, "wt"),
            P(None, "wt"),
            P(None, "wt"),
            P(None, "wt"),
            P(None, "wt"),
            P(None, "wt"),
        ),
        out_specs=(
            P("wt", "seq", None),
            P("wt", "seq", None),
            P(None, "wt", None),
            P(None, "wt", None),
            P(None, "wt", None),
            P(None, "wt", None),
            P(None, "wt", "seq"),
            P(None, "wt", "seq"),
            P(None, "wt"),
            P(None, "wt"),
            P(None, "wt"),
            P(None, "wt"),
            P(None, "wt"),
            P(None, "wt"),
        ),
        check_vma=False,
    )
```

```python
import functools
import math

import jax
import jax.numpy as jnp
from jax import lax
from jax.experimental import pallas as pl
from jax.experimental.pallas import tpu as pltpu
from jax.sharding import PartitionSpec as P

HEAD_DIM = 64
NS_STEPS = 5
STEP = 10

norm_eps = 1e-06
rope_base = 1000000.0
coef_a = 3.4445
coef_b = -4.775
coef_c = 2.0315
momentum_decay = 0.95
matrix_rate = 0.5
decay_rate = 0.01
first_decay = 0.9
second_decay = 0.95
vector_rate = 0.25
adam_eps = 1e-08
ortho_eps = 1e-07
masked_score = -1e30
tile = 256
vmem_limit = 62 * 2**20

MLP_OWNERS = (0, 2, 4)
ATTN_OWNERS = (1, 3, 5, 6)

f32 = jnp.float32
bf16 = jnp.bfloat16


def dot32(a, b, ca, cb):
    return lax.dot_general(a, b, (((ca,), (cb,)), ((), ())), preferred_element_type=f32)


def doc_layout(bounds, length):
    places = jnp.arange(length, dtype=jnp.int32)
    first_bound = bounds[0]
    second_bound = bounds[1]
    doc_index = (places >= first_bound).astype(jnp.int32) + (places >= second_bound).astype(
        jnp.int32
    )
    doc_start = jnp.where(
        places < first_bound, 0, jnp.where(places < second_bound, first_bound, second_bound)
    )
    return (doc_index, (places - doc_start).astype(f32))


def rope_tables(position, cols):
    half_dim = HEAD_DIM // 2
    lane = jnp.arange(cols, dtype=jnp.int32) % HEAD_DIM
    frequency = rope_base ** (-2.0 * jnp.arange(half_dim, dtype=f32) / HEAD_DIM)
    angles = position[:, None] * frequency[None, :]
    repeat = cols // half_dim
    cosine = jnp.concatenate([jnp.cos(angles)] * repeat, 1)
    sine = jnp.concatenate([jnp.sin(angles)] * repeat, 1)
    return cosine, jnp.where(lane < half_dim, -1.0, 1.0)[None, :] * sine


def swap_halves(values):
    half_dim = HEAD_DIM // 2
    parts = []
    for first in range(0, values.shape[1], HEAD_DIM):
        parts.append(values[:, first + half_dim : first + HEAD_DIM])
        parts.append(values[:, first : first + half_dim])
    return jnp.concatenate(parts, axis=1)


def visible(bounds_ref, first, rows, length):
    query = first + lax.broadcasted_iota(jnp.int32, (rows, length), 0)
    key = lax.broadcasted_iota(jnp.int32, (rows, length), 1)
    one, two = bounds_ref[0, 0], bounds_ref[0, 1]
    start = jnp.where(query < one, 0, jnp.where(query < two, one, two))
    return (key <= query) & (key >= start)


def slot_of(chips, value):
    slot, bits = 0, chips
    while bits > 1:
        slot = slot * 2 + (value & 1)
        value = value >> 1
        bits //= 2
    return slot


def front_kernel(
    bounds_ref,
    place_ref,
    same_ref,
    other_ref,
    weight_ref,
    gain_ref,
    bias_ref,
    cosine_ref,
    sine_ref,
    x_ref,
    normed_ref,
    query_ref,
    key_ref,
    value_ref,
    attended_ref,
    log_ref,
):
    length = x_ref.shape[0]
    cols = query_ref.shape[1]
    chips, rows, _ = same_ref.shape
    for chip in range(chips):
        at = pl.ds(chip * 2 * rows, 2 * rows)
        slot = slot_of(chips, place_ref[0] ^ chip)
        low = pl.ds(chip * 2 * rows + place_ref[1] * rows, rows)
        high = pl.ds(chip * 2 * rows + (1 - place_ref[1]) * rows, rows)
        x_ref[low, :] = same_ref[slot]
        x_ref[high, :] = other_ref[slot]
        x = x_ref[at, :].astype(f32)
        inverse = lax.rsqrt(jnp.mean(x * x, axis=-1, keepdims=True) + norm_eps)
        normed = (x * inverse * gain_ref[...]).astype(bf16)
        normed_ref[at, :] = normed
        projected = (dot32(normed, weight_ref[...], 1, 0) + bias_ref[...]).astype(bf16).astype(f32)
        cosine, sine = cosine_ref[at, :], sine_ref[at, :]
        query = projected[:, :cols]
        key = projected[:, cols : 2 * cols]
        query_ref[at, :] = (query * cosine + swap_halves(query) * sine).astype(bf16)
        key_ref[at, :] = (key * cosine + swap_halves(key) * sine).astype(bf16)
        value_ref[at, :] = projected[:, 2 * cols :].astype(bf16)
    for first in range(0, length, tile):
        at, keys = pl.ds(first, tile), pl.ds(0, first + tile)
        allowed = visible(bounds_ref, first, tile, first + tile)
        attended = []
        for head in range(cols // HEAD_DIM):
            lanes = pl.ds(head * HEAD_DIM, HEAD_DIM)
            scores = dot32(query_ref[at, lanes], key_ref[keys, lanes], 1, 1)
            scores = jnp.where(allowed, scores * HEAD_DIM ** (-0.5), masked_score)
            peak = jnp.max(scores, axis=-1, keepdims=True)
            exponent = jnp.exp(scores - peak)
            total = jnp.sum(exponent, axis=-1, keepdims=True)
            weights = (exponent * (1.0 / total)).astype(bf16)
            attended.append(dot32(weights, value_ref[keys, lanes], 1, 0))
            log_ref[at, pl.ds(head, 1)] = peak + jnp.log(total)
        attended_ref[at, :] = jnp.concatenate(attended, axis=1).astype(bf16)


def vmem_specs(count):
    return [pl.BlockSpec(memory_space=pltpu.VMEM)] * count


def whole_spec(shape):
    return pl.BlockSpec(shape, lambda i: (0,) * len(shape))


def whole_specs(arrays):
    return [whole_spec(value.shape) for value in arrays]


def any_specs(count):
    return [pl.BlockSpec(memory_space=pl.ANY)] * count


def smem_spec():
    return pl.BlockSpec(memory_space=pltpu.SMEM)


def front(bounds, place, same, other, weight, gain, bias, cosine, sine):
    chips, rows, width = same.shape
    length, cols = cosine.shape
    part = jax.ShapeDtypeStruct((length, cols), bf16)
    shapes = [
        jax.ShapeDtypeStruct((length, width), bf16),
        jax.ShapeDtypeStruct((length, width), bf16),
        part,
        part,
        part,
        part,
        jax.ShapeDtypeStruct((length, cols // HEAD_DIM), f32),
    ]
    args = (same, other, weight, gain, bias, cosine, sine)
    return pl.pallas_call(
        front_kernel,
        grid=(1,),
        in_specs=[smem_spec()] * 2 + whole_specs(args),
        out_specs=whole_specs(shapes),
        out_shape=shapes,
        compiler_params=pltpu.CompilerParams(vmem_limit_bytes=vmem_limit),
        cost_estimate=pl.CostEstimate(
            flops=8 * 10**9, bytes_accessed=8 * 10**6, transcendentals=2 * 10**6
        ),
        name="front",
    )(bounds, place, *args)


def store_split(place_ref, mine_ref, other_ref, index, value):
    rows = value.shape[0] // 2
    core = place_ref[1]
    top, low = value[:rows], value[rows:]
    mine_ref[0, index] = jnp.where(core == 0, top, low)
    other_ref[0, index] = jnp.where(core == 0, low, top).astype(bf16)


def split_out(chips, sums, rows, width):
    spec = pl.BlockSpec(
        (1, sums, rows, width), lambda i, place: (slot_of(chips, i ^ place[0]), 0, 0, 0)
    )
    shape = (chips, sums, rows, width)
    return [spec, spec], [jax.ShapeDtypeStruct(shape, f32), jax.ShapeDtypeStruct(shape, bf16)]


def middle_kernel(
    place_ref,
    same_ref,
    other_ref,
    x_ref,
    dy_ref,
    weight_ref,
    gain_ref,
    normed_ref,
    d_gate_ref,
    d_up_ref,
    hidden_ref,
    d_mine_ref,
    d_other_ref,
    resid_ref,
    gain_part_ref,
):
    width = x_ref.shape[1]
    cols = d_gate_ref.shape[1]
    rows = resid_ref.shape[0]
    gate_w = weight_ref.at[:, pl.ds(width, cols)]
    up_w = weight_ref.at[:, pl.ds(width + cols, cols)]
    down_w = weight_ref.at[:, pl.ds(width + 2 * cols, cols)]
    attended = []
    for chip in range(same_ref.shape[0]):
        slot = slot_of(same_ref.shape[0], place_ref[0] ^ chip)
        same, other = same_ref[slot], other_ref[slot]
        attended.append(jnp.where(place_ref[1] == 0, same, other))
        attended.append(jnp.where(place_ref[1] == 0, other, same))
    attended = jnp.concatenate(attended, axis=1)
    resid = x_ref[...].astype(f32) + dot32(attended, weight_ref[:, pl.ds(0, width)], 1, 0)

    @pl.when(pl.program_id(0) == place_ref[0])
    def _():
        resid_ref[...] = jnp.where(place_ref[1] == 0, resid[:rows], resid[rows:])

    inverse = lax.rsqrt(jnp.mean(resid * resid, axis=-1, keepdims=True) + norm_eps)
    normed = (resid * inverse * gain_ref[...]).astype(bf16)
    normed_ref[...] = normed
    gate = dot32(normed, gate_w[...], 1, 0)
    up = dot32(normed, up_w[...], 1, 0)
    d_hidden = dot32(dy_ref[...], down_w[...], 1, 0)
    sigmoid = jax.nn.sigmoid(gate)
    silu = gate * sigmoid
    hidden = (silu * up).astype(bf16)
    hidden_ref[...] = hidden
    d_gate = (d_hidden * up * (sigmoid * (1.0 + gate * (1.0 - sigmoid)))).astype(bf16)
    d_up = (d_hidden * silu).astype(bf16)
    d_gate_ref[...] = d_gate
    d_up_ref[...] = d_up
    d_normed = dot32(d_gate, gate_w[...], 1, 1) + dot32(d_up, up_w[...], 1, 1)
    store_split(place_ref, d_mine_ref, d_other_ref, 0, d_normed)

    @pl.when(pl.program_id(0) == 0)
    def _():
        gain_part_ref[...] = jnp.zeros_like(gain_part_ref)

    gain_part_ref[...] += jnp.sum(d_normed * resid * inverse, axis=0, keepdims=True)


def middle(place, same, other, x, dy, weight, gain):
    chips, length, head_cols = same.shape
    count = 2 * chips
    width = x.shape[1]
    cols = (weight.shape[1] - width) // 3
    half = length // count
    rows = 2 * half

    def block(size):
        return pl.BlockSpec((rows, size), lambda i, place: (i, 0))

    def whole(shape):
        return pl.BlockSpec(shape, lambda i, place: (0,) * len(shape))

    split_specs, split_shapes = split_out(chips, 1, half, width)
    wide = jax.ShapeDtypeStruct((length, cols), bf16)
    return pl.pallas_call(
        middle_kernel,
        grid_spec=pltpu.PrefetchScalarGridSpec(
            num_scalar_prefetch=1,
            grid=(chips,),
            in_specs=[
                pl.BlockSpec((chips, rows, head_cols), lambda i, place: (0, i, 0)),
                pl.BlockSpec((chips, rows, head_cols), lambda i, place: (0, i, 0)),
                block(width),
                block(width),
                whole(weight.shape),
                whole(gain.shape),
            ],
            out_specs=[
                block(width),
                block(cols),
                block(cols),
                block(cols),
                *split_specs,
                whole((half, width)),
                whole((1, width)),
            ],
        ),
        out_shape=[
            jax.ShapeDtypeStruct((length, width), bf16),
            wide,
            wide,
            wide,
            *split_shapes,
            jax.ShapeDtypeStruct((half, width), f32),
            jax.ShapeDtypeStruct((1, width), f32),
        ],
        compiler_params=pltpu.CompilerParams(vmem_limit_bytes=vmem_limit),
        cost_estimate=pl.CostEstimate(
            flops=10 * 10**9, bytes_accessed=20 * 10**6, transcendentals=10**6
        ),
        name="middle",
    )(place, same, other, x, dy, weight, gain)


def pair_kernel(kept, extra, mine_ref, got_ref, *refs):
    keep_ref, sends = refs[extra], refs[extra + 1 :]
    for slot in range(kept):
        keep_ref[slot] = mine_ref[slot] + got_ref[slot].astype(f32)
    for slot in range(kept, mine_ref.shape[0]):
        value = (mine_ref[slot] + got_ref[slot].astype(f32)).astype(bf16)
        if len(sends) == 1:
            sends[0][slot - kept] = value
        else:
            sends[slot - kept][0] = value


def pair_sums(mine, got, kept, together, after):
    slots, sums, rows, width = mine.shape
    step = 32

    def spec(count):
        return pl.BlockSpec((count, sums, step, width), lambda i: (0, 0, i, 0))

    counts = [slots - kept] if together else [1] * (slots - kept)
    return pl.pallas_call(
        functools.partial(pair_kernel, kept, len(after)),
        grid=(rows // step,),
        in_specs=[spec(slots)] * 2 + any_specs(len(after)),
        out_specs=[spec(kept)] + [spec(count) for count in counts],
        out_shape=[jax.ShapeDtypeStruct((kept, sums, rows, width), f32)]
        + [jax.ShapeDtypeStruct((count, sums, rows, width), bf16) for count in counts],
        compiler_params=pltpu.CompilerParams(vmem_limit_bytes=vmem_limit),
        name="pair_sums",
    )(mine, got, *after)


def post_kernel(extra, own_ref, resid_ref, dy_ref, gain_ref, weight_ref, *refs):
    arrived, (pair_ref, d_resid_ref) = refs[: -2 - extra], refs[-2:]
    d_normed = own_ref[0, 0]
    for ref in arrived:
        d_normed = d_normed + ref[0, 0].astype(f32)
    resid = resid_ref[...]
    inverse = lax.rsqrt(jnp.mean(resid * resid, axis=-1, keepdims=True) + norm_eps)
    scaled = d_normed * gain_ref[...]
    d_resid = (
        dy_ref[...].astype(f32)
        + inverse * scaled
        - resid * (inverse * inverse * inverse) * jnp.mean(scaled * resid, axis=-1, keepdims=True)
    )
    d_resid_ref[...] = d_resid
    low = d_resid.astype(bf16)
    d_attn = dot32(low, weight_ref[...], 1, 1).astype(bf16)
    cols = pair_ref.shape[3]
    for part in range(pair_ref.shape[0]):
        pair_ref[part, 0] = d_attn[:, part * cols : (part + 1) * cols]
        pair_ref[part, 1] = low[:, part * cols : (part + 1) * cols]


def post(own, arrived, resid, dy, gain, weight, count, after):
    rows, width = resid.shape
    cols = width // count

    def whole(shape):
        return pl.BlockSpec(shape, lambda i: (0,) * len(shape))

    return pl.pallas_call(
        functools.partial(post_kernel, len(after)),
        grid=(1,),
        in_specs=[whole(own.shape), whole(resid.shape), whole(dy.shape), whole(gain.shape)]
        + [whole((width, width))]
        + [whole(value.shape) for value in arrived]
        + any_specs(len(after)),
        out_specs=[whole((count, 2, rows, cols)), whole((rows, width))],
        out_shape=[
            jax.ShapeDtypeStruct((count, 2, rows, cols), bf16),
            jax.ShapeDtypeStruct((rows, width), f32),
        ],
        compiler_params=pltpu.CompilerParams(vmem_limit_bytes=vmem_limit),
        name="post",
    )(own, resid, dy, gain, weight, *arrived, *after)


def mlp_grads_kernel(
    parts, extra, normed_ref, dy_ref, d_gate_ref, d_up_ref, hidden_ref, *refs
):
    out_ref = refs[extra]
    shard = out_ref.shape[0] // (3 * parts)
    for part in range(parts):
        at = pl.ds(part * shard, shard)
        normed = normed_ref[:, at]
        pairs = [(normed, d_gate_ref), (normed, d_up_ref), (dy_ref[:, at], hidden_ref)]
        for index, (left, right_ref) in enumerate(pairs):
            out_ref[pl.ds((3 * part + index) * shard, shard), :] = dot32(
                left, right_ref[...], 0, 0
            ).astype(bf16)


def mlp_grads(normed, dy, d_gate, d_up, hidden, parts, after):
    width = normed.shape[1]
    args = (normed, dy, d_gate, d_up, hidden)
    shape = jax.ShapeDtypeStruct((3 * width, hidden.shape[1]), bf16)
    return pl.pallas_call(
        functools.partial(mlp_grads_kernel, parts, len(after)),
        grid=(1,),
        in_specs=whole_specs(args) + any_specs(len(after)),
        out_specs=whole_spec(shape.shape),
        out_shape=shape,
        compiler_params=pltpu.CompilerParams(vmem_limit_bytes=vmem_limit),
        cost_estimate=pl.CostEstimate(
            flops=3 * 10**9, bytes_accessed=9 * 10**6, transcendentals=0
        ),
        name="mlp_grads",
    )(*args, *after)


def back_kernel(
    parts,
    bounds_ref,
    control_ref,
    query_ref,
    key_ref,
    value_ref,
    log_ref,
    arrived_ref,
    normed_ref,
    same_ref,
    other_ref,
    cosine_ref,
    sine_ref,
    weight_ref,
    gain_ref,
    gain_two_ref,
    squares_ref,
    d_qkv_ref,
    *refs,
):
    grads_refs, (d_key_ref, d_value_ref, d_attn_ref, d_resid_ref) = refs[:parts], refs[parts:]
    length, cols = query_ref.shape
    count, _, rows, _ = arrived_ref.shape
    scale = HEAD_DIM ** (-0.5)
    for part in range(count):
        d_attn_ref[pl.ds(part * rows, rows), :] = arrived_ref[part, 0]
        d_resid_ref[pl.ds(part * rows, rows), :] = arrived_ref[part, 1]
    d_key_ref[...] = jnp.zeros_like(d_key_ref)
    d_value_ref[...] = jnp.zeros_like(d_value_ref)

    def undo(values, at):
        return values * cosine_ref[at, :] - swap_halves(values) * sine_ref[at, :]

    for first in range(0, length, tile):
        at, keys = pl.ds(first, tile), pl.ds(0, first + tile)
        allowed = visible(bounds_ref, first, tile, first + tile)
        d_query, d_key, d_value = [], [], []
        for head in range(cols // HEAD_DIM):
            lanes = pl.ds(head * HEAD_DIM, HEAD_DIM)
            query, d_out = query_ref[at, lanes], d_attn_ref[at, lanes]
            key, value = key_ref[keys, lanes], value_ref[keys, lanes]
            scores = jnp.where(allowed, dot32(query, key, 1, 1) * scale, masked_score)
            weights = jnp.exp(scores - log_ref[at, pl.ds(head, 1)])
            d_value.append(dot32(weights.astype(bf16), d_out, 0, 0))
            d_weights = dot32(d_out, value, 1, 1)
            inner = jnp.sum(weights * d_weights, axis=-1, keepdims=True)
            d_scores = (weights * (d_weights - inner)).astype(bf16)
            d_query.append(dot32(d_scores, key, 1, 0) * scale)
            d_key.append(dot32(d_scores, query, 0, 0) * scale)
        d_key_ref[keys, :] += jnp.concatenate(d_key, axis=1)
        d_value_ref[keys, :] += jnp.concatenate(d_value, axis=1)
        d_qkv_ref[at, pl.ds(0, cols)] = undo(jnp.concatenate(d_query, axis=1), at).astype(bf16)
    for first in range(0, length, tile):
        at = pl.ds(first, tile)
        d_qkv_ref[at, pl.ds(cols, cols)] = undo(d_key_ref[at, :], at).astype(bf16)
        d_qkv_ref[at, pl.ds(2 * cols, cols)] = d_value_ref[at, :].astype(bf16)
    shard = gain_ref.shape[1] // parts
    pad = grads_refs[0].shape[1]
    pieces = shard // cols
    bias = jnp.sum(d_qkv_ref[...].astype(f32), axis=0, keepdims=True)
    lane = lax.broadcasted_iota(jnp.int32, squares_ref.shape, 1)
    row = lax.broadcasted_iota(jnp.int32, squares_ref.shape, 0)
    squares = jnp.sum(jnp.where(lane == row, squares_ref[...], 0.0), axis=0, keepdims=True)
    squares_high = squares.astype(bf16).astype(f32)
    rest = jnp.zeros((1, shard - squares.shape[1]), f32)

    def wide(value):
        return value if shard == 128 else jnp.concatenate([value, rest], axis=1)

    for part in range(parts):
        block = control_ref[2] ^ part
        grads_ref = grads_refs[part]
        at = pl.ds(pl.multiple_of(block * shard, 128), shard)
        grads = dot32(normed_ref[:, at], d_qkv_ref[...], 0, 0)
        gain_one = lax.dot_general(
            jnp.ones((8, 3 * cols), f32),
            grads * weight_ref[at, :].astype(f32),
            (((1,), (1,)), ((), ())),
            precision=lax.Precision.HIGHEST,
            preferred_element_type=f32,
        )[0:1]
        grads = grads.astype(bf16)
        for index in range(3):
            grads_ref[pl.ds(index * shard, shard), pl.ds(0, cols)] = grads[
                :, index * cols : (index + 1) * cols
            ]
        for piece in range(pieces):
            place = block * pieces + piece
            slot = slot_of(same_ref.shape[0], (place >> 1) ^ (control_ref[1] >> 1))
            near = ((place ^ control_ref[1]) & 1) == 0
            attended = jnp.where(near, same_ref[slot], other_ref[slot])
            grads_ref[pl.ds(3 * shard + piece * cols, cols), pl.ds(0, cols)] = dot32(
                attended, d_resid_ref[...], 0, 0
            ).astype(bf16)
        if pad > cols:
            grads_ref[pl.ds(0, 4 * shard), pl.ds(cols, pad - cols)] = jnp.zeros(
                (4 * shard, pad - cols), bf16
            )
        small = [gain_one / gain_ref[:, at], gain_two_ref[:, at]]
        for index in range(3):
            own = bias[:, index * cols : (index + 1) * cols]
            small.append(
                jnp.concatenate(
                    [
                        jnp.where(block * pieces + piece == control_ref[1], own, 0.0)
                        for piece in range(pieces)
                    ],
                    axis=1,
                )
            )
        small += [wide(squares_high), wide(squares - squares_high), jnp.zeros((1, shard), f32)]
        small = jnp.concatenate(small, axis=0)
        small = [small[:, first : first + 128] for first in range(0, shard, 128)]
        small += [jnp.zeros((8, 128), f32)] * (2 - len(small))
        grads_ref[pl.ds(4 * shard, 16), :] = jnp.concatenate(small, axis=0).astype(bf16)


def back(bounds, control, args, parts):
    query, normed = args[0], args[5]
    length, cols = query.shape
    width = normed.shape[1]
    pad = -(-cols // 128) * 128
    shapes = [jax.ShapeDtypeStruct((length, 3 * cols), bf16)]
    shapes += [jax.ShapeDtypeStruct((4 * width // parts + 16, pad), bf16)] * parts
    results = pl.pallas_call(
        functools.partial(back_kernel, parts),
        grid=(1,),
        in_specs=[smem_spec()] * 2 + whole_specs(args),
        out_specs=whole_specs(shapes),
        out_shape=shapes,
        scratch_shapes=[
            pltpu.VMEM((length, cols), f32),
            pltpu.VMEM((length, cols), f32),
            pltpu.VMEM((length, cols), bf16),
            pltpu.VMEM((length, cols), bf16),
        ],
        compiler_params=pltpu.CompilerParams(vmem_limit_bytes=vmem_limit),
        cost_estimate=pl.CostEstimate(
            flops=10 * 10**9, bytes_accessed=8 * 10**6, transcendentals=2 * 10**6
        ),
        name="back",
    )(bounds, control, *args)
    return results[0], results[1:]


def late_kernel(place_ref, hidden_ref, down_ref, d_qkv_ref, weight_ref, mine_ref, other_ref):
    store_split(place_ref, mine_ref, other_ref, 0, dot32(hidden_ref[...], down_ref[...], 1, 1))
    store_split(place_ref, mine_ref, other_ref, 1, dot32(d_qkv_ref[...], weight_ref[...], 1, 1))


def late_sums(place, hidden, down, d_qkv, weight, count):
    length, cols = d_qkv.shape
    width = weight.shape[0]
    chips = count // 2
    half = length // count
    rows = 2 * half

    def block(size):
        return pl.BlockSpec((rows, size), lambda i, place: (i, 0))

    def whole(shape):
        return pl.BlockSpec(shape, lambda i, place: (0, 0))

    split_specs, split_shapes = split_out(chips, 2, half, width)
    return pl.pallas_call(
        late_kernel,
        grid_spec=pltpu.PrefetchScalarGridSpec(
            num_scalar_prefetch=1,
            grid=(chips,),
            in_specs=[
                block(hidden.shape[1]),
                whole(down.shape),
                block(cols),
                whole(weight.shape),
            ],
            out_specs=split_specs,
        ),
        out_shape=split_shapes,
        compiler_params=pltpu.CompilerParams(vmem_limit_bytes=vmem_limit),
        cost_estimate=pl.CostEstimate(
            flops=2 * 10**9, bytes_accessed=16 * 10**6, transcendentals=0
        ),
        name="late_sums",
    )(place, hidden, down, d_qkv, weight)


def picked_kernel(pick_ref, momentum_ref, out_ref):
    count, rows, pad = out_ref.shape
    cols = momentum_ref.shape[2] // count
    for turn in range(count):
        value = momentum_ref[0, :, pl.ds(turn * cols, cols)] * momentum_decay
        out_ref[turn, :, pl.ds(0, cols)] = value
        if pad > cols:
            out_ref[turn, :, pl.ds(cols, pad - cols)] = jnp.zeros((rows, pad - cols), f32)


def picked(momentum, pick, count):
    rows, width = momentum.shape[1:]
    pad = -(-(width // count) // 128) * 128
    step = min(64, rows)
    return pl.pallas_call(
        picked_kernel,
        grid_spec=pltpu.PrefetchScalarGridSpec(
            num_scalar_prefetch=1,
            grid=(rows // step,),
            in_specs=[pl.BlockSpec((1, step, width), lambda i, pick: (pick[0], i, 0))],
            out_specs=pl.BlockSpec((count, step, pad), lambda i, pick: (0, i, 0)),
        ),
        out_shape=jax.ShapeDtypeStruct((count, rows, pad), f32),
        compiler_params=pltpu.CompilerParams(vmem_limit_bytes=vmem_limit),
        cost_estimate=pl.CostEstimate(
            flops=rows * width, bytes_accessed=8 * rows * width, transcendentals=0
        ),
        name="picked",
    )(pick, momentum)


def squares_kernel(order_ref, attn_ref, mlp_ref, out_ref):
    @pl.when(pl.program_id(0) == 0)
    def _():
        out_ref[...] = jnp.zeros_like(out_ref)

    at = 0
    for ref in (attn_ref, mlp_ref):
        for index in range(ref.shape[0]):
            value = ref[index].astype(bf16).astype(f32)
            total = jnp.sum(jnp.sum(value * value, axis=0, keepdims=True), axis=1, keepdims=True)
            out_ref[pl.ds(at, 1), :] += jnp.broadcast_to(total, (1, out_ref.shape[1]))
            at += 1


def block_kernel(extra, pick_ref, share_ref, old_ref, *refs):
    refs[extra][...] = (old_ref[...] + share_ref[...].astype(f32)).astype(bf16)


def new_block(share, old, pick, after):
    count, shard, pad = old.shape
    step = 2
    return pl.pallas_call(
        functools.partial(block_kernel, len(after)),
        grid_spec=pltpu.PrefetchScalarGridSpec(
            num_scalar_prefetch=1,
            grid=(count // step,),
            in_specs=[
                pl.BlockSpec((step, shard, pad), lambda i, pick: (i, pick[0], 0)),
                pl.BlockSpec((step, shard, pad), lambda i, pick: (i, 0, 0)),
            ]
            + any_specs(len(after)),
            out_specs=pl.BlockSpec((step, shard, pad), lambda i, pick: (i, 0, 0)),
        ),
        out_shape=jax.ShapeDtypeStruct(old.shape, bf16),
        compiler_params=pltpu.CompilerParams(vmem_limit_bytes=vmem_limit),
        cost_estimate=pl.CostEstimate(
            flops=old.size, bytes_accessed=8 * old.size, transcendentals=0
        ),
        name="new_block",
    )(pick, share, old, *after)


def sums_of_squares(order, attn, mlp):
    rows = attn.shape[1]
    step = min(64, rows)
    return pl.pallas_call(
        squares_kernel,
        grid=(rows // step,),
        in_specs=[
            smem_spec(),
            pl.BlockSpec((attn.shape[0], step, attn.shape[2]), lambda i: (0, i, 0)),
            pl.BlockSpec((mlp.shape[0], step, mlp.shape[2]), lambda i: (0, i, 0)),
        ],
        out_specs=pl.BlockSpec((8, 128), lambda i: (0, 0)),
        out_shape=jax.ShapeDtypeStruct((8, 128), f32),
        compiler_params=pltpu.CompilerParams(vmem_limit_bytes=vmem_limit),
        cost_estimate=pl.CostEstimate(
            flops=2 * (attn.size + mlp.size),
            bytes_accessed=4 * (attn.size + mlp.size),
            transcendentals=0,
        ),
        name="sums_of_squares",
    )(order, attn, mlp)


def pack_kernel(place_ref, master_ref, vectors_ref, *refs):
    out_ref = refs[-1]
    shard = master_ref.shape[1]
    cols = out_ref.shape[1] // 3
    for index in range(3):
        value = master_ref[index].astype(bf16)
        part = value[:, :cols]
        for at in range(1, value.shape[1] // cols):
            part = jnp.where(place_ref[1] == at, value[:, at * cols : (at + 1) * cols], part)
        out_ref[pl.ds(0, shard), pl.ds(index * cols, cols)] = part
    out_ref[pl.ds(shard, 16), :] = vectors_ref[...].astype(bf16)


def pack(seq_index, master, vectors, cols, after):
    shard = master.shape[1]
    lanes = max(cols, 128)
    place = jnp.stack([seq_index // (lanes // cols), seq_index % (lanes // cols)])
    shape = (shard + 16, 3 * cols)
    return pl.pallas_call(
        pack_kernel,
        grid_spec=pltpu.PrefetchScalarGridSpec(
            num_scalar_prefetch=1,
            grid=(1,),
            in_specs=[
                pl.BlockSpec((3, shard, lanes), lambda i, place: (0, 0, place[0])),
                pl.BlockSpec(vectors.shape, lambda i, place: (0, 0)),
            ]
            + any_specs(len(after)),
            out_specs=pl.BlockSpec(shape, lambda i, place: (0, 0)),
        ),
        out_shape=jax.ShapeDtypeStruct(shape, bf16),
        compiler_params=pltpu.CompilerParams(vmem_limit_bytes=vmem_limit),
        name="pack",
    )(place, master, vectors, *after)


def assemble_kernel(places, wt_ref, *refs):
    pieces, out_ref, arrived = refs[: len(places)], refs[-2], refs[-1]
    copies = []
    for at, (bits, first, rows) in enumerate(places):
        start = pl.multiple_of((wt_ref[0] ^ bits) * rows + first, 16)
        target = out_ref.at[pl.ds(start, pieces[at].shape[0]), :]
        copies.append(pltpu.make_async_copy(pieces[at], target, arrived.at[at]))
    for copy in copies:
        copy.start()
    for copy in copies:
        copy.wait()


def assemble(wt_index, pieces, places, rows):
    size = rows * pieces[0].shape[1]
    return pl.pallas_call(
        functools.partial(assemble_kernel, places),
        in_specs=[smem_spec()] + any_specs(len(pieces)),
        out_specs=vmem_specs(1)[0],
        out_shape=jax.ShapeDtypeStruct((rows, pieces[0].shape[1]), pieces[0].dtype),
        scratch_shapes=[pltpu.SemaphoreType.DMA((len(pieces),))],
        compiler_params=pltpu.CompilerParams(vmem_limit_bytes=vmem_limit),
        cost_estimate=pl.CostEstimate(flops=0, bytes_accessed=4 * size, transcendentals=0),
        name="assemble",
    )(wt_index.reshape(1), *pieces)


def norm_backward(d_normed, values, inverse, gain_row):
    scaled = d_normed * gain_row
    return inverse * scaled - values * inverse**3 * jnp.mean(
        scaled * values, axis=-1, keepdims=True
    )


def ortho_kernel(places, extra, control_ref, *refs):
    pieces, outs = refs[: len(places)], refs[len(places) + extra : -8]
    whole, gram, prod, gram_low, prod_low, poly_low, rows, arrived = refs[-8:]
    parts, count = arrived.shape
    shard, pad = outs[0].shape[1:]
    width = gram.shape[0]
    tiles = width // tile

    def upper(j):
        return pl.ds(j * tile, tile), pl.ds(j * tile, width - j * tile)

    def mirror(low):
        for j in range(1, tiles):
            for i in range(j):
                here, there = pl.ds(i * tile, tile), pl.ds(j * tile, tile)
                low[there, here] = low[here, there].T

    @pl.when(control_ref[0] == 1)
    def _():
        copies = [[] for _ in range(parts)]
        for (part, first), piece in zip(places, pieces):
            for turn in range(first, first + piece.shape[0]):
                copies[part].append(
                    pltpu.make_async_copy(
                        piece.at[turn - first],
                        whole.at[pl.ds(part * shard, shard), pl.ds(turn * pad, pad)],
                        arrived.at[part, turn],
                    )
                )
        for part in range(parts):
            for copy in copies[part]:
                copy.start()
        for part in range(parts):
            for copy in copies[part]:
                copy.wait()
        diagonal = lax.broadcasted_iota(jnp.int32, (tile, tile), 0) == lax.broadcasted_iota(
            jnp.int32, (tile, tile), 1
        )
        squares = jnp.zeros((1, 1), f32)
        for j in range(tiles):
            up, at = upper(j)
            gram[up, at] = dot32(whole[up, :], whole[at, :], 1, 1)
            entries = jnp.where(diagonal, gram[up, up], 0.0)
            squares = squares + jnp.sum(
                jnp.sum(entries, axis=1, keepdims=True), axis=0, keepdims=True
            )
        inverse = 1.0 / (jnp.sqrt(squares) + ortho_eps)
        for j in range(tiles):
            up, at = upper(j)
            scaled = gram[up, at] * (inverse * inverse)
            gram[up, at] = scaled
            gram_low[up, at] = scaled.astype(bf16)
        mirror(gram_low)

        def step(index, carry):
            poly = poly_low.at[index]
            for j in range(tiles):
                up, at = upper(j)
                poly[up, at] = (
                    coef_b * gram[up, at] + coef_c * dot32(gram_low[up, :], gram_low[:, at], 1, 0)
                ).astype(bf16)
            mirror(poly)
            for j in range(tiles):
                up, at = upper(j)
                value = coef_a * gram[up, at] + dot32(poly[up, :], gram_low[:, at], 1, 0)
                prod[up, at] = value
                prod_low[up, at] = value.astype(bf16)
            mirror(prod_low)
            for j in range(tiles):
                up, at = upper(j)
                value = coef_a * prod[up, at] + dot32(prod_low[up, :], poly[:, at], 1, 0)
                gram[up, at] = value
                gram_low[up, at] = value.astype(bf16)
            mirror(gram_low)
            return carry

        lax.fori_loop(0, NS_STEPS - 1, step, 0)
        unit = lax.broadcasted_iota(jnp.int32, (shard, width), 0) == lax.broadcasted_iota(
            jnp.int32, (shard, width), 1
        )
        rows[...] = (
            coef_a * unit.astype(f32)
            + coef_b * gram[pl.ds(0, shard), :]
            + coef_c * dot32(gram_low[pl.ds(0, shard), :], gram_low[...], 1, 0)
        )

        def apply(index, carry):
            value = rows[...]
            rows[...] = coef_a * value + dot32(
                value.astype(bf16), poly_low[NS_STEPS - 2 - index], 1, 0
            )
            return carry

        lax.fori_loop(0, NS_STEPS - 1, apply, 0)
        scaled = (rows[...] * inverse).astype(bf16)
        for turn in range(count // 2):
            chip = lax.rem((control_ref[1] >> 1) + turn, count // 2)
            for core in range(2):
                lanes = pl.ds(pl.multiple_of((2 * chip + core) * pad, 128), pad)
                outs[turn][core] = dot32(scaled, whole[:, lanes], 1, 0).astype(bf16)


def orthogonalize(control, pieces, places, parts, after):
    count, shard, pad = pieces[0].shape
    width = shard * parts
    return pl.pallas_call(
        functools.partial(ortho_kernel, places, len(after)),
        out_shape=[jax.ShapeDtypeStruct((2, shard, pad), bf16)] * (count // 2),
        in_specs=[smem_spec()] + any_specs(len(pieces) + len(after)),
        out_specs=vmem_specs(count // 2),
        scratch_shapes=[
            pltpu.VMEM((width, count * pad), bf16),
            pltpu.VMEM((width, width), f32),
            pltpu.VMEM((width, width), f32),
            pltpu.VMEM((width, width), bf16),
            pltpu.VMEM((width, width), bf16),
            pltpu.VMEM((NS_STEPS - 1, width, width), bf16),
            pltpu.VMEM((shard, width), f32),
            pltpu.SemaphoreType.DMA((parts, count)),
        ],
        compiler_params=pltpu.CompilerParams(vmem_limit_bytes=vmem_limit),
        cost_estimate=pl.CostEstimate(
            flops=30 * 10**9, bytes_accessed=4 * count * shard * pad, transcendentals=0
        ),
        name="orthogonalize",
    )(control, *pieces, *after)


def update_kernel(owners, flip, extra, control_ref, rate_ref, own_ref, *refs):
    chips = len(refs) - extra - 2
    arrived, other_ref, out_ref = refs[:chips], refs[chips], refs[-1]
    cols = own_ref.shape[1 if flip else 2]
    chip, core = control_ref[1] >> 1, control_ref[1] & 1
    for index, owner in enumerate(owners):
        turn = lax.rem(chip - owner // 2 + chips, chips)
        for at in range(chips):

            @pl.when(turn == at)
            def _():
                step = jnp.where(core == owner % 2, arrived[at][core], other_ref[at])
                step = step.astype(f32)
                step = step.T[:cols] if flip else step[:, :cols]
                out_ref[index] = (
                    own_ref[index] * (1.0 - matrix_rate * decay_rate) - rate_ref[index] * step
                )


def update(control, rate, own, arrived, other, owners, flip, after):
    return pl.pallas_call(
        functools.partial(update_kernel, owners, flip, len(after)),
        grid=(1,),
        in_specs=[smem_spec()] * 2 + whole_specs((own, *arrived, other)) + any_specs(len(after)),
        out_specs=whole_spec(own.shape),
        out_shape=jax.ShapeDtypeStruct(own.shape, f32),
        compiler_params=pltpu.CompilerParams(vmem_limit_bytes=vmem_limit),
        name="update",
    )(control, rate, own, *arrived, other, *after)


def finish_kernel(matrices, *refs):
    shares, momentum_ref, (grad_ref, new_ref) = refs[:matrices], refs[matrices], refs[-2:]
    count = shares[0].shape[0]
    cols = grad_ref.shape[2] // count
    for index in range(matrices):
        for turn in range(count):
            at = pl.ds(turn * cols, cols)
            grad = shares[index][turn].astype(f32)[:, :cols]
            grad_ref[index, :, at] = grad
            new_ref[index, :, at] = momentum_decay * momentum_ref[index, :, at] + grad


def finish(share, momentum, after):
    count, _, pad = share.shape
    matrices, shard, width = momentum.shape
    step = min(64, shard)
    steps = shard // step
    whole = pl.BlockSpec((matrices, step, width), lambda i: (0, i, 0))
    parts = [
        pl.BlockSpec((count, step, pad), lambda i, index=index: (0, index * steps + i, 0))
        for index in range(matrices)
    ]
    size = matrices * shard * width
    return pl.pallas_call(
        functools.partial(finish_kernel, matrices),
        grid=(steps,),
        in_specs=parts + [whole] + any_specs(len(after)),
        out_specs=[whole, whole],
        out_shape=[jax.ShapeDtypeStruct(momentum.shape, f32)] * 2,
        compiler_params=pltpu.CompilerParams(vmem_limit_bytes=vmem_limit),
        cost_estimate=pl.CostEstimate(
            flops=2 * size, bytes_accessed=14 * size, transcendentals=0
        ),
        name="finish",
    )(*[share] * matrices, momentum, *after)


def adam_update(parameter, gradient, first_state, second_state):
    first_new = first_decay * first_state + (1.0 - first_decay) * gradient
    second_new = second_decay * second_state + (1.0 - second_decay) * gradient * gradient
    first_hat = first_new / (1.0 - first_decay**STEP)
    second_hat = second_new / (1.0 - second_decay**STEP)
    return (parameter - vector_rate * first_hat / (jnp.sqrt(second_hat) + adam_eps), second_new)


def swap(value, axis, bits, count):
    return lax.ppermute(value, axis, [(i, i ^ bits) for i in range(count)])


def sum_all(value, axis, count):
    bits = 1
    while bits < count:
        value = value + swap(value, axis, bits, count)
        bits *= 2
    return value


def near_wt(block, wt_count):
    return [swap(block, "wt", bits, wt_count) for bits in range(1, min(wt_count, 3))]


def far_wt(block, near, wt_count):
    rows = block.shape[0]
    if wt_count == 4:
        half = rows // 2
        pieces = [swap(near[0][:half], "wt", 2, wt_count), swap(near[1][half:], "wt", 1, wt_count)]
        return pieces, [(3, 0), (3, half)]
    places = [(bits, 0) for bits in range(1 + len(near), wt_count)]
    return [swap(block, "wt", bits, wt_count) for bits, _ in places], places


def sum_wt(parts, wt_count):
    total = parts[0].astype(f32)
    for bits in range(1, wt_count):
        total = total + swap(parts[bits], "wt", bits, wt_count).astype(f32)
    return total


def chip_order(seq_count):
    chips = seq_count // 2
    return [slot_of(chips, slot) for slot in range(chips)]


def gather_chips(block, seq_count):
    return [block] + [swap(block, "seq", 2 * bits, seq_count) for bits in chip_order(seq_count)[1:]]


def both_cores(blocks, seq_count):
    same = jnp.stack(blocks)
    return same, swap(same, "seq", 1, seq_count)


def send_chips(sends, seq_count):
    return [
        swap(value, "seq", 2 * bits, seq_count)
        for bits, value in zip(chip_order(seq_count)[1:], sends)
    ]


def send_owned(value, bits, owners, wt_count):
    pairs = [
        (owner * wt_count + w, owner * wt_count + (w ^ bits))
        for owner in owners
        for w in range(wt_count)
    ]
    return lax.ppermute(value, ("seq", "wt"), pairs)


def near_owned(block, owners, wt_count):
    return [send_owned(block, bits, owners, wt_count) for bits in range(1, min(wt_count, 3))]


def gather_owned(block, near, owners, wt_count):
    pieces = [block] + near
    places = [(part, 0) for part in range(len(pieces))]
    if wt_count == 4:
        half = block.shape[0] // 2
        pieces.append(send_owned(near[0][:half], 2, owners, wt_count))
        pieces.append(send_owned(near[1][half:], 1, owners, wt_count))
        return pieces, places + [(3, 0), (3, half)]
    for bits in range(len(pieces), wt_count):
        pieces.append(send_owned(block, bits, owners, wt_count))
        places.append((bits, 0))
    return pieces, places


def direct_owned(block, owners, wt_count):
    pieces = [block] + [send_owned(block, bits, owners, wt_count) for bits in range(1, wt_count)]
    return pieces, [(part, 0) for part in range(wt_count)]


def spread_chips(blocks, owners, seq_count):
    chips = seq_count // 2
    return [blocks[0]] + [
        lax.ppermute(
            blocks[turn],
            "seq",
            [(owner, (owner // 2 + turn) % chips * 2 + owner % 2) for owner in owners],
        )
        for turn in range(1, chips)
    ]


def spread_cores(arrived, core, seq_count):
    sent = [lax.dynamic_index_in_dim(value, 1 - core, 0, keepdims=False) for value in arrived]
    return swap(jnp.stack(sent), "seq", 1, seq_count)


def per_device(
    tokens,
    cotangent,
    doc_bounds,
    attn_master,
    mlp_master,
    attn_momentum,
    mlp_momentum,
    gains,
    gain_first,
    gain_second,
    qkv_bias,
    bias_first,
    bias_second,
):
    seq_count = lax.axis_size("seq")
    wt_count = lax.axis_size("wt")
    seq_index = lax.axis_index("seq")
    wt_index = lax.axis_index("wt")
    row_count = tokens.shape[1]
    width = tokens.shape[2]
    ff = mlp_master.shape[2]
    shard = attn_master.shape[1]
    length = row_count * seq_count
    head_cols = width // seq_count
    ff_cols = ff // seq_count

    place = jnp.stack([seq_index // 2, seq_index % 2])

    x_same, x_other = both_cores(gather_chips(tokens[0], seq_count), seq_count)
    own_dy, x_same = lax.optimization_barrier((cotangent[0], x_same))
    dy_low = lax.all_gather(own_dy, "seq", axis=0, tiled=True)

    vectors = jnp.pad(jnp.concatenate([gains, qkv_bias], 0), ((0, 11), (0, 3 * head_cols - shard)))
    qkv_w = pack(seq_index, attn_master, vectors, head_cols, [])
    qkv_w = lax.all_gather(qkv_w, "wt", axis=0)
    bounds, qkv_w = lax.optimization_barrier((doc_bounds, qkv_w))
    _, position = doc_layout(bounds[0], length)
    cosine, sine = rope_tables(position, head_cols)
    place_own, qkv_w = lax.optimization_barrier((seq_index, qkv_w))
    attn_own = lax.dynamic_slice_in_dim(attn_master, place_own * head_cols, head_cols, 2)
    mlp_own = lax.dynamic_slice_in_dim(mlp_master, place_own * ff_cols, ff_cols, 2)
    ff_pad = -(-ff_cols // 128) * 128
    wide_own = jnp.pad(mlp_own, ((0, 0), (0, 0), (0, ff_pad - ff_cols)))
    wide_own = jnp.concatenate([attn_master[3], wide_own[0], wide_own[1], wide_own[2]], 1)
    wide_own = wide_own.astype(bf16)
    wide_near = near_wt(wide_own, wt_count)
    vectors = jnp.moveaxis(qkv_w[:, shard : shard + 5, :shard], 0, 1).reshape(5, width).astype(f32)
    qkv_w = qkv_w[:, :shard].reshape(width, 3 * head_cols)

    bias_own = lax.dynamic_slice_in_dim(vectors[2:5], seq_index * head_cols, head_cols, 1)
    x_low, normed_one, query, key, value, attended, log_total = front(
        doc_bounds,
        place,
        x_same,
        x_other,
        qkv_w,
        vectors[0:1],
        bias_own.reshape(1, 3 * head_cols),
        cosine,
        sine,
    )
    a_blocks = gather_chips(attended, seq_count)

    mlp_pick = jnp.minimum(seq_index // 2, 2).reshape(1)
    attn_pick = jnp.minimum(seq_index // 2, 3).reshape(1)
    mlp_pick, attn_pick, attended = lax.optimization_barrier((mlp_pick, attn_pick, attended))
    squares = sums_of_squares(mlp_pick, attn_master, mlp_master)
    wide_near, squares = lax.optimization_barrier((wide_near, squares))
    wide_far, far_places = far_wt(wide_own, wide_near, wt_count)
    mlp_old = picked(mlp_momentum, mlp_pick, seq_count)
    attn_old = picked(attn_momentum, attn_pick, seq_count)
    near_places = [(bits, 0) for bits in range(1 + len(wide_near))]
    wide_w = assemble(
        wt_index,
        [wide_own] + wide_near + wide_far,
        [(bits, first, shard) for bits, first in near_places + far_places],
        width,
    )
    a_blocks, wide_w, squares, mlp_old, attn_old = lax.optimization_barrier(
        (a_blocks, wide_w, squares, mlp_old, attn_old)
    )
    a_same, a_other = both_cores(a_blocks, seq_count)

    normed_two, d_gate, d_up, hidden, d_mine, d_other, resid_own, gain_part_two = middle(
        place, a_same, a_other, x_low, dy_low, wide_w, vectors[1:2]
    )

    control = jnp.stack([jnp.zeros_like(seq_index), seq_index, wt_index])
    mlp_part = mlp_grads(normed_two, dy_low, d_gate, d_up, hidden, wt_count, [])
    mlp_share = lax.psum_scatter(mlp_part, "wt", scatter_dimension=0, tiled=True)
    got = swap(d_other, "seq", 1, seq_count)
    own, *sends = pair_sums(d_mine, got, 1, False, [mlp_part])
    arrived = send_chips(sends, seq_count)
    pair, d_resid = post(
        own, arrived, resid_own, cotangent[0], vectors[1:2], wide_w, seq_count, []
    )
    pair = lax.all_to_all(pair, "seq", split_axis=0, concat_axis=0)
    pair, mlp_share = lax.optimization_barrier((pair, mlp_share))
    mlp_share = lax.all_gather(mlp_share, "seq", axis=0)

    args = (query, key, value, log_total, pair, normed_one, a_same, a_other, cosine, sine)
    args += (qkv_w, vectors[0:1], gain_part_two, squares)
    d_qkv, attn_part = back(doc_bounds, control, args, wt_count)

    def control_of(owners):
        active = functools.reduce(jnp.logical_or, [seq_index == owner for owner in owners])
        return jnp.stack([active.astype(jnp.int32), seq_index, wt_index])

    attn_share = sum_wt(attn_part, wt_count)
    squares = jnp.sum(attn_share[4 * shard + 5 : 4 * shard + 7, :7], axis=0)
    attn_share = attn_share.astype(bf16)
    attn_share = lax.all_gather(attn_share, "seq", axis=0)

    mine, other = late_sums(
        place, hidden, wide_w[:, width + 2 * ff_pad :], d_qkv, qkv_w, seq_count
    )
    late, *sends = pair_sums(mine, swap(other, "seq", 1, seq_count), 1, False, [])

    mlp_block = new_block(mlp_share, mlp_old, mlp_pick, [late])
    mlp_near = near_owned(mlp_block, MLP_OWNERS, wt_count)
    mlp_grad, mlp_mom = finish(mlp_share, mlp_momentum, [mlp_block])
    mlp_near, done = lax.optimization_barrier((mlp_near, mlp_grad[0, :8, :128]))
    mlp_pieces, mlp_places = gather_owned(mlp_block, mlp_near, MLP_OWNERS, wt_count)
    sends, attn_share = lax.optimization_barrier((sends, attn_share))
    late_arrived = send_chips(sends, seq_count)
    attn_block = new_block(attn_share, attn_old, attn_pick, [])
    attn_near = near_owned(attn_block, ATTN_OWNERS, wt_count)
    attn_near, mlp_pieces = lax.optimization_barrier((attn_near, mlp_pieces))
    attn_pieces, attn_places = gather_owned(attn_block, attn_near, ATTN_OWNERS, wt_count)
    mlp_blocks = orthogonalize(
        control_of(MLP_OWNERS), mlp_pieces, mlp_places, wt_count, [done, *attn_pieces[1:]]
    )
    attn_blocks = orthogonalize(
        control_of(ATTN_OWNERS), attn_pieces, attn_places, wt_count, [mlp_blocks[0]]
    )
    mlp_blocks, attn_blocks, late_arrived = lax.optimization_barrier(
        (mlp_blocks, attn_blocks, late_arrived)
    )
    attn_grad, attn_mom = finish(attn_share, attn_momentum, attn_blocks[:1])

    attn_rate = matrix_rate * math.sqrt(width) * jnp.sqrt(squares[:4] / (width * width))
    mlp_rate = matrix_rate * math.sqrt(ff) * jnp.sqrt(squares[4:] / (width * ff))
    core = seq_index % 2
    mlp_arrived = spread_chips(mlp_blocks, MLP_OWNERS, seq_count)
    attn_arrived = spread_chips(attn_blocks, ATTN_OWNERS, seq_count)

    total = late[0]
    for value in late_arrived:
        total = total + value[0].astype(f32)
    layer_out = (resid_own + total[0]).astype(bf16)
    x_own = tokens[0].astype(f32)
    inverse_own = lax.rsqrt(jnp.mean(x_own * x_own, axis=-1, keepdims=True) + norm_eps)
    d_input_norm = norm_backward(total[1], x_own, inverse_own, vectors[0])
    tokens_grad = d_resid + d_input_norm

    mlp_arrived, attn_arrived, layer_out, tokens_grad = lax.optimization_barrier(
        (mlp_arrived, attn_arrived, layer_out, tokens_grad)
    )
    mlp_other = spread_cores(mlp_arrived, core, seq_count)
    attn_other = spread_cores(attn_arrived, core, seq_count)
    attn_new = update(
        control, attn_rate, attn_own, attn_arrived, attn_other, ATTN_OWNERS, False, []
    )
    mlp_new = update(
        control,
        mlp_rate,
        mlp_own.swapaxes(1, 2),
        mlp_arrived,
        mlp_other,
        MLP_OWNERS,
        True,
        [],
    ).swapaxes(1, 2)

    small = jnp.sum(attn_share[:, 4 * shard :].astype(f32), axis=0).reshape(2, 8, 128)
    small = jnp.moveaxis(small[: shard // 128], 0, 1).reshape(8, shard)
    gain_grad = small[:2]
    bias_grad = small[2:5]
    gain_new, gain_second_new = adam_update(gains, gain_grad, gain_first, gain_second)
    bias_new, bias_second_new = adam_update(qkv_bias, bias_grad, bias_first, bias_second)
    return (
        layer_out[None],
        tokens_grad[None],
        attn_grad,
        mlp_grad,
        attn_mom,
        mlp_mom,
        attn_new,
        mlp_new,
        gain_grad,
        gain_second_new,
        gain_new,
        bias_grad,
        bias_second_new,
        bias_new,
    )


def solution(mesh):
    return jax.shard_map(
        per_device,
        mesh=mesh,
        in_specs=(
            P("wt", "seq", None),
            P("wt", "seq", None),
            P("wt", None),
            P(None, "wt", None),
            P(None, "wt", None),
            P(None, "wt", None),
            P(None, "wt", None),
            P(None, "wt"),
            P(None, "wt"),
            P(None, "wt"),
            P(None, "wt"),
            P(None, "wt"),
            P(None, "wt"),
        ),
        out_specs=(
            P("wt", "seq", None),
            P("wt", "seq", None),
            P(None, "wt", None),
            P(None, "wt", None),
            P(None, "wt", None),
            P(None, "wt", None),
            P(None, "wt", "seq"),
            P(None, "wt", "seq"),
            P(None, "wt"),
            P(None, "wt"),
            P(None, "wt"),
            P(None, "wt"),
            P(None, "wt"),
            P(None, "wt"),
        ),
        check_vma=False,
    )
```
